512 devices in a mesh: dom: 512 (over z, y, x, core).
Axes of the slice: x: 4, y: 4, z: 16, core: 2. Of those that a mesh axis runs over, the one named last changes fastest.
Arguments:
- dofs: float32 [56, 9, 65536], P(None, None, 'dom'), may hold values from -6 to 6
- star: float32 [3, 9, 9, 65536], P(None, None, None, 'dom'), may hold values from -5 to 5
- flux_self: float32 [4, 9, 9, 65536], P(None, None, None, 'dom'), may hold values from -0.5 to 0.5
- flux_other: float32 [4, 9, 9, 65536], P(None, None, None, 'dom'), may hold values from -0.5 to 0.5
- labels: int32 [65536], P('dom'), may hold values from 0 to 1, as said below
- neighbour_source: int32 [4, 65536], P(None, 'dom'), may hold values from 0 to 607, as said below
- orientation: int32 [4, 65536], P(None, 'dom'), may hold values from 0 to 2
- fine_send: int32 [4, 6144], P(None, 'dom'), may hold values from 0 to 511, as said below
- coarse_send: int32 [4, 6144], P(None, 'dom'), may hold values from 0 to 511, as said below
- stiff_time: float32 [3, 35, 56], replicated, may hold values from -2 to 2
- stiff_vol: float32 [3, 56, 35], replicated, may hold values from -0.109375 to 0.109375
- face_back: float32 [4, 21, 56], replicated, may hold values from -0.75 to 0.75
- face_front: float32 [4, 56, 21], replicated, may hold values from -1.25 to 1.25
- face_turn: float32 [3, 21, 21], replicated, may hold values from -1.25 to 1.25
Outputs:
- new_dofs: float32 [56, 9, 65536], P(None, None, 'dom')
The draws below stay inside these ranges and needn't reach their ends.
Inputs may be any that keep to these rules, and one draw needn't show every extreme that they name: `labels`: each partition holds 1 to 64 elements of label 1, exactly 64 on some partition. `neighbour_source`: below 512, the value names face value // 128 of local element value % 128; above, a received slot of the source table; every received slot of a partition is named by exactly one of its faces. `fine_send`: each entry is j * 128 + e with e a local element of label 1 and j one of its faces. `coarse_send`: each entry is j * 128 + e with e a local element of label 0 and j one of its faces.
All inputs are finite; a program needn't handle non-finite values.
Results may differ from the reference program's by a relative error of at most 0.0003.
Values sent between devices are 32-bit elements; how exact they have to be, the bound alone decides.
No kernel may reach another device: no remote copies, remote signals or barrier semaphores. Data moves between devices by JAX's collectives and lax.ppermute only.
A program may use at most 128 MiB of HBM per device.

```python
import math
import jax
import jax.numpy as jnp
from jax import lax

ORDER = 6
NQ = 9
NB = 56
NB_LOW = 35
NF = 21
SUBSTEPS = 4
PEERS = 4
E_DEV = 128
FINE_MAX = 64
SLOTS = 12
ELEMS = 65536
N_DOM = 512


def layout(key):
    devices = ELEMS // E_DEV
    base_key = jax.random.fold_in(key, 101)
    first_key, second_key, pick_key, order_key = jax.random.split(base_key, 4)
    first_draw = jax.random.randint(first_key, (devices,), 1, FINE_MAX + 1)
    second_draw = jax.random.randint(second_key, (devices,), 1, FINE_MAX + 1)
    busiest = jax.random.randint(pick_key, (), 0, devices)
    counts = jnp.where(jnp.arange(devices) == busiest, FINE_MAX, jnp.minimum(first_draw, second_draw))
    orders = jax.vmap(lambda subkey: jax.random.permutation(subkey, E_DEV))(jax.random.split(order_key, devices))
    rank_table = jnp.argsort(orders, axis=1)
    fine_table = (rank_table < counts[:, None]).astype(jnp.int32)
    return (orders, counts, fine_table)


def element_scale(key):
    orders, counts, fine_table = layout(key)
    return jnp.where(fine_table.reshape(-1) == 1, 4.0, 1.0)


def scaled_entries(key, leading, spread):
    entries = jnp.clip(jax.random.normal(key, (leading, NQ, NQ, ELEMS), jnp.float32), -4.0, 4.0)
    return entries * spread


def draw_star(key, part):
    factor = element_scale(key)
    key = jax.random.fold_in(key, 2)
    return (scaled_entries(key, 3, 0.25) * factor).astype(jnp.float32)


def draw_flux_self(key, part):
    factor = element_scale(key)
    key = jax.random.fold_in(key, 6)
    return (scaled_entries(key, 4, 0.02) * factor).astype(jnp.float32)


def draw_flux_other(key, part):
    factor = element_scale(key)
    key = jax.random.fold_in(key, 7)
    return (scaled_entries(key, 4, 0.02) * factor).astype(jnp.float32)


def draw_labels(key, part):
    orders, counts, fine_table = layout(key)
    return fine_table.reshape(-1).astype(jnp.int32)


def draw_neighbour_source(key, part):
    key = jax.random.fold_in(key, 3)
    devices = ELEMS // E_DEV
    face_total = 4 * E_DEV
    halo_total = 2 * PEERS * SLOTS
    local_key, place_key = jax.random.split(key, 2)
    local_codes = jax.random.randint(local_key, (devices, face_total), 0, face_total)
    places = jax.vmap(lambda subkey: jax.random.permutation(subkey, face_total))(jax.random.split(place_key, devices))
    rank_table = jnp.argsort(places, axis=1)
    code_table = jnp.where(rank_table < halo_total, face_total + rank_table, local_codes)
    return code_table.reshape(devices, 4, E_DEV).transpose(1, 0, 2).reshape(4, ELEMS).astype(jnp.int32)


def send_codes(key, orders, lower, upper):
    devices = ELEMS // E_DEV
    pick_key, face_key = jax.random.split(key, 2)
    chosen = jax.random.randint(pick_key, (devices, PEERS * SLOTS), lower[:, None], upper[:, None])
    members = jnp.take_along_axis(orders, chosen, axis=1)
    face_pick = jax.random.randint(face_key, (devices, PEERS * SLOTS), 0, 4)
    code_table = (face_pick * E_DEV + members).reshape(devices, PEERS, SLOTS)
    return code_table.transpose(1, 0, 2).reshape(PEERS, devices * SLOTS).astype(jnp.int32)


def draw_fine_send(key, part):
    orders, counts, fine_table = layout(key)
    key = jax.random.fold_in(key, 4)
    return send_codes(key, orders, jnp.zeros_like(counts), counts)


def draw_coarse_send(key, part):
    orders, counts, fine_table = layout(key)
    key = jax.random.fold_in(key, 8)
    return send_codes(key, orders, counts, jnp.full_like(counts, E_DEV))


def plant(drawn, rng, least, largest):
    extent = drawn.shape
    index_at = [jax.random.randint(jax.random.fold_in(rng, axis), (), 0, extent[axis]) for axis in range(len(extent))]
    drawn = drawn.at[tuple(index_at)].set(least)
    longest = extent.index(max(extent))
    index_at[longest] = (index_at[longest] + 1) % extent[longest]
    return drawn.at[tuple(index_at)].set(largest)


def shard_levels(key, extent, cuts, least, high):
    def one(position, blocks):
        draws = jax.random.uniform(jax.random.fold_in(jax.random.fold_in(key, 6), position), (blocks,), jnp.float32, least / len(cuts), high / len(cuts))
        return jnp.repeat(jnp.exp(draws), extent[position] // blocks).reshape((-1,) + (1,) * (len(extent) - position - 1))

    factor_of = one(*cuts[0])
    for cut in cuts[1:]:
        factor_of = factor_of * one(*cut)
    return factor_of


def centred(own_key, shape, scale, limit, cuts=(), dtype=jnp.bfloat16):
    values = scale * jax.random.normal(own_key, shape, jnp.float32)
    if cuts:
        values = values * shard_levels(own_key, shape, cuts, -0.22, 0.18)
    return jnp.clip(values, -limit, limit).astype(dtype)


def setup_inputs(seed: int = 0) -> dict:
    arg_keys = jax.random.split(jax.random.key(seed), 15)
    dofs = centred(arg_keys[0], (NB, NQ, ELEMS), 1.0, 6.0, ((2, 512),), jnp.float32)
    star = draw_star(jax.random.fold_in(arg_keys[14], 71), 0)
    flux_self = draw_flux_self(jax.random.fold_in(arg_keys[14], 71), 0)
    flux_other = draw_flux_other(jax.random.fold_in(arg_keys[14], 71), 0)
    labels = draw_labels(jax.random.fold_in(arg_keys[14], 71), 0)
    neighbour_source = draw_neighbour_source(jax.random.fold_in(arg_keys[14], 71), 0)
    orientation = plant(jax.random.randint(arg_keys[6], (4, ELEMS), 0, 3), jax.random.fold_in(arg_keys[6], 1), 0, 2).astype(jnp.int32)
    fine_send = draw_fine_send(jax.random.fold_in(arg_keys[14], 71), 0)
    coarse_send = draw_coarse_send(jax.random.fold_in(arg_keys[14], 71), 0)
    stiff_time = centred(arg_keys[9], (3, NB_LOW, NB), (NB // 6) ** -0.5, 2.0, (), jnp.float32)
    stiff_vol = centred(arg_keys[10], (3, NB, NB_LOW), (100 * NB_LOW) ** -0.5, 0.109375, (), jnp.float32)
    face_back = centred(arg_keys[11], (4, NF, NB), NB ** -0.5, 0.75, (), jnp.float32)
    face_front = centred(arg_keys[12], (4, NB, NF), NF ** -0.5, 1.25, (), jnp.float32)
    face_turn = centred(arg_keys[13], (3, NF, NF), NF ** -0.5, 1.25, (), jnp.float32)
    return dict(dofs=dofs, star=star, flux_self=flux_self, flux_other=flux_other, labels=labels, neighbour_source=neighbour_source, orientation=orientation, fine_send=fine_send, coarse_send=coarse_send, stiff_time=stiff_time, stiff_vol=stiff_vol, face_back=face_back, face_front=face_front, face_turn=face_turn)


PRECISE = lax.Precision.HIGHEST


def basis_count(degree):
    return (degree + 1) * (degree + 2) * (degree + 3) // 6


def taylor_weights(start, stop):
    return [(stop ** (depth + 1) - start ** (depth + 1)) / math.factorial(depth + 1) for depth in range(ORDER)]


def derivatives(field_now, star_block, stiff_time):
    chain = [field_now]
    for depth in range(ORDER - 1):
        width_now = basis_count(ORDER - 1 - depth)
        width_next = basis_count(ORDER - 2 - depth)
        partial_terms = jnp.einsum("dab,bqe->daqe", stiff_time[:, :width_next, :width_now], chain[-1], precision=PRECISE)
        chain.append(-jnp.einsum("daqe,dqpe->ape", partial_terms, star_block, precision=PRECISE))
    return chain


def integrate(chain, weights):
    total = jnp.zeros(chain[0].shape, jnp.float32)
    for depth in range(ORDER):
        term = weights[depth] * chain[depth]
        total = total + jnp.pad(term, ((0, chain[0].shape[0] - term.shape[0]), (0, 0), (0, 0)))
    return total


def volume(integral, star_block, stiff_vol):
    inner = jnp.einsum("dab,bqe->daqe", stiff_vol, integral[:stiff_vol.shape[2]], precision=PRECISE)
    return jnp.einsum("daqe,dqpe->ape", inner, star_block, precision=PRECISE)


def project(integral, face_back):
    return jnp.einsum("jfb,bqe->fqje", face_back, integral, precision=PRECISE)


def surface(own_faces, remote_faces, turn_codes, self_block, other_block, face_front, face_turn):
    turned = jnp.zeros(remote_faces.shape, jnp.float32)
    for turn_code in range(3):
        rotated = jnp.einsum("fg,gqie->fqie", face_turn[turn_code], remote_faces, precision=PRECISE)
        turned = turned + jnp.where(turn_codes[None, None] == turn_code, rotated, 0.0)
    inner = jnp.einsum("fqie,iqpe->fpie", own_faces, self_block, precision=PRECISE)
    inner = inner + jnp.einsum("fqie,iqpe->fpie", turned, other_block, precision=PRECISE)
    return jnp.einsum("ibf,fpie->bpe", face_front, inner, precision=PRECISE)


def peer_offset(peer_index):
    return (peer_index // 2 + 1) * (1 - 2 * (peer_index % 2))


def by_device(array):
    shaped = array.reshape(array.shape[:-1] + (N_DOM, E_DEV))
    return jnp.moveaxis(shaped, -2, 0)


def from_devices(array):
    moved = jnp.moveaxis(array, 0, -2)
    return moved.reshape(moved.shape[:-2] + (N_DOM * E_DEV,))


def shift_devices(block, offset_value):
    blank = jnp.zeros_like(block[:abs(offset_value)])
    if offset_value > 0:
        return jnp.concatenate([blank, block[:-offset_value]], axis=0)
    return jnp.concatenate([block[-offset_value:], blank], axis=0)


def build_table(faces_dev, fine_lists, coarse_lists):
    groups = NF * NQ
    local_table = faces_dev.reshape(N_DOM, groups, 4 * E_DEV)
    pieces = [local_table]
    for send_lists in (fine_lists, coarse_lists):
        sent = jnp.take_along_axis(local_table, send_lists.reshape(N_DOM, 1, PEERS * SLOTS), axis=2)
        sent = sent.reshape(N_DOM, groups, PEERS, SLOTS)
        arrived = [shift_devices(sent[:, :, peer_index], peer_offset(peer_index)) for peer_index in range(PEERS)]
        pieces.append(jnp.stack(arrived, axis=2).reshape(N_DOM, groups, PEERS * SLOTS))
    return jnp.concatenate(pieces, axis=2)


def look_up(source_table, source_dev):
    picked = jnp.take_along_axis(source_table, source_dev.reshape(N_DOM, 1, 4 * E_DEV), axis=2)
    return picked.reshape(N_DOM, NF, NQ, 4, E_DEV)


def reference(dofs, star, flux_self, flux_other, labels, neighbour_source, orientation, fine_send, coarse_send, stiff_time, stiff_vol, face_back, face_front, face_turn):
    start_dev = by_device(dofs)
    star_dev = by_device(star)
    self_dev = by_device(flux_self)
    other_dev = by_device(flux_other)
    fine_dev = by_device(labels) == 1
    source_dev = by_device(neighbour_source)
    turn_dev = by_device(orientation)
    fine_lists = fine_send.reshape(PEERS, N_DOM, SLOTS).transpose(1, 0, 2)
    coarse_lists = coarse_send.reshape(PEERS, N_DOM, SLOTS).transpose(1, 0, 2)

    def start_chain(items):
        return derivatives(items[0], items[1], stiff_time)

    chain_start = lax.map(start_chain, (start_dev, star_dev))
    state = start_dev
    faces_sum = jnp.zeros((N_DOM, NF, NQ, 4, E_DEV), jnp.float32)
    table_sum = jnp.zeros((N_DOM, NF * NQ, 4 * E_DEV + 2 * PEERS * SLOTS), jnp.float32)
    first_weights = taylor_weights(0.0, 1.0 / SUBSTEPS)
    for substep_index in range(SUBSTEPS):
        coarse_weights = taylor_weights(substep_index / SUBSTEPS, (substep_index + 1) / SUBSTEPS)

        def step_parts(items):
            field_now, chain, star_block, mask = items
            coarse_part = integrate(chain, coarse_weights)
            if substep_index == 0:
                integral = coarse_part
            else:
                fine_part = integrate(derivatives(field_now, star_block, stiff_time), first_weights)
                integral = jnp.where(mask, fine_part, coarse_part)
            return integral, project(integral, face_back)

        integral_dev, faces_dev = lax.map(step_parts, (state, chain_start, star_dev, fine_dev))
        source_table = build_table(faces_dev, fine_lists, coarse_lists)
        table_sum = table_sum + source_table
        faces_sum = faces_sum + faces_dev
        neighbours = look_up(source_table, source_dev)

        def step_update(items):
            field_now, integral, own_faces, remote_faces, star_block, self_block, other_block, turn_codes, mask = items
            moved = field_now + volume(integral, star_block, stiff_vol) - surface(own_faces, remote_faces, turn_codes, self_block, other_block, face_front, face_turn)
            return jnp.where(mask, moved, field_now)

        state = lax.map(step_update, (state, integral_dev, faces_dev, neighbours, star_dev, self_dev, other_dev, turn_dev, fine_dev))
    neighbours_sum = look_up(table_sum, source_dev)
    whole_weights = taylor_weights(0.0, 1.0)

    def final_update(items):
        field_now, first_field, chain, own_faces, remote_faces, star_block, self_block, other_block, turn_codes, mask = items
        whole_integral = integrate(chain, whole_weights)
        coarse_new = first_field + volume(whole_integral, star_block, stiff_vol) - surface(own_faces, remote_faces, turn_codes, self_block, other_block, face_front, face_turn)
        return jnp.where(mask, field_now, coarse_new)

    result = lax.map(final_update, (state, start_dev, chain_start, faces_sum, neighbours_sum, star_dev, self_dev, other_dev, turn_dev, fine_dev))
    return from_devices(result)
```

```python
import functools
import math

import jax
import jax.numpy as jnp
from jax import lax
from jax.experimental import pallas as pl
from jax.experimental.pallas import tpu as pltpu
from jax.sharding import PartitionSpec as P

ORDER = 6
SUBSTEPS = 4
NQ = 9
NB = 56
NLOW = 35
NF = 21
PEERS = 4
SLOTS = 12
LANES = 128
FPAD = 24
VPAD = 40
BOTH = 2 * SLOTS
WIDTH = 256
COLS = NQ * LANES
FACES = 4 * LANES
REM = 12 * FPAD
OWN = 4 * FPAD
DEEP = REM + OWN + 3 * VPAD
LEVELS = [(0, 35, 40, 56), (120, 20, 24, 40), (192, 10, 16, 24), (240, 4, 8, 16), (264, 1, 8, 8)]
BACK = 288
CHAIN_ROWS = BACK + OWN
HIGH = lax.Precision.HIGH
HIGHEST = lax.Precision.HIGHEST
F32 = jnp.float32
BF16 = jnp.bfloat16


def taylor_weights(start, stop):
    return [
        (stop ** (depth + 1) - start ** (depth + 1)) / math.factorial(depth + 1)
        for depth in range(ORDER)
    ]


def lanes(index):
    return slice(index * LANES, (index + 1) * LANES)


def iota(shape, dim):
    return lax.broadcasted_iota(jnp.int32, shape, dim)


def halves(value):
    top = value.astype(BF16)
    return top, (value - top.astype(F32)).astype(BF16)


def pick(value, hot, contract=((1,), (0,))):
    top, rest = halves(value)
    dims = (contract, ((), ()))
    return lax.dot_general(top, hot, dims, preferred_element_type=F32) + lax.dot_general(
        rest, hot, dims, preferred_element_type=F32
    )


def products(blocks, row_of, rows):
    totals = [None] * NQ
    for position, block in enumerate(blocks):
        for q in range(NQ):
            left = block(q)
            for p in range(NQ):
                term = left * row_of(position, q, p)
                totals[p] = term if totals[p] is None else totals[p] + term
    return totals


def chain_weights(stiff_time, face_back, out):
    out[...] = jnp.zeros(out.shape, F32)
    for start, valid, padded, _ in LEVELS:
        for d in range(3):
            out[start + d * padded : start + d * padded + valid, 0:NB] = stiff_time[d, 0:valid, :]
    for j in range(4):
        out[BACK + j * FPAD : BACK + j * FPAD + NF, 0:NB] = face_back[j]


def chain_of(first, star, weights, terms):
    now = first
    chain = [first]
    offset = 0
    for start, _, padded, width in LEVELS:
        terms[0 : 3 * padded, :] = jnp.dot(
            weights[start : start + 3 * padded, 0:width],
            now,
            precision=HIGH,
            preferred_element_type=F32,
        )
        blocks = [
            lambda q, d=d: terms[d * padded : (d + 1) * padded, lanes(q)] for d in range(3)
        ]
        totals = products(blocks, lambda d, q, p: star[d, q, p : p + 1, :], padded)
        now = jnp.concatenate(totals, axis=1)
        chain.append(now)
    return chain


def integral_of(chain, weights):
    pieces = []
    edges = [0, 8, 16, 24, 40, 56]
    for low, high in zip(edges[:-1], edges[1:]):
        total = None
        for depth in range(ORDER):
            if chain[depth].shape[0] < high:
                continue
            term = (weights[depth] * (-1) ** depth) * chain[depth][low:high]
            total = term if total is None else total + term
        pieces.append(total)
    return jnp.concatenate(pieces, axis=0)


def face_table(faces):
    rows = []
    for q in range(NQ):
        rows.append(
            jnp.concatenate(
                [faces[j * FPAD : (j + 1) * FPAD, lanes(q)] for j in range(4)], axis=1
            )
        )
    rows.append(jnp.zeros((WIDTH - NQ * FPAD, FACES), F32))
    return jnp.concatenate(rows, axis=0)


def project_and_send(integral, weights, lists, odd, faces_out, pair_out, far_out):
    faces = jnp.dot(
        weights[BACK : BACK + OWN, 0:NB], integral, precision=HIGH, preferred_element_type=F32
    )
    faces_out[...] = faces
    top, rest = halves(face_table(faces))
    hot = jnp.where(lists[...] == iota((PEERS * BOTH, FACES), 1), 1.0, 0.0).astype(BF16)
    dims = (((1,), (1,)), ((), ()))
    sent = lax.dot_general(hot, top, dims, preferred_element_type=F32) + lax.dot_general(
        hot, rest, dims, preferred_element_type=F32
    )
    first, second = sent[0:BOTH], sent[BOTH : 2 * BOTH]
    pair_out[0:BOTH, :] = jnp.where(odd, second, first)
    pair_out[BOTH : 2 * BOTH, :] = jnp.where(odd, first, second)
    far_out[...] = sent[2 * BOTH : 4 * BOTH]


def first_kernel(
    place, dofs, star, stiff_time, face_back, lists,
    state_out, low_out, coarse_out, faces_out, pair_out, far_out, weights_out, terms,
):
    odd = lax.rem(place[0], 2) == 1
    chain_weights(stiff_time, face_back, weights_out)
    state = jnp.concatenate([dofs[:, q, :] for q in range(NQ)], axis=1)
    state_out[...] = state
    chain = chain_of(state, star, weights_out, terms)
    integral = integral_of(chain, taylor_weights(0.0, 1.0 / SUBSTEPS))
    low_out[...] = integral[0:VPAD]
    project_and_send(integral, weights_out, lists, odd, faces_out, pair_out, far_out)
    for step in range(1, SUBSTEPS):
        coarse_out[step - 1] = integral_of(
            chain, taylor_weights(step / SUBSTEPS, (step + 1) / SUBSTEPS)
        )


def prepare_kernel(
    source, orientation, flux_other, face_front, face_turn, stiff_vol,
    slot_flux_out, slot_code_out, slot_hot_out, lift_out, table,
):
    row = iota((LANES, LANES), 0)
    peer = (row >= BOTH).astype(jnp.int32) + (row >= 2 * BOTH).astype(jnp.int32)
    peer = peer + (row >= 3 * BOTH).astype(jnp.int32)
    inner = row - BOTH * peer
    kind = (inner >= SLOTS).astype(jnp.int32)
    wanted = kind * (PEERS * SLOTS - SLOTS) + peer * SLOTS + inner + FACES
    wanted = jnp.where(row < PEERS * BOTH, wanted, -1)
    blocks = [jnp.where(source[i : i + 1, :] == wanted, 1.0, 0.0) for i in range(4)]
    slot_hot_out[...] = blocks[0] + blocks[1] + blocks[2] + blocks[3]
    hot = jnp.concatenate(blocks, axis=1).astype(BF16)
    codes = jnp.concatenate(
        [
            jnp.where(iota((16, LANES), 0) - 3 * i == orientation[i : i + 1, :], 1.0, 0.0)
            for i in range(4)
        ],
        axis=1,
    ).astype(BF16)
    dims = (((1,), (1,)), ((), ()))
    slot_code_out[...] = lax.dot_general(codes, hot, dims, preferred_element_type=F32)
    table[...] = jnp.zeros(table.shape, F32)
    for i in range(4):
        for q in range(NQ):
            table[16 * q : 16 * q + NQ, lanes(i)] = flux_other[i, q]
    slot_flux_out[...] = pick(table[...], hot, ((1,), (1,)))

    def placed(rows, offset):
        return jnp.where(
            iota((rows, DEEP), 1) == iota((rows, DEEP), 0) + offset, 1.0, 0.0
        )

    total = jnp.zeros((NB, DEEP), F32)
    for i in range(4):
        spread = placed(NF, REM + FPAD * i)
        for code in range(3):
            spread = spread + jnp.dot(
                face_turn[code], placed(NF, FPAD * (3 * i + code)),
                precision=HIGHEST, preferred_element_type=F32,
            )
        total = total - jnp.dot(
            face_front[i], spread, precision=HIGHEST, preferred_element_type=F32
        )
    for d in range(3):
        total = total + jnp.dot(
            stiff_vol[d], placed(NLOW, REM + OWN + VPAD * d),
            precision=HIGHEST, preferred_element_type=F32,
        )
    lift_out[...] = total


def local_kernel(
    state, low, faces, star, flux_self, flux_other, source, orientation, lift, out, stack,
):
    column = iota((FACES, LANES), 0)
    hot = jnp.concatenate(
        [
            jnp.where(column == source[i : i + 1, :], 1.0, 0.0).astype(BF16)
            for i in range(4)
        ],
        axis=1,
    )
    found = pick(face_table(faces[...]), hot)
    for d in range(3):
        totals = products(
            [lambda q: low[:, lanes(q)]], lambda _, q, p: star[d, q, p : p + 1, :], VPAD
        )
        base = REM + OWN + VPAD * d
        for p in range(NQ):
            stack[base : base + VPAD, lanes(p)] = totals[p]
    for i in range(4):
        totals = products(
            [lambda q: faces[i * FPAD : (i + 1) * FPAD, lanes(q)]],
            lambda _, q, p: flux_self[i, q, p : p + 1, :],
            FPAD,
        )
        for p in range(NQ):
            stack[REM + FPAD * i : REM + FPAD * (i + 1), lanes(p)] = totals[p]
    for i in range(4):
        totals = products(
            [lambda q: found[q * FPAD : (q + 1) * FPAD, lanes(i)]],
            lambda _, q, p: flux_other[i, q, p : p + 1, :],
            FPAD,
        )
        for code in range(3):
            mask = jnp.where(orientation[i : i + 1, :] == code, 1.0, 0.0)
            base = FPAD * (3 * i + code)
            for p in range(NQ):
                stack[base : base + FPAD, lanes(p)] = totals[p] * mask
    out[...] = state[...] + jnp.dot(
        lift[...], stack[...], precision=HIGH, preferred_element_type=F32
    )


def remote_part(position, near, upper, lower, slot_flux, slot_code, slot_hot, lift, stack):
    odd = lax.rem(position, 2) == 1
    behind_up = lax.rem(position, 4) < 2
    up, down = upper[...], lower[...]
    behind = jnp.where(behind_up, up, down)
    ahead = jnp.where(behind_up, down, up)
    here = near[0:BOTH, :]
    relayed = slice(2 * BOTH, 3 * BOTH)
    rows = jnp.concatenate(
        [
            jnp.where(odd, here, behind[relayed]),
            jnp.where(odd, ahead[relayed], here),
            behind[0:BOTH],
            ahead[BOTH : 2 * BOTH],
            jnp.zeros((LANES - PEERS * BOTH, WIDTH), F32),
        ],
        axis=0,
    )
    received = jnp.transpose(rows)
    totals = products(
        [lambda q: received[q * FPAD : (q + 1) * FPAD]],
        lambda _, q, p: slot_flux[16 * q + p : 16 * q + p + 1, :],
        FPAD,
    )
    for code in range(12):
        mask = slot_code[code : code + 1, :]
        for p in range(NQ):
            stack[FPAD * code : FPAD * (code + 1), lanes(p)] = totals[p] * mask
    lifted = jnp.dot(
        lift[:, 0:REM], stack[...], precision=HIGH, preferred_element_type=F32
    )
    by_slot = jnp.concatenate([lifted[:, lanes(p)] for p in range(NQ)], axis=0)
    by_element = pick(by_slot, slot_hot[...].astype(BF16))
    return jnp.concatenate([by_element[p * NB : (p + 1) * NB] for p in range(NQ)], axis=1)


def next_kernel(
    place, state, near, upper, lower, slot_flux, slot_code, slot_hot, lift,
    star, coarse, labels, weights, lists,
    state_out, low_out, faces_out, pair_out, far_out, stack, terms, *, step,
):
    position = place[0]
    odd = lax.rem(position, 2) == 1
    now = state[...] + remote_part(
        position, near, upper, lower, slot_flux, slot_code, slot_hot, lift, stack
    )
    state_out[...] = now
    chain = chain_of(now, star, weights, terms)
    fine = integral_of(chain, taylor_weights(0.0, 1.0 / SUBSTEPS))
    mask = labels[...] == 1
    integral = jnp.concatenate(
        [jnp.where(mask, fine[:, lanes(q)], coarse[step - 1, :, lanes(q)]) for q in range(NQ)],
        axis=1,
    )
    low_out[...] = integral[0:VPAD]
    project_and_send(integral, weights, lists, odd, faces_out, pair_out, far_out)


def last_kernel(
    place, state, near, upper, lower, slot_flux, slot_code, slot_hot, lift, out, stack
):
    total = state[...] + remote_part(
        place[0], near, upper, lower, slot_flux, slot_code, slot_hot, lift, stack
    )
    for q in range(NQ):
        out[:, q, :] = total[:, lanes(q)]


def floats(*shape):
    return jax.ShapeDtypeStruct(shape, F32)


def call(kernel, args, outs, scratch, scalars=0, flops=2.0e7):
    smem = pl.BlockSpec(memory_space=pltpu.SMEM)
    vmem = pl.BlockSpec(memory_space=pltpu.VMEM)
    moved = 4 * sum(math.prod(item.shape) for item in list(args) + list(outs))
    return pl.pallas_call(
        kernel,
        in_specs=[smem] * scalars + [vmem] * (len(args) - scalars),
        out_specs=[vmem] * len(outs),
        out_shape=outs,
        scratch_shapes=[pltpu.VMEM(shape, F32) for shape in scratch],
        compiler_params=pltpu.CompilerParams(vmem_limit_bytes=40 * 2**20),
        cost_estimate=pl.CostEstimate(flops=int(flops), bytes_accessed=moved, transcendentals=0),
    )(*args)


def swaps(count, first):
    pairs = []
    for low in range(count - 2):
        if low % 4 in (first, first + 1):
            pairs += [(low, low + 2), (low + 2, low)]
    return pairs


def local(
    dofs, star, flux_self, flux_other, labels, neighbour_source, orientation,
    fine_send, coarse_send, stiff_time, stiff_vol, face_back, face_front, face_turn,
):
    count = lax.axis_size("dom")
    partners = [(source, source ^ 1) for source in range(count)]
    place = lax.axis_index("dom").astype(jnp.int32).reshape(1)
    lists = jnp.concatenate([fine_send, coarse_send], axis=1).reshape(PEERS * BOTH, 1)
    labels = labels.reshape(1, LANES)
    sent_shapes = [floats(OWN, COLS), floats(2 * BOTH, WIDTH), floats(2 * BOTH, WIDTH)]
    state, low, coarse, faces, pair, far, weights = call(
        first_kernel,
        (place, dofs, star, stiff_time, face_back, lists),
        [floats(NB, COLS), floats(VPAD, COLS), floats(SUBSTEPS - 1, NB, COLS)]
        + sent_shapes
        + [floats(CHAIN_ROWS, LANES)],
        [(120, COLS)],
        scalars=1,
    )
    slot_flux, slot_code, slot_hot, lift = call(
        prepare_kernel,
        (neighbour_source, orientation, flux_other, face_front, face_turn, stiff_vol),
        [floats(16 * NQ, LANES), floats(16, LANES), floats(LANES, LANES), floats(NB, DEEP)],
        [(16 * NQ, FACES)],
    )
    for step in range(SUBSTEPS):
        near = lax.ppermute(pair, "dom", partners)
        message = jnp.concatenate([far, near[BOTH:]], axis=0)
        upper = lax.ppermute(message, "dom", swaps(count, 2))
        lower = lax.ppermute(message, "dom", swaps(count, 0))
        (state,) = call(
            local_kernel,
            (state, low, faces, star, flux_self, flux_other, neighbour_source, orientation, lift),
            [floats(NB, COLS)],
            [(DEEP, COLS)],
        )
        received = (place, state, near, upper, lower, slot_flux, slot_code, slot_hot, lift)
        if step + 1 < SUBSTEPS:
            state, low, faces, pair, far = call(
                functools.partial(next_kernel, step=step + 1),
                received + (star, coarse, labels, weights, lists),
                [floats(NB, COLS), floats(VPAD, COLS)] + sent_shapes,
                [(REM, COLS), (120, COLS)],
                scalars=1,
            )
    (result,) = call(
        last_kernel, received, [floats(NB, NQ, LANES)], [(REM, COLS)], scalars=1
    )
    return result


def solution(mesh):
    split = P(None, None, "dom")
    face = P(None, None, None, "dom")
    row = P(None, "dom")
    in_specs = (split, face, face, face, P("dom"), row, row, row, row, P(), P(), P(), P(), P())
    return jax.shard_map(local, mesh=mesh, in_specs=in_specs, out_specs=split, check_vma=False)
```

```python
import functools
import math

import jax
import jax.numpy as jnp
from jax import lax
from jax.experimental import pallas as pl
from jax.experimental.pallas import tpu as pltpu
from jax.sharding import PartitionSpec as P

ORDER = 6
SUBSTEPS = 4
NQ = 9
NB = 56
NLOW = 35
NF = 21
PEERS = 4
SLOTS = 12
LANES = 128
FPAD = 24
VPAD = 40
BOTH = 2 * SLOTS
WIDTH = 256
COLS = NQ * LANES
FACES = 4 * LANES
REM = 12 * FPAD
OWN = 4 * FPAD
DEEP = REM + OWN + 3 * VPAD
DEEP_PAD = 512
LEVELS = [(0, 35, 40, 56), (120, 20, 24, 40), (192, 10, 16, 24), (240, 4, 8, 16), (264, 1, 8, 8)]
BACK = 288
CHAIN_ROWS = BACK + OWN
HIGH = lax.Precision.HIGH
HIGHEST = lax.Precision.HIGHEST
F32 = jnp.float32
BF16 = jnp.bfloat16


def taylor_weights(start, stop):
    return [
        (stop ** (depth + 1) - start ** (depth + 1)) / math.factorial(depth + 1)
        for depth in range(ORDER)
    ]


def lanes(index):
    return slice(index * LANES, (index + 1) * LANES)


def iota(shape, dim):
    return lax.broadcasted_iota(jnp.int32, shape, dim)


def halves(value):
    top = value.astype(BF16)
    return top, (value - top.astype(F32)).astype(BF16)


def pick(value, hot, contract=((1,), (0,))):
    top, rest = halves(value)
    dims = (contract, ((), ()))
    return lax.dot_general(top, hot, dims, preferred_element_type=F32) + lax.dot_general(
        rest, hot, dims, preferred_element_type=F32
    )


def products(blocks, row_of, rows):
    totals = [None] * NQ
    for position, block in enumerate(blocks):
        for q in range(NQ):
            left = block(q)
            for p in range(NQ):
                term = left * row_of(position, q, p)
                totals[p] = term if totals[p] is None else totals[p] + term
    return totals


def chain_weights(stiff_time, face_back, out):
    out[...] = jnp.zeros(out.shape, F32)
    for start, valid, padded, _ in LEVELS:
        for d in range(3):
            out[start + d * padded : start + d * padded + valid, 0:NB] = stiff_time[d, 0:valid, :]
    for j in range(4):
        out[BACK + j * FPAD : BACK + j * FPAD + NF, 0:NB] = face_back[:, j, :]


def chain_of(first, star, weights, terms):
    now = first
    chain = [first]
    offset = 0
    for start, _, padded, width in LEVELS:
        terms[0 : 3 * padded, :] = jnp.dot(
            weights[start : start + 3 * padded, 0:width],
            now,
            precision=HIGH,
            preferred_element_type=F32,
        )
        blocks = [
            lambda q, d=d: terms[d * padded : (d + 1) * padded, lanes(q)] for d in range(3)
        ]
        totals = products(blocks, lambda d, q, p: star[q, p, d : d + 1, :], padded)
        now = jnp.concatenate(totals, axis=1)
        chain.append(now)
    return chain


def integral_of(chain, weights):
    pieces = []
    edges = [0, 8, 16, 24, 40, 56]
    for low, high in zip(edges[:-1], edges[1:]):
        total = None
        for depth in range(ORDER):
            if chain[depth].shape[0] < high:
                continue
            term = (weights[depth] * (-1) ** depth) * chain[depth][low:high]
            total = term if total is None else total + term
        pieces.append(total)
    return jnp.concatenate(pieces, axis=0)


def face_table(faces):
    rows = []
    for q in range(NQ):
        rows.append(
            jnp.concatenate(
                [faces[j * FPAD : (j + 1) * FPAD, lanes(q)] for j in range(4)], axis=1
            )
        )
    rows.append(jnp.zeros((WIDTH - NQ * FPAD, FACES), F32))
    return jnp.concatenate(rows, axis=0)


def project_and_send(integral, weights, lists, position, faces_out, pair_out, up_out, down_out):
    faces = jnp.dot(
        weights[BACK : BACK + OWN, 0:NB], integral, precision=HIGH, preferred_element_type=F32
    )
    faces_out[...] = faces
    top, rest = halves(face_table(faces))
    hot = jnp.concatenate(
        [
            jnp.where(lists[...] == iota((PEERS * BOTH, LANES), 1) + LANES * j, 1.0, 0.0)
            for j in range(4)
        ],
        axis=1,
    ).astype(BF16)
    dims = (((1,), (1,)), ((), ()))
    sent = lax.dot_general(hot, top, dims, preferred_element_type=F32) + lax.dot_general(
        hot, rest, dims, preferred_element_type=F32
    )
    odd = lax.rem(position, 2) == 1
    first, second = sent[0:BOTH], sent[BOTH : 2 * BOTH]
    pair_out[0:BOTH, :] = jnp.where(odd, second, first)
    pair_out[BOTH : 2 * BOTH, :] = jnp.where(odd, first, second)
    behind_up = lax.rem(position, 4) < 2
    ahead, behind = sent[2 * BOTH : 3 * BOTH], sent[3 * BOTH : 4 * BOTH]
    up_out[...] = jnp.where(behind_up, behind, ahead)
    down_out[...] = jnp.where(behind_up, ahead, behind)


def list_column(fine, coarse):
    row = iota((PEERS * BOTH, LANES), 0)
    peer = (row >= BOTH).astype(jnp.int32) + (row >= 2 * BOTH).astype(jnp.int32)
    peer = peer + (row >= 3 * BOTH).astype(jnp.int32)
    inner = row - BOTH * peer
    total = jnp.zeros((PEERS * BOTH, LANES), F32)
    for kind, entries in enumerate((fine, coarse)):
        here = iota((PEERS * BOTH, LANES), 1) == inner - kind * SLOTS
        for k in range(PEERS):
            total = total + jnp.where(here & (peer == k), entries[k : k + 1, :], 0.0)
    column = jnp.sum(total, axis=1, keepdims=True)
    return jnp.broadcast_to(column, (PEERS * BOTH, LANES)).astype(jnp.int32)


def first_kernel(
    place, dofs, star, stiff_time, face_back, fine_send, coarse_send, labels, *rest
):
    later = rest[:7]
    (
        state_out, low_out, coarse_out, faces_out, pair_out, up_out, down_out,
        weights_out, star_out, labels_out, lists_out,
    ) = rest[7:18]
    later_out = rest[18:25]
    terms, time_here, back_here, wide, fine_here, coarse_here, ready = rest[25:]
    position = place[0]
    moves = [
        (stiff_time, time_here),
        (face_back, back_here),
        (star, star_out),
        (fine_send, fine_here),
        (coarse_send, coarse_here),
        (labels, labels_out),
    ]
    moves += [(dofs.at[q], state_out.at[:, lanes(q)]) for q in range(NQ)]
    moves += list(zip(later, later_out))
    copies = [
        pltpu.make_async_copy(source, target, ready.at[number])
        for number, (source, target) in enumerate(moves)
    ]
    for copy in copies:
        copy.start()
    copies[0].wait()
    copies[1].wait()
    chain_weights(time_here, back_here, weights_out)
    for copy in copies[6 : 6 + NQ]:
        copy.wait()
    copies[2].wait()
    state = state_out[...]
    chain = chain_of(state, star_out, weights_out, terms)
    integral = integral_of(chain, taylor_weights(0.0, 1.0 / SUBSTEPS))
    low_out[...] = integral[0:VPAD]
    for copy in copies[3:6]:
        copy.wait()
    wide[...] = jnp.zeros(wide.shape, F32)
    wide[0:PEERS, 0:SLOTS] = fine_here[...].astype(F32)
    wide[8 : 8 + PEERS, 0:SLOTS] = coarse_here[...].astype(F32)
    lists_out[...] = list_column(wide[0:PEERS], wide[8 : 8 + PEERS])
    project_and_send(
        integral, weights_out, lists_out, position, faces_out, pair_out, up_out, down_out
    )
    for step in range(1, SUBSTEPS):
        coarse_out[step - 1] = integral_of(
            chain, taylor_weights(step / SUBSTEPS, (step + 1) / SUBSTEPS)
        )
    for copy in copies[6 + NQ :]:
        copy.wait()


def prepare_kernel(
    source, orientation, flux_other, face_front, face_turn, stiff_vol,
    slot_flux_out, slot_code_out, slot_hot_out, lift_out, table, fronts, tall,
):
    row = iota((LANES, LANES), 0)
    peer = (row >= BOTH).astype(jnp.int32) + (row >= 2 * BOTH).astype(jnp.int32)
    peer = peer + (row >= 3 * BOTH).astype(jnp.int32)
    inner = row - BOTH * peer
    kind = (inner >= SLOTS).astype(jnp.int32)
    wanted = kind * (PEERS * SLOTS - SLOTS) + peer * SLOTS + inner + FACES
    wanted = jnp.where(row < PEERS * BOTH, wanted, -1)
    blocks = [jnp.where(source[i : i + 1, :] == wanted, 1.0, 0.0) for i in range(4)]
    slot_hot_out[...] = blocks[0] + blocks[1] + blocks[2] + blocks[3]
    hot = jnp.concatenate(blocks, axis=1).astype(BF16)
    codes = jnp.concatenate(
        [
            jnp.where(iota((16, LANES), 0) - 3 * i == orientation[i : i + 1, :], 1.0, 0.0)
            for i in range(4)
        ],
        axis=1,
    ).astype(BF16)
    dims = (((1,), (1,)), ((), ()))
    slot_code_out[...] = lax.dot_general(codes, hot, dims, preferred_element_type=F32)
    table[...] = jnp.zeros(table.shape, F32)
    for i in range(4):
        for q in range(NQ):
            table[16 * q : 16 * q + NQ, lanes(i)] = flux_other[q, :, i, :]
    slot_flux_out[...] = pick(table[...], hot, ((1,), (1,)))

    fronts[...] = jnp.zeros(fronts.shape, F32)
    tall[...] = jnp.zeros(tall.shape, F32)
    for i in range(4):
        fronts[0:NF, i * LANES : i * LANES + NB] = face_front[:, i, :]
    for code in range(3):
        turned = lax.dot_general(
            face_turn[code], fronts[0:NF, :], (((0,), (0,)), ((), ())),
            precision=HIGHEST, preferred_element_type=F32,
        )
        for i in range(4):
            start = FPAD * (3 * i + code)
            tall[start : start + NF, :] = -turned[:, lanes(i)]
    for i in range(4):
        start = REM + FPAD * i
        tall[start : start + NF, :] = -fronts[0:NF, lanes(i)]
    for d in range(3):
        start = REM + OWN + VPAD * d
        tall[start : start + NLOW, 0:NB] = stiff_vol[d]
    lift_out[...] = jnp.transpose(tall[...])[0:NB]


def local_kernel(
    state, low, faces, star, flux_self, flux_other, source, orientation, lift, out, stack,
):
    column = iota((FACES, LANES), 0)
    hot = jnp.concatenate(
        [
            jnp.where(column == source[i : i + 1, :], 1.0, 0.0).astype(BF16)
            for i in range(4)
        ],
        axis=1,
    )
    found = pick(face_table(faces[...]), hot)
    for d in range(3):
        totals = products(
            [lambda q: low[:, lanes(q)]], lambda _, q, p: star[q, p, d : d + 1, :], VPAD
        )
        base = REM + OWN + VPAD * d
        for p in range(NQ):
            stack[base : base + VPAD, lanes(p)] = totals[p]
    for i in range(4):
        totals = products(
            [lambda q: faces[i * FPAD : (i + 1) * FPAD, lanes(q)]],
            lambda _, q, p: flux_self[q, p, i : i + 1, :],
            FPAD,
        )
        for p in range(NQ):
            stack[REM + FPAD * i : REM + FPAD * (i + 1), lanes(p)] = totals[p]
    for i in range(4):
        totals = products(
            [lambda q: found[q * FPAD : (q + 1) * FPAD, lanes(i)]],
            lambda _, q, p: flux_other[q, p, i : i + 1, :],
            FPAD,
        )
        for code in range(3):
            mask = jnp.where(orientation[i : i + 1, :] == code, 1.0, 0.0)
            base = FPAD * (3 * i + code)
            for p in range(NQ):
                stack[base : base + FPAD, lanes(p)] = totals[p] * mask
    out[...] = state[...] + jnp.dot(
        lift[:, 0:DEEP], stack[...], precision=HIGH, preferred_element_type=F32
    )


def remote_part(position, near, upper, lower, slot_flux, slot_code, slot_hot, lift, stack):
    odd = lax.rem(position, 2) == 1
    behind_up = lax.rem(position, 4) < 2
    up, down = upper[...], lower[...]
    behind = jnp.where(behind_up, up, down)
    ahead = jnp.where(behind_up, down, up)
    here = near[0:BOTH, :]
    relayed = slice(BOTH, 2 * BOTH)
    rows = jnp.concatenate(
        [
            jnp.where(odd, here, behind[relayed]),
            jnp.where(odd, ahead[relayed], here),
            behind[0:BOTH],
            ahead[0:BOTH],
            jnp.zeros((LANES - PEERS * BOTH, WIDTH), F32),
        ],
        axis=0,
    )
    received = jnp.transpose(rows)
    totals = products(
        [lambda q: received[q * FPAD : (q + 1) * FPAD]],
        lambda _, q, p: slot_flux[16 * q + p : 16 * q + p + 1, :],
        FPAD,
    )
    for code in range(12):
        mask = slot_code[code : code + 1, :]
        for p in range(NQ):
            stack[FPAD * code : FPAD * (code + 1), lanes(p)] = totals[p] * mask
    lifted = jnp.dot(
        lift[:, 0:REM], stack[...], precision=HIGH, preferred_element_type=F32
    )
    by_slot = jnp.concatenate([lifted[:, lanes(p)] for p in range(NQ)], axis=0)
    by_element = pick(by_slot, slot_hot[...].astype(BF16))
    return jnp.concatenate([by_element[p * NB : (p + 1) * NB] for p in range(NQ)], axis=1)


def next_kernel(
    place, state, near, upper, lower, slot_flux, slot_code, slot_hot, lift,
    star, coarse, labels, weights, lists,
    state_out, low_out, faces_out, pair_out, up_out, down_out, stack, terms, *, step,
):
    position = place[0]
    now = state[...] + remote_part(
        position, near, upper, lower, slot_flux, slot_code, slot_hot, lift, stack
    )
    state_out[...] = now
    chain = chain_of(now, star, weights, terms)
    fine = integral_of(chain, taylor_weights(0.0, 1.0 / SUBSTEPS))
    mask = labels[...] == 1
    integral = jnp.concatenate(
        [jnp.where(mask, fine[:, lanes(q)], coarse[step - 1, :, lanes(q)]) for q in range(NQ)],
        axis=1,
    )
    low_out[...] = integral[0:VPAD]
    project_and_send(
        integral, weights, lists, position, faces_out, pair_out, up_out, down_out
    )


def last_kernel(
    place, state, near, upper, lower, slot_flux, slot_code, slot_hot, lift, out, stack
):
    total = state[...] + remote_part(
        place[0], near, upper, lower, slot_flux, slot_code, slot_hot, lift, stack
    )
    for q in range(NQ):
        out[q] = total[:, lanes(q)]


def floats(*shape):
    return jax.ShapeDtypeStruct(shape, F32)


def call(kernel, args, outs, scratch, scalars=0, inside=False, flops=2.0e7):
    smem = pl.BlockSpec(memory_space=pltpu.SMEM)
    vmem = pl.BlockSpec(memory_space=pltpu.VMEM)
    given = pl.BlockSpec(memory_space=pl.ANY) if inside else vmem
    if inside:
        args = args[:scalars] + tuple(
            pltpu.with_memory_space_constraint(item, pltpu.HBM) for item in args[scalars:]
        )
    moved = 4 * sum(math.prod(item.shape) for item in list(args) + list(outs))
    return pl.pallas_call(
        kernel,
        in_specs=[smem] * scalars + [given] * (len(args) - scalars),
        out_specs=[vmem] * len(outs),
        out_shape=outs,
        scratch_shapes=[
            pltpu.VMEM(item, F32) if isinstance(item, tuple) else item for item in scratch
        ],
        compiler_params=pltpu.CompilerParams(vmem_limit_bytes=40 * 2**20),
        cost_estimate=pl.CostEstimate(flops=int(flops), bytes_accessed=moved, transcendentals=0),
    )(*args)


def swaps(count, first):
    pairs = []
    for low in range(count - 2):
        if low % 4 in (first, first + 1):
            pairs += [(low, low + 2), (low + 2, low)]
    return pairs


def local(
    dofs, star, flux_self, flux_other, labels, neighbour_source, orientation,
    fine_send, coarse_send, stiff_time, stiff_vol, face_back, face_front, face_turn,
):
    count = lax.axis_size("dom")
    partners = [(source, source ^ 1) for source in range(count)]
    place = lax.axis_index("dom").astype(jnp.int32).reshape(1)
    labels = labels.reshape(1, LANES)
    later = (
        flux_self.transpose(1, 2, 0, 3),
        flux_other.transpose(1, 2, 0, 3),
        neighbour_source,
        orientation,
        face_front.transpose(2, 0, 1),
        face_turn,
        stiff_vol.transpose(0, 2, 1),
    )
    star = star.transpose(1, 2, 0, 3)
    back = face_back.transpose(1, 0, 2)
    message = floats(BOTH, WIDTH)
    sent_shapes = [floats(OWN, COLS), floats(2 * BOTH, WIDTH), message, message]
    like = lambda item: jax.ShapeDtypeStruct(item.shape, item.dtype)
    found = call(
        first_kernel,
        (place, dofs.transpose(1, 0, 2), star, stiff_time, back, fine_send, coarse_send, labels)
        + later,
        [floats(NB, COLS), floats(VPAD, COLS), floats(SUBSTEPS - 1, NB, COLS)]
        + sent_shapes
        + [floats(CHAIN_ROWS, LANES), like(star), like(labels)]
        + [jax.ShapeDtypeStruct((PEERS * BOTH, LANES), jnp.int32)]
        + [like(item) for item in later],
        [(120, COLS), stiff_time.shape, back.shape, (16, LANES)]
        + [pltpu.VMEM(item.shape, jnp.int32) for item in (fine_send, coarse_send)]
        + [pltpu.SemaphoreType.DMA((6 + NQ + len(later),))],
        scalars=1,
        inside=True,
    )
    state, low, coarse, faces, pair, up, down, weights, star, labels, lists = found[:11]
    flux_self, flux_other, source, orientation, front, turn, vol = found[11:]
    slot_flux, slot_code, slot_hot, lift = call(
        prepare_kernel,
        (source, orientation, flux_other, front, turn, vol),
        [floats(16 * NQ, LANES), floats(16, LANES), floats(LANES, LANES), floats(NB, DEEP_PAD)],
        [(16 * NQ, FACES), (FPAD, FACES), (DEEP_PAD, LANES)],
    )
    for step in range(SUBSTEPS):
        near = lax.ppermute(pair, "dom", partners)
        if step == 0:
            up, down, lift = lax.optimization_barrier((up, down, lift))
        upper = lax.ppermute(jnp.concatenate([up, near[BOTH:]], axis=0), "dom", swaps(count, 2))
        lower = lax.ppermute(jnp.concatenate([down, near[BOTH:]], axis=0), "dom", swaps(count, 0))
        (state,) = call(
            local_kernel,
            (state, low, faces, star, flux_self, flux_other, source, orientation, lift),
            [floats(NB, COLS)],
            [(DEEP, COLS)],
        )
        received = (place, state, near, upper, lower, slot_flux, slot_code, slot_hot, lift)
        if step + 1 < SUBSTEPS:
            state, low, faces, pair, up, down = call(
                functools.partial(next_kernel, step=step + 1),
                received + (star, coarse, labels, weights, lists),
                [floats(NB, COLS), floats(VPAD, COLS)] + sent_shapes,
                [(REM, COLS), (120, COLS)],
                scalars=1,
            )
    (result,) = call(
        last_kernel, received, [floats(NQ, NB, LANES)], [(REM, COLS)], scalars=1
    )
    return result.transpose(1, 0, 2)


def solution(mesh):
    split = P(None, None, "dom")
    face = P(None, None, None, "dom")
    row = P(None, "dom")
    in_specs = (split, face, face, face, P("dom"), row, row, row, row, P(), P(), P(), P(), P())
    return jax.shard_map(local, mesh=mesh, in_specs=in_specs, out_specs=split, check_vma=False)
```

```python
import functools
import math

import jax
import jax.numpy as jnp
from jax import lax
from jax.experimental import pallas as pl
from jax.experimental.pallas import tpu as pltpu
from jax.sharding import PartitionSpec as P

ORDER = 6
SUBSTEPS = 4
NQ = 9
NB = 56
NLOW = 35
NF = 21
PEERS = 4
SLOTS = 12
LANES = 128
FPAD = 24
VPAD = 40
BOTH = 2 * SLOTS
WIDTH = 256
COLS = NQ * LANES
FACES = 4 * LANES
REM = 12 * FPAD
OWN = 4 * FPAD
DEEP = REM + OWN + 3 * VPAD
DEEP_PAD = 512
LEVELS = [(0, 35, 40, 56), (120, 20, 24, 40), (192, 10, 16, 24), (240, 4, 8, 16), (264, 1, 8, 8)]
BACK = 288
CHAIN_ROWS = BACK + OWN
HIGH = lax.Precision.HIGH
HIGHEST = lax.Precision.HIGHEST
F32 = jnp.float32
BF16 = jnp.bfloat16


def taylor_weights(start, stop):
    return [
        (stop ** (depth + 1) - start ** (depth + 1)) / math.factorial(depth + 1)
        for depth in range(ORDER)
    ]


def lanes(index):
    return slice(index * LANES, (index + 1) * LANES)


def iota(shape, dim):
    return lax.broadcasted_iota(jnp.int32, shape, dim)


def halves(value):
    top = value.astype(BF16)
    return top, (value - top.astype(F32)).astype(BF16)


def pick(value, hot, contract=((1,), (0,))):
    top, rest = halves(value)
    dims = (contract, ((), ()))
    return lax.dot_general(top, hot, dims, preferred_element_type=F32) + lax.dot_general(
        rest, hot, dims, preferred_element_type=F32
    )


def products(blocks, row_of, rows):
    totals = [None] * NQ
    for position, block in enumerate(blocks):
        for q in range(NQ):
            left = block(q)
            for p in range(NQ):
                term = left * row_of(position, q, p)
                totals[p] = term if totals[p] is None else totals[p] + term
    return totals


def chain_weights(stiff_time, face_back, out):
    out[...] = jnp.zeros(out.shape, F32)
    for start, valid, padded, _ in LEVELS:
        for d in range(3):
            out[start + d * padded : start + d * padded + valid, 0:NB] = stiff_time[d, 0:valid, :]
    for j in range(4):
        out[BACK + j * FPAD : BACK + j * FPAD + NF, 0:NB] = face_back[:, j, :]


def chain_of(first, star, weights, terms):
    now = first
    chain = [first]
    offset = 0
    for start, _, padded, width in LEVELS:
        terms[0 : 3 * padded, :] = jnp.dot(
            weights[start : start + 3 * padded, 0:width],
            now,
            precision=HIGH,
            preferred_element_type=F32,
        )
        blocks = [
            lambda q, d=d: terms[d * padded : (d + 1) * padded, lanes(q)] for d in range(3)
        ]
        totals = products(blocks, lambda d, q, p: star[q, p, d : d + 1, :], padded)
        now = jnp.concatenate(totals, axis=1)
        chain.append(now)
    return chain


def integral_of(chain, weights):
    pieces = []
    edges = [0, 8, 16, 24, 40, 56]
    for low, high in zip(edges[:-1], edges[1:]):
        total = None
        for depth in range(ORDER):
            if chain[depth].shape[0] < high:
                continue
            term = (weights[depth] * (-1) ** depth) * chain[depth][low:high]
            total = term if total is None else total + term
        pieces.append(total)
    return jnp.concatenate(pieces, axis=0)


def face_table(faces):
    rows = []
    for q in range(NQ):
        rows.append(
            jnp.concatenate(
                [faces[j * FPAD : (j + 1) * FPAD, lanes(q)] for j in range(4)], axis=1
            )
        )
    rows.append(jnp.zeros((WIDTH - NQ * FPAD, FACES), F32))
    return jnp.concatenate(rows, axis=0)


def project_and_send(integral, weights, lists, position, faces_out, pair_out, up_out, down_out):
    faces = jnp.dot(
        weights[BACK : BACK + OWN, 0:NB], integral, precision=HIGH, preferred_element_type=F32
    )
    faces_out[...] = faces
    top, rest = halves(face_table(faces))
    hot = jnp.concatenate(
        [
            jnp.where(lists[...] == iota((PEERS * BOTH, LANES), 1) + LANES * j, 1.0, 0.0)
            for j in range(4)
        ],
        axis=1,
    ).astype(BF16)
    dims = (((1,), (1,)), ((), ()))
    sent = lax.dot_general(hot, top, dims, preferred_element_type=F32) + lax.dot_general(
        hot, rest, dims, preferred_element_type=F32
    )
    odd = lax.rem(position, 2) == 1
    first, second = sent[0:BOTH], sent[BOTH : 2 * BOTH]
    pair_out[0:BOTH, :] = jnp.where(odd, second, first)
    pair_out[BOTH : 2 * BOTH, :] = jnp.where(odd, first, second)
    behind_up = lax.rem(position, 4) < 2
    ahead, behind = sent[2 * BOTH : 3 * BOTH], sent[3 * BOTH : 4 * BOTH]
    up_out[...] = jnp.where(behind_up, behind, ahead)
    down_out[...] = jnp.where(behind_up, ahead, behind)


def list_column(fine, coarse):
    row = iota((PEERS * BOTH, LANES), 0)
    peer = (row >= BOTH).astype(jnp.int32) + (row >= 2 * BOTH).astype(jnp.int32)
    peer = peer + (row >= 3 * BOTH).astype(jnp.int32)
    inner = row - BOTH * peer
    total = jnp.zeros((PEERS * BOTH, LANES), F32)
    for kind, entries in enumerate((fine, coarse)):
        here = iota((PEERS * BOTH, LANES), 1) == inner - kind * SLOTS
        for k in range(PEERS):
            total = total + jnp.where(here & (peer == k), entries[k : k + 1, :], 0.0)
    column = jnp.sum(total, axis=1, keepdims=True)
    return jnp.broadcast_to(column, (PEERS * BOTH, LANES)).astype(jnp.int32)


def first_kernel(
    place, dofs, star, stiff_time, face_back, fine_send, coarse_send, labels, *rest
):
    later = rest[:7]
    (
        state_out, low_out, coarse_out, faces_out, pair_out, up_out, down_out,
        weights_out, star_out, labels_out, lists_out,
    ) = rest[7:18]
    later_out = rest[18:25]
    terms, time_here, back_here, wide, fine_here, coarse_here, ready = rest[25:]
    position = place[0]
    moves = [
        (stiff_time, time_here),
        (face_back, back_here),
        (star, star_out),
        (fine_send, fine_here),
        (coarse_send, coarse_here),
        (labels, labels_out),
    ]
    moves += [(dofs.at[q], state_out.at[:, lanes(q)]) for q in range(NQ)]
    moves += list(zip(later, later_out))
    copies = [
        pltpu.make_async_copy(source, target, ready.at[number])
        for number, (source, target) in enumerate(moves)
    ]
    for copy in copies:
        copy.start()
    copies[0].wait()
    copies[1].wait()
    chain_weights(time_here, back_here, weights_out)
    for copy in copies[6 : 6 + NQ]:
        copy.wait()
    copies[2].wait()
    state = state_out[...]
    chain = chain_of(state, star_out, weights_out, terms)
    integral = integral_of(chain, taylor_weights(0.0, 1.0 / SUBSTEPS))
    low_out[...] = integral[0:VPAD]
    for copy in copies[3:6]:
        copy.wait()
    wide[...] = jnp.zeros(wide.shape, F32)
    wide[0:PEERS, 0:SLOTS] = fine_here[...].astype(F32)
    wide[8 : 8 + PEERS, 0:SLOTS] = coarse_here[...].astype(F32)
    lists_out[...] = list_column(wide[0:PEERS], wide[8 : 8 + PEERS])
    project_and_send(
        integral, weights_out, lists_out, position, faces_out, pair_out, up_out, down_out
    )
    for step in range(1, SUBSTEPS):
        coarse_out[step - 1] = integral_of(
            chain, taylor_weights(step / SUBSTEPS, (step + 1) / SUBSTEPS)
        )
    for copy in copies[6 + NQ :]:
        copy.wait()


def prepare_kernel(
    source, orientation, flux_other, face_front, face_turn, stiff_vol,
    slot_flux_out, slot_code_out, slot_hot_out, lift_out, table, fronts, tall,
):
    row = iota((LANES, LANES), 0)
    peer = (row >= BOTH).astype(jnp.int32) + (row >= 2 * BOTH).astype(jnp.int32)
    peer = peer + (row >= 3 * BOTH).astype(jnp.int32)
    inner = row - BOTH * peer
    kind = (inner >= SLOTS).astype(jnp.int32)
    wanted = kind * (PEERS * SLOTS - SLOTS) + peer * SLOTS + inner + FACES
    wanted = jnp.where(row < PEERS * BOTH, wanted, -1)
    blocks = [jnp.where(source[i : i + 1, :] == wanted, 1.0, 0.0) for i in range(4)]
    slot_hot_out[...] = blocks[0] + blocks[1] + blocks[2] + blocks[3]
    hot = jnp.concatenate(blocks, axis=1).astype(BF16)
    codes = jnp.concatenate(
        [
            jnp.where(iota((16, LANES), 0) - 3 * i == orientation[i : i + 1, :], 1.0, 0.0)
            for i in range(4)
        ],
        axis=1,
    ).astype(BF16)
    dims = (((1,), (1,)), ((), ()))
    slot_code_out[...] = lax.dot_general(codes, hot, dims, preferred_element_type=F32)
    table[...] = jnp.zeros(table.shape, F32)
    for i in range(4):
        for q in range(NQ):
            table[16 * q : 16 * q + NQ, lanes(i)] = flux_other[q, :, i, :]
    slot_flux_out[...] = pick(table[...], hot, ((1,), (1,)))

    fronts[...] = jnp.zeros(fronts.shape, F32)
    tall[...] = jnp.zeros(tall.shape, F32)
    for i in range(4):
        fronts[0:NF, i * LANES : i * LANES + NB] = face_front[:, i, :]
    for code in range(3):
        turned = lax.dot_general(
            face_turn[code], fronts[0:NF, :], (((0,), (0,)), ((), ())),
            precision=HIGHEST, preferred_element_type=F32,
        )
        for i in range(4):
            start = FPAD * (3 * i + code)
            tall[start : start + NF, :] = -turned[:, lanes(i)]
    for i in range(4):
        start = REM + FPAD * i
        tall[start : start + NF, :] = -fronts[0:NF, lanes(i)]
    for d in range(3):
        start = REM + OWN + VPAD * d
        tall[start : start + NLOW, 0:NB] = stiff_vol[d]
    lift_out[...] = jnp.transpose(tall[...])[0:NB]


def local_kernel(
    state, low, faces, star, flux_self, flux_other, source, orientation, lift, out, stack,
):
    column = iota((FACES, LANES), 0)
    hot = jnp.concatenate(
        [
            jnp.where(column == source[i : i + 1, :], 1.0, 0.0).astype(BF16)
            for i in range(4)
        ],
        axis=1,
    )
    found = pick(face_table(faces[...]), hot)
    for d in range(3):
        totals = products(
            [lambda q: low[:, lanes(q)]], lambda _, q, p: star[q, p, d : d + 1, :], VPAD
        )
        base = REM + OWN + VPAD * d
        for p in range(NQ):
            stack[base : base + VPAD, lanes(p)] = totals[p]
    for i in range(4):
        totals = products(
            [lambda q: faces[i * FPAD : (i + 1) * FPAD, lanes(q)]],
            lambda _, q, p: flux_self[q, p, i : i + 1, :],
            FPAD,
        )
        for p in range(NQ):
            stack[REM + FPAD * i : REM + FPAD * (i + 1), lanes(p)] = totals[p]
    for i in range(4):
        totals = products(
            [lambda q: found[q * FPAD : (q + 1) * FPAD, lanes(i)]],
            lambda _, q, p: flux_other[q, p, i : i + 1, :],
            FPAD,
        )
        for code in range(3):
            mask = jnp.where(orientation[i : i + 1, :] == code, 1.0, 0.0)
            base = FPAD * (3 * i + code)
            for p in range(NQ):
                stack[base : base + FPAD, lanes(p)] = totals[p] * mask
    out[...] = state[...] + jnp.dot(
        lift[:, 0:DEEP], stack[...], precision=HIGH, preferred_element_type=F32
    )


def remote_part(position, near, upper, lower, slot_flux, slot_code, slot_hot, lift, stack):
    odd = lax.rem(position, 2) == 1
    behind_up = lax.rem(position, 4) < 2
    up, down = upper[...], lower[...]
    behind = jnp.where(behind_up, up, down)
    ahead = jnp.where(behind_up, down, up)
    here = near[0:BOTH, :]
    relayed = slice(BOTH, 2 * BOTH)
    rows = jnp.concatenate(
        [
            jnp.where(odd, here, behind[relayed]),
            jnp.where(odd, ahead[relayed], here),
            behind[0:BOTH],
            ahead[0:BOTH],
            jnp.zeros((LANES - PEERS * BOTH, WIDTH), F32),
        ],
        axis=0,
    )
    received = jnp.transpose(rows)
    totals = products(
        [lambda q: received[q * FPAD : (q + 1) * FPAD]],
        lambda _, q, p: slot_flux[16 * q + p : 16 * q + p + 1, :],
        FPAD,
    )
    for code in range(12):
        mask = slot_code[code : code + 1, :]
        for p in range(NQ):
            stack[FPAD * code : FPAD * (code + 1), lanes(p)] = totals[p] * mask
    lifted = jnp.dot(
        lift[:, 0:REM], stack[...], precision=HIGH, preferred_element_type=F32
    )
    by_slot = jnp.concatenate([lifted[:, lanes(p)] for p in range(NQ)], axis=0)
    by_element = pick(by_slot, slot_hot[...].astype(BF16))
    return jnp.concatenate([by_element[p * NB : (p + 1) * NB] for p in range(NQ)], axis=1)


def next_kernel(
    place, state, near, upper, lower, slot_flux, slot_code, slot_hot, lift,
    star, coarse, labels, weights, lists,
    state_out, low_out, faces_out, pair_out, up_out, down_out, stack, terms, *, step,
):
    position = place[0]
    now = state[...] + remote_part(
        position, near, upper, lower, slot_flux, slot_code, slot_hot, lift, stack
    )
    state_out[...] = now
    chain = chain_of(now, star, weights, terms)
    fine = integral_of(chain, taylor_weights(0.0, 1.0 / SUBSTEPS))
    mask = labels[...] == 1
    integral = jnp.concatenate(
        [jnp.where(mask, fine[:, lanes(q)], coarse[step - 1, :, lanes(q)]) for q in range(NQ)],
        axis=1,
    )
    low_out[...] = integral[0:VPAD]
    project_and_send(
        integral, weights, lists, position, faces_out, pair_out, up_out, down_out
    )


def last_kernel(
    place, state, near, upper, lower, slot_flux, slot_code, slot_hot, lift, out, stack
):
    total = state[...] + remote_part(
        place[0], near, upper, lower, slot_flux, slot_code, slot_hot, lift, stack
    )
    for q in range(NQ):
        out[q] = total[:, lanes(q)]


def floats(*shape):
    return jax.ShapeDtypeStruct(shape, F32)


def call(kernel, args, outs, scratch, scalars=0, inside=False, flops=2.0e7):
    smem = pl.BlockSpec(memory_space=pltpu.SMEM)
    vmem = pl.BlockSpec(memory_space=pltpu.VMEM)
    given = pl.BlockSpec(memory_space=pl.ANY) if inside else vmem
    if inside:
        args = args[:scalars] + tuple(
            pltpu.with_memory_space_constraint(item, pltpu.HBM) for item in args[scalars:]
        )
    moved = 4 * sum(math.prod(item.shape) for item in list(args) + list(outs))
    return pl.pallas_call(
        kernel,
        in_specs=[smem] * scalars + [given] * (len(args) - scalars),
        out_specs=[vmem] * len(outs),
        out_shape=outs,
        scratch_shapes=[
            pltpu.VMEM(item, F32) if isinstance(item, tuple) else item for item in scratch
        ],
        compiler_params=pltpu.CompilerParams(vmem_limit_bytes=40 * 2**20),
        cost_estimate=pl.CostEstimate(flops=int(flops), bytes_accessed=moved, transcendentals=0),
    )(*args)


def swaps(count, first):
    pairs = []
    for low in range(count - 2):
        if low % 4 in (first, first + 1):
            pairs += [(low, low + 2), (low + 2, low)]
    return pairs


def local(
    dofs, star, flux_self, flux_other, labels, neighbour_source, orientation,
    fine_send, coarse_send, stiff_time, stiff_vol, face_back, face_front, face_turn,
):
    count = lax.axis_size("dom")
    partners = [(source, source ^ 1) for source in range(count)]
    place = lax.axis_index("dom").astype(jnp.int32).reshape(1)
    labels = labels.reshape(1, LANES)
    later = (
        flux_self.transpose(1, 2, 0, 3),
        flux_other.transpose(1, 2, 0, 3),
        neighbour_source,
        orientation,
        face_front.transpose(2, 0, 1),
        face_turn,
        stiff_vol.transpose(0, 2, 1),
    )
    star = star.transpose(1, 2, 0, 3)
    back = face_back.transpose(1, 0, 2)
    message = floats(BOTH, WIDTH)
    sent_shapes = [floats(OWN, COLS), floats(2 * BOTH, WIDTH), message, message]
    like = lambda item: jax.ShapeDtypeStruct(item.shape, item.dtype)
    found = call(
        first_kernel,
        (place, dofs.transpose(1, 0, 2), star, stiff_time, back, fine_send, coarse_send, labels)
        + later,
        [floats(NB, COLS), floats(VPAD, COLS), floats(SUBSTEPS - 1, NB, COLS)]
        + sent_shapes
        + [floats(CHAIN_ROWS, LANES), like(star), like(labels)]
        + [jax.ShapeDtypeStruct((PEERS * BOTH, LANES), jnp.int32)]
        + [like(item) for item in later],
        [(120, COLS), stiff_time.shape, back.shape, (16, LANES)]
        + [pltpu.VMEM(item.shape, jnp.int32) for item in (fine_send, coarse_send)]
        + [pltpu.SemaphoreType.DMA((6 + NQ + len(later),))],
        scalars=1,
        inside=True,
    )
    state, low, coarse, faces, pair, up, down, weights, star, labels, lists = found[:11]
    flux_self, flux_other, source, orientation, front, turn, vol = found[11:]
    slot_flux, slot_code, slot_hot, lift = call(
        prepare_kernel,
        (source, orientation, flux_other, front, turn, vol),
        [floats(16 * NQ, LANES), floats(16, LANES), floats(LANES, LANES), floats(NB, DEEP_PAD)],
        [(16 * NQ, FACES), (FPAD, FACES), (DEEP_PAD, LANES)],
    )
    for step in range(SUBSTEPS):
        near = lax.ppermute(pair, "dom", partners)
        if step == 0:
            up, down, lift = lax.optimization_barrier((up, down, lift))
        lower = jnp.concatenate([down, near[BOTH:]], axis=0)
        lower, up, relayed = lax.optimization_barrier((lower, up, near[BOTH:]))
        upper = jnp.concatenate([up, relayed], axis=0)
        upper = lax.ppermute(upper, "dom", swaps(count, 2))
        lower = lax.ppermute(lower, "dom", swaps(count, 0))
        (state,) = call(
            local_kernel,
            (state, low, faces, star, flux_self, flux_other, source, orientation, lift),
            [floats(NB, COLS)],
            [(DEEP, COLS)],
        )
        received = (place, state, near, upper, lower, slot_flux, slot_code, slot_hot, lift)
        if step + 1 < SUBSTEPS:
            state, low, faces, pair, up, down = call(
                functools.partial(next_kernel, step=step + 1),
                received + (star, coarse, labels, weights, lists),
                [floats(NB, COLS), floats(VPAD, COLS)] + sent_shapes,
                [(REM, COLS), (120, COLS)],
                scalars=1,
            )
    (result,) = call(
        last_kernel, received, [floats(NQ, NB, LANES)], [(REM, COLS)], scalars=1
    )
    return result.transpose(1, 0, 2)


def solution(mesh):
    split = P(None, None, "dom")
    face = P(None, None, None, "dom")
    row = P(None, "dom")
    in_specs = (split, face, face, face, P("dom"), row, row, row, row, P(), P(), P(), P(), P())
    return jax.shard_map(local, mesh=mesh, in_specs=in_specs, out_specs=split, check_vma=False)
```

```python
import functools
import math

import jax
import jax.numpy as jnp
from jax import lax
from jax.experimental import pallas as pl
from jax.experimental.pallas import tpu as pltpu
from jax.sharding import PartitionSpec as P

ORDER = 6
SUBSTEPS = 4
NQ = 9
NB = 56
NLOW = 35
NF = 21
PEERS = 4
SLOTS = 12
LANES = 128
FPAD = 24
VPAD = 40
BOTH = 2 * SLOTS
WIDTH = 256
COLS = NQ * LANES
FACES = 4 * LANES
REM = 12 * FPAD
SLOT_PAD = 32
SLOT_REM = 12 * SLOT_PAD
OWN = 4 * FPAD
DEEP = REM + OWN + 3 * VPAD
DEEP_PAD = 512
LEVELS = [(0, 35, 40, 128), (128, 20, 24, 80), (208, 10, 16, 48), (256, 4, 8, 32), (288, 1, 8, 32)]
BACK = 320
CHAIN_ROWS = BACK + OWN
TAIL = 96
PART = 64
HIGH = lax.Precision.HIGH
HIGHEST = lax.Precision.HIGHEST
F32 = jnp.float32
BF16 = jnp.bfloat16


def taylor_weights(start, stop):
    return [
        (stop ** (depth + 1) - start ** (depth + 1)) / math.factorial(depth + 1)
        for depth in range(ORDER)
    ]


def lanes(index):
    return slice(index * LANES, (index + 1) * LANES)


def iota(shape, dim):
    return lax.broadcasted_iota(jnp.int32, shape, dim)


def halves(value):
    top = value.astype(BF16)
    return top, (value - top.astype(F32)).astype(BF16)


def pick(value, hot):
    return jnp.dot(
        jnp.concatenate(halves(value), axis=1),
        jnp.concatenate([hot, hot], axis=0),
        preferred_element_type=F32,
    )


def pick_rows(hot, value):
    return lax.dot_general(
        jnp.concatenate([hot, hot], axis=1),
        jnp.concatenate(halves(value), axis=1),
        (((1,), (1,)), ((), ())),
        preferred_element_type=F32,
    )


def pick_across(value, hot):
    return lax.dot_general(
        jnp.concatenate(halves(value), axis=1),
        jnp.concatenate([hot, hot], axis=1),
        (((1,), (1,)), ((), ())),
        preferred_element_type=F32,
    )


def stacked(value):
    top = value.astype(BF16).astype(F32)
    rest = value - top
    fill = PART - value.shape[0]
    gap = [jnp.zeros((fill, value.shape[1]), F32)] if fill else []
    return jnp.concatenate([top] + gap + [rest] + gap + [top] + gap, axis=0).astype(BF16)


def products(blocks, row_of, rows):
    totals = [None] * NQ
    for q in range(NQ):
        for position, block in enumerate(blocks):
            left = block(q)
            for p in range(NQ):
                term = left * row_of(position, q, p)
                totals[p] = term if totals[p] is None else totals[p] + term
    return totals


def chain_weights(stiff_time, face_back, out, raw):
    raw[...] = jnp.zeros(raw.shape, F32)
    for start, valid, padded, _ in LEVELS:
        for d in range(3):
            raw[start + d * padded : start + d * padded + valid, 0:NB] = stiff_time[d, 0:valid, :]
    for j in range(4):
        raw[BACK + j * FPAD : BACK + j * FPAD + NF, 0:NB] = face_back[:, j, :]
    once = raw[...]
    top = once.astype(BF16).astype(F32)
    out[:, 0:LANES] = (top + pltpu.roll(top, PART, 1)).astype(BF16)
    out[:, LANES : 2 * LANES] = (once - top).astype(BF16)


def weigh(weights, start, rows, value):
    return jnp.dot(
        weights[start : start + rows, 0 : 3 * PART], stacked(value), preferred_element_type=F32
    )


def chain_of(first, star, weights):
    now = first
    chain = [first]
    for start, _, padded, rows in LEVELS:
        found = weigh(weights, start, rows, now)
        blocks = [
            lambda q, d=d: found[d * padded : (d + 1) * padded, lanes(q)] for d in range(3)
        ]
        totals = products(blocks, lambda d, q, p: star[q, p, d : d + 1, :], padded)
        now = jnp.concatenate(totals, axis=1)
        chain.append(now)
    return chain


def integral_of(chain, weights):
    pieces = []
    edges = [0, 8, 16, 24, 40, 56]
    for low, high in zip(edges[:-1], edges[1:]):
        total = None
        for depth in range(ORDER):
            if chain[depth].shape[0] < high:
                continue
            term = (weights[depth] * (-1) ** depth) * chain[depth][low:high]
            total = term if total is None else total + term
        pieces.append(total)
    return jnp.concatenate(pieces, axis=0)


def face_table(faces):
    rows = []
    for q in range(NQ):
        rows.append(
            jnp.concatenate(
                [faces[j * FPAD : (j + 1) * FPAD, lanes(q)] for j in range(4)], axis=1
            )
        )
    rows.append(jnp.zeros((WIDTH - NQ * FPAD, FACES), F32))
    return jnp.concatenate(rows, axis=0)


def project_and_send(integral, weights, lists, position, faces_out, pair_out, up_out, down_out):
    faces = weigh(weights, BACK, OWN, integral)
    faces_out[...] = faces
    hot = jnp.concatenate(
        [
            jnp.where(lists[...] == iota((PEERS * BOTH, LANES), 1) + LANES * j, 1.0, 0.0)
            for j in range(4)
        ],
        axis=1,
    ).astype(BF16)
    sent = pick_rows(hot, face_table(faces))
    odd = lax.rem(position, 2) == 1
    first, second = sent[0:BOTH], sent[BOTH : 2 * BOTH]
    pair_out[0:BOTH, :] = jnp.where(odd, second, first)
    pair_out[BOTH : 2 * BOTH, :] = jnp.where(odd, first, second)
    behind_up = lax.rem(position, 4) < 2
    ahead, behind = sent[2 * BOTH : 3 * BOTH], sent[3 * BOTH : 4 * BOTH]
    up_out[...] = jnp.where(behind_up, behind, ahead)
    down_out[...] = jnp.where(behind_up, ahead, behind)


def list_column(fine, coarse):
    row = iota((PEERS * BOTH, LANES), 0)
    peer = (row >= BOTH).astype(jnp.int32) + (row >= 2 * BOTH).astype(jnp.int32)
    peer = peer + (row >= 3 * BOTH).astype(jnp.int32)
    inner = row - BOTH * peer
    total = jnp.zeros((PEERS * BOTH, LANES), F32)
    for kind, entries in enumerate((fine, coarse)):
        here = iota((PEERS * BOTH, LANES), 1) == inner - kind * SLOTS
        for k in range(PEERS):
            total = total + jnp.where(here & (peer == k), entries[k : k + 1, :], 0.0)
    column = jnp.sum(total, axis=1, keepdims=True)
    return jnp.broadcast_to(column, (PEERS * BOTH, LANES)).astype(jnp.int32)


def first_kernel(
    place, dofs, star, stiff_time, face_back, fine_send, coarse_send, labels, *rest
):
    later = rest[:7]
    (
        state_out, low_out, tail_out, faces_out, pair_out, up_out, down_out,
        weights_out, star_out, labels_out, lists_out,
    ) = rest[7:18]
    later_out = rest[18:25]
    raw, dofs_here, time_here, back_here, wide, fine_here, coarse_here, ready = rest[25:]
    position = place[0]
    moves = [
        (dofs, dofs_here),
        (stiff_time, time_here),
        (face_back, back_here),
        (star, star_out),
        (fine_send, fine_here),
        (coarse_send, coarse_here),
        (labels, labels_out),
    ]
    first = len(moves)
    moves += list(zip(later, later_out))
    copies = [
        pltpu.make_async_copy(source, target, ready.at[number])
        for number, (source, target) in enumerate(moves)
    ]
    for copy in copies:
        copy.start()
    for copy in copies[1:3]:
        copy.wait()
    chain_weights(time_here, back_here, weights_out, raw)
    copies[0].wait()
    state = jnp.concatenate([dofs_here[q] for q in range(NQ)], axis=1)
    state_out[...] = state
    copies[3].wait()
    chain = chain_of(state, star_out, weights_out)
    integral = integral_of(chain, taylor_weights(0.0, 1.0 / SUBSTEPS))
    low_out[...] = integral[0:VPAD]
    for copy in copies[4:first]:
        copy.wait()
    wide[...] = jnp.zeros(wide.shape, F32)
    wide[0:PEERS, 0:SLOTS] = fine_here[...].astype(F32)
    wide[8 : 8 + PEERS, 0:SLOTS] = coarse_here[...].astype(F32)
    lists_out[...] = list_column(wide[0:PEERS], wide[8 : 8 + PEERS])
    project_and_send(
        integral, weights_out, lists_out, position, faces_out, pair_out, up_out, down_out
    )
    tail_out[...] = jnp.concatenate(chain[1:], axis=0)
    for copy in copies[first:]:
        copy.wait()


def prepare_kernel(
    state, tail, source, orientation, flux_other, face_front, face_turn, stiff_vol,
    coarse_out, slot_flux_out, slot_code_out, slot_hot_out, lift_out, slot_lift_out,
    table, fronts, tall, slot_tall,
):
    chain = [state[...]]
    start = 0
    for _, _, padded, _ in LEVELS:
        chain.append(tail[start : start + padded, :])
        start += padded
    for step in range(1, SUBSTEPS):
        coarse_out[step - 1] = integral_of(
            chain, taylor_weights(step / SUBSTEPS, (step + 1) / SUBSTEPS)
        )
    row = iota((LANES, LANES), 0)
    peer = (row >= BOTH).astype(jnp.int32) + (row >= 2 * BOTH).astype(jnp.int32)
    peer = peer + (row >= 3 * BOTH).astype(jnp.int32)
    inner = row - BOTH * peer
    kind = (inner >= SLOTS).astype(jnp.int32)
    wanted = kind * (PEERS * SLOTS - SLOTS) + peer * SLOTS + inner + FACES
    wanted = jnp.where(row < PEERS * BOTH, wanted, -1)
    blocks = [jnp.where(source[i : i + 1, :] == wanted, 1.0, 0.0) for i in range(4)]
    slot_hot_out[...] = blocks[0] + blocks[1] + blocks[2] + blocks[3]
    hot = jnp.concatenate(blocks, axis=1).astype(BF16)
    codes = jnp.concatenate(
        [
            jnp.where(iota((16, LANES), 0) - 3 * i == orientation[i : i + 1, :], 1.0, 0.0)
            for i in range(4)
        ],
        axis=1,
    ).astype(BF16)
    dims = (((1,), (1,)), ((), ()))
    slot_code_out[...] = lax.dot_general(codes, hot, dims, preferred_element_type=F32)
    table[...] = jnp.zeros(table.shape, F32)
    for i in range(4):
        for q in range(NQ):
            table[16 * q : 16 * q + NQ, lanes(i)] = flux_other[q, :, i, :]
    slot_flux_out[...] = pick_across(table[...], hot)

    fronts[...] = jnp.zeros(fronts.shape, F32)
    tall[...] = jnp.zeros(tall.shape, F32)
    slot_tall[...] = jnp.zeros(slot_tall.shape, F32)
    for i in range(4):
        fronts[0:NF, i * LANES : i * LANES + NB] = face_front[:, i, :]
    for code in range(3):
        turned = lax.dot_general(
            face_turn[code], fronts[0:NF, :], (((0,), (0,)), ((), ())),
            precision=HIGHEST, preferred_element_type=F32,
        )
        for i in range(4):
            start = FPAD * (3 * i + code)
            tall[start : start + NF, :] = -turned[:, lanes(i)]
            start = SLOT_PAD * (3 * i + code)
            slot_tall[start : start + NF, :] = -turned[:, lanes(i)]
    for i in range(4):
        start = REM + FPAD * i
        tall[start : start + NF, :] = -fronts[0:NF, lanes(i)]
    for d in range(3):
        start = REM + OWN + VPAD * d
        tall[start : start + NLOW, 0:NB] = stiff_vol[d]
    lift_out[...] = jnp.transpose(tall[...])[0:NB]
    whole = jnp.transpose(slot_tall[...])[0:PART]
    top = whole.astype(BF16)
    slot_lift_out[0:PART, 0:SLOT_REM] = top
    slot_lift_out[0:PART, SLOT_REM:] = top
    slot_lift_out[PART:, 0:SLOT_REM] = (whole - top.astype(F32)).astype(BF16)
    slot_lift_out[PART:, SLOT_REM:] = jnp.zeros((PART, SLOT_REM), BF16)


def local_kernel(
    state, low, faces, star, flux_self, flux_other, source, orientation, lift, out, stack,
):
    column = iota((FACES, LANES), 0)
    hot = jnp.concatenate(
        [
            jnp.where(column == source[i : i + 1, :], 1.0, 0.0).astype(BF16)
            for i in range(4)
        ],
        axis=1,
    )
    found = pick(face_table(faces[...]), hot)
    for d in range(3):
        totals = products(
            [lambda q: low[:, lanes(q)]], lambda _, q, p: star[q, p, d : d + 1, :], VPAD
        )
        base = REM + OWN + VPAD * d
        for p in range(NQ):
            stack[base : base + VPAD, lanes(p)] = totals[p]
    for i in range(4):
        totals = products(
            [lambda q: faces[i * FPAD : (i + 1) * FPAD, lanes(q)]],
            lambda _, q, p: flux_self[q, p, i : i + 1, :],
            FPAD,
        )
        for p in range(NQ):
            stack[REM + FPAD * i : REM + FPAD * (i + 1), lanes(p)] = totals[p]
    for i in range(4):
        totals = products(
            [lambda q: found[q * FPAD : (q + 1) * FPAD, lanes(i)]],
            lambda _, q, p: flux_other[q, p, i : i + 1, :],
            FPAD,
        )
        for code in range(3):
            mask = jnp.where(orientation[i : i + 1, :] == code, 1.0, 0.0)
            base = FPAD * (3 * i + code)
            for p in range(NQ):
                stack[base : base + FPAD, lanes(p)] = totals[p] * mask
    out[...] = state[...] + jnp.dot(
        lift[:, 0:DEEP], stack[...], precision=HIGH, preferred_element_type=F32
    )


def remote_part(position, near, upper, lower, slot_flux, slot_code, slot_hot, lift, stack):
    odd = lax.rem(position, 2) == 1
    behind_up = lax.rem(position, 4) < 2
    up, down = upper[...], lower[...]
    behind = jnp.where(behind_up, up, down)
    ahead = jnp.where(behind_up, down, up)
    here = near[0:BOTH, :]
    relayed = slice(BOTH, 2 * BOTH)
    rows = jnp.concatenate(
        [
            jnp.where(odd, here, behind[relayed]),
            jnp.where(odd, ahead[relayed], here),
            behind[0:BOTH],
            ahead[0:BOTH],
            jnp.zeros((LANES - PEERS * BOTH, WIDTH), F32),
        ],
        axis=0,
    )
    received = jnp.transpose(rows)
    totals = products(
        [lambda q: received[q * FPAD : (q + 1) * FPAD]],
        lambda _, q, p: slot_flux[16 * q + p : 16 * q + p + 1, :],
        FPAD,
    )
    codes = [
        jnp.broadcast_to(slot_code[code : code + 1, :], (SLOT_PAD, LANES)).astype(BF16)
        for code in range(12)
    ]
    gap = jnp.zeros((SLOT_PAD - FPAD, LANES), F32)
    for p in range(NQ):
        for half, part in enumerate(halves(jnp.concatenate([totals[p], gap], axis=0))):
            for code in range(12):
                start = SLOT_REM * half + SLOT_PAD * code
                stack[start : start + SLOT_PAD, lanes(p)] = part * codes[code]
    lifted = jnp.dot(lift[...], stack[...], preferred_element_type=F32)
    lifted = lifted[0:NB] + lifted[PART : PART + NB]
    by_slot = jnp.concatenate([lifted[:, lanes(p)] for p in range(NQ)], axis=0)
    by_element = pick(by_slot, slot_hot[...].astype(BF16))
    return jnp.concatenate([by_element[p * NB : (p + 1) * NB] for p in range(NQ)], axis=1)


def next_kernel(
    place, state, near, upper, lower, slot_flux, slot_code, slot_hot, lift,
    star, coarse, labels, weights, lists,
    state_out, low_out, faces_out, pair_out, up_out, down_out, stack, *, step,
):
    position = place[0]
    now = state[...] + remote_part(
        position, near, upper, lower, slot_flux, slot_code, slot_hot, lift, stack
    )
    state_out[...] = now
    chain = chain_of(now, star, weights)
    fine = integral_of(chain, taylor_weights(0.0, 1.0 / SUBSTEPS))
    mask = labels[...] == 1
    integral = jnp.concatenate(
        [jnp.where(mask, fine[:, lanes(q)], coarse[step - 1, :, lanes(q)]) for q in range(NQ)],
        axis=1,
    )
    low_out[...] = integral[0:VPAD]
    project_and_send(
        integral, weights, lists, position, faces_out, pair_out, up_out, down_out
    )


def last_kernel(
    place, state, near, upper, lower, slot_flux, slot_code, slot_hot, lift, out, stack
):
    total = state[...] + remote_part(
        place[0], near, upper, lower, slot_flux, slot_code, slot_hot, lift, stack
    )
    for q in range(NQ):
        out[q] = total[:, lanes(q)]


def floats(*shape):
    return jax.ShapeDtypeStruct(shape, F32)


def call(kernel, args, outs, scratch, scalars=0, inside=False, flops=2.0e7):
    smem = pl.BlockSpec(memory_space=pltpu.SMEM)
    vmem = pl.BlockSpec(memory_space=pltpu.VMEM)
    given = pl.BlockSpec(memory_space=pl.ANY) if inside else vmem
    if inside:
        args = args[:scalars] + tuple(
            pltpu.with_memory_space_constraint(item, pltpu.HBM) for item in args[scalars:]
        )
    moved = 4 * sum(math.prod(item.shape) for item in list(args) + list(outs))
    return pl.pallas_call(
        kernel,
        in_specs=[smem] * scalars + [given] * (len(args) - scalars),
        out_specs=[vmem] * len(outs),
        out_shape=outs,
        scratch_shapes=[
            pltpu.VMEM(item, F32) if isinstance(item, tuple) else item for item in scratch
        ],
        compiler_params=pltpu.CompilerParams(vmem_limit_bytes=40 * 2**20),
        cost_estimate=pl.CostEstimate(flops=int(flops), bytes_accessed=moved, transcendentals=0),
    )(*args)


def swaps(count, first):
    pairs = []
    for low in range(count - 2):
        if low % 4 in (first, first + 1):
            pairs += [(low, low + 2), (low + 2, low)]
    return pairs


def local(
    dofs, star, flux_self, flux_other, labels, neighbour_source, orientation,
    fine_send, coarse_send, stiff_time, stiff_vol, face_back, face_front, face_turn,
):
    count = lax.axis_size("dom")
    partners = [(source, source ^ 1) for source in range(count)]
    place = lax.axis_index("dom").astype(jnp.int32).reshape(1)
    labels = labels.reshape(1, LANES)
    later = (
        flux_self.transpose(1, 2, 0, 3),
        flux_other.transpose(1, 2, 0, 3),
        neighbour_source,
        orientation,
        face_front.transpose(2, 0, 1),
        face_turn,
        stiff_vol.transpose(0, 2, 1),
    )
    star = star.transpose(1, 2, 0, 3)
    back = face_back.transpose(1, 0, 2)
    message = floats(BOTH, WIDTH)
    stack = pltpu.VMEM((2 * SLOT_REM, COLS), BF16)
    sent_shapes = [floats(OWN, COLS), floats(2 * BOTH, WIDTH), message, message]
    like = lambda item: jax.ShapeDtypeStruct(item.shape, item.dtype)
    found = call(
        first_kernel,
        (place, dofs.transpose(1, 0, 2), star, stiff_time, back, fine_send, coarse_send, labels)
        + later,
        [floats(NB, COLS), floats(VPAD, COLS), floats(TAIL, COLS)]
        + sent_shapes
        + [jax.ShapeDtypeStruct((CHAIN_ROWS, 2 * LANES), BF16), like(star), like(labels)]
        + [jax.ShapeDtypeStruct((PEERS * BOTH, LANES), jnp.int32)]
        + [like(item) for item in later],
        [(CHAIN_ROWS, LANES), (NQ, NB, LANES), stiff_time.shape, back.shape, (16, LANES)]
        + [pltpu.VMEM(item.shape, jnp.int32) for item in (fine_send, coarse_send)]
        + [pltpu.SemaphoreType.DMA((7 + len(later),))],
        scalars=1,
        inside=True,
    )
    state, low, tail, faces, pair, up, down, weights, star, labels, lists = found[:11]
    flux_self, flux_other, source, orientation, front, turn, vol = found[11:]
    coarse, slot_flux, slot_code, slot_hot, lift, slot_lift = call(
        prepare_kernel,
        (state, tail, source, orientation, flux_other, front, turn, vol),
        [floats(SUBSTEPS - 1, NB, COLS), floats(16 * NQ, LANES), floats(16, LANES), floats(LANES, LANES), floats(NB, DEEP_PAD),
         jax.ShapeDtypeStruct((2 * PART, 2 * SLOT_REM), BF16)],
        [(16 * NQ, FACES), (FPAD, FACES), (DEEP_PAD, LANES), (SLOT_REM, LANES)],
    )
    for step in range(SUBSTEPS):
        near = lax.ppermute(pair, "dom", partners)
        if step == 0:
            up, down, lift = lax.optimization_barrier((up, down, lift))
        lower = jnp.concatenate([down, near[BOTH:]], axis=0)
        lower, up, relayed = lax.optimization_barrier((lower, up, near[BOTH:]))
        upper = jnp.concatenate([up, relayed], axis=0)
        upper = lax.ppermute(upper, "dom", swaps(count, 2))
        lower = lax.ppermute(lower, "dom", swaps(count, 0))
        (state,) = call(
            local_kernel,
            (state, low, faces, star, flux_self, flux_other, source, orientation, lift),
            [floats(NB, COLS)],
            [(DEEP, COLS)],
        )
        received = (place, state, near, upper, lower, slot_flux, slot_code, slot_hot, slot_lift)
        if step + 1 < SUBSTEPS:
            state, low, faces, pair, up, down = call(
                functools.partial(next_kernel, step=step + 1),
                received + (star, coarse, labels, weights, lists),
                [floats(NB, COLS), floats(VPAD, COLS)] + sent_shapes,
                [stack],
                scalars=1,
            )
    (result,) = call(
        last_kernel, received, [floats(NQ, NB, LANES)], [stack], scalars=1
    )
    return result.transpose(1, 0, 2)


def solution(mesh):
    split = P(None, None, "dom")
    face = P(None, None, None, "dom")
    row = P(None, "dom")
    in_specs = (split, face, face, face, P("dom"), row, row, row, row, P(), P(), P(), P(), P())
    return jax.shard_map(local, mesh=mesh, in_specs=in_specs, out_specs=split, check_vma=False)
```

```python
import functools
import math

import jax
import jax.numpy as jnp
from jax import lax
from jax.experimental import pallas as pl
from jax.experimental.pallas import tpu as pltpu
from jax.sharding import PartitionSpec as P

ORDER = 6
SUBSTEPS = 4
NQ = 9
NB = 56
NLOW = 35
NF = 21
PEERS = 4
SLOTS = 12
LANES = 128
FPAD = 24
VPAD = 40
BOTH = 2 * SLOTS
WIDTH = 256
COLS = NQ * LANES
FACES = 4 * LANES
REM = 12 * FPAD
SLOT_PAD = 32
SLOT_REM = 12 * SLOT_PAD
OWN = 4 * FPAD
DEEP = REM + OWN + 3 * VPAD
DEEP_PAD = 512
LEVELS = [(0, 35, 40, 128), (128, 20, 24, 80), (208, 10, 16, 48), (256, 4, 8, 32), (288, 1, 8, 32)]
BACK = 320
CHAIN_ROWS = BACK + OWN
TAIL = 96
PART = 64
HIGH = lax.Precision.HIGH
HIGHEST = lax.Precision.HIGHEST
F32 = jnp.float32
BF16 = jnp.bfloat16


def taylor_weights(start, stop):
    return [
        (stop ** (depth + 1) - start ** (depth + 1)) / math.factorial(depth + 1)
        for depth in range(ORDER)
    ]


def lanes(index):
    return slice(index * LANES, (index + 1) * LANES)


def iota(shape, dim):
    return lax.broadcasted_iota(jnp.int32, shape, dim)


def halves(value):
    top = value.astype(BF16)
    return top, (value - top.astype(F32)).astype(BF16)


def pick(value, hot):
    return jnp.dot(
        jnp.concatenate(halves(value), axis=1),
        jnp.concatenate([hot, hot], axis=0),
        preferred_element_type=F32,
    )


def pick_rows(hot, value):
    return lax.dot_general(
        jnp.concatenate([hot, hot], axis=1),
        jnp.concatenate(halves(value), axis=1),
        (((1,), (1,)), ((), ())),
        preferred_element_type=F32,
    )


def pick_across(value, hot):
    return lax.dot_general(
        jnp.concatenate(halves(value), axis=1),
        jnp.concatenate([hot, hot], axis=1),
        (((1,), (1,)), ((), ())),
        preferred_element_type=F32,
    )


def stacked(value):
    top = value.astype(BF16).astype(F32)
    rest = value - top
    fill = PART - value.shape[0]
    gap = [jnp.zeros((fill, value.shape[1]), F32)] if fill else []
    return jnp.concatenate([top] + gap + [rest] + gap + [top] + gap, axis=0).astype(BF16)


def products(blocks, row_of, rows):
    totals = [None] * NQ
    for q in range(NQ):
        for position, block in enumerate(blocks):
            left = block(q)
            for p in range(NQ):
                term = left * row_of(position, q, p)
                totals[p] = term if totals[p] is None else totals[p] + term
    return totals


def chain_weights(stiff_time, face_back, out, raw):
    raw[...] = jnp.zeros(raw.shape, F32)
    for start, valid, padded, _ in LEVELS:
        for d in range(3):
            raw[start + d * padded : start + d * padded + valid, 0:NB] = stiff_time[d, 0:valid, :]
    for j in range(4):
        raw[BACK + j * FPAD : BACK + j * FPAD + NF, 0:NB] = face_back[:, j, :]
    once = raw[...]
    top = once.astype(BF16).astype(F32)
    out[:, 0:LANES] = (top + pltpu.roll(top, PART, 1)).astype(BF16)
    out[:, LANES : 2 * LANES] = (once - top).astype(BF16)


def weigh(weights, start, rows, value):
    return jnp.dot(
        weights[start : start + rows, 0 : 3 * PART], stacked(value), preferred_element_type=F32
    )


def chain_of(first, star, weights):
    now = first
    chain = [first]
    for start, _, padded, rows in LEVELS:
        found = weigh(weights, start, rows, now)
        blocks = [
            lambda q, d=d: found[d * padded : (d + 1) * padded, lanes(q)] for d in range(3)
        ]
        totals = products(blocks, lambda d, q, p: star[q, p, d : d + 1, :], padded)
        now = jnp.concatenate(totals, axis=1)
        chain.append(now)
    return chain


def integral_of(chain, weights):
    pieces = []
    edges = [0, 8, 16, 24, 40, 56]
    for low, high in zip(edges[:-1], edges[1:]):
        total = None
        for depth in range(ORDER):
            if chain[depth].shape[0] < high:
                continue
            term = (weights[depth] * (-1) ** depth) * chain[depth][low:high]
            total = term if total is None else total + term
        pieces.append(total)
    return jnp.concatenate(pieces, axis=0)


def face_table(faces):
    rows = []
    for q in range(NQ):
        rows.append(
            jnp.concatenate(
                [faces[j * FPAD : (j + 1) * FPAD, lanes(q)] for j in range(4)], axis=1
            )
        )
    rows.append(jnp.zeros((WIDTH - NQ * FPAD, FACES), F32))
    return jnp.concatenate(rows, axis=0)


def project_and_send(integral, weights, lists, position, faces_out, pair_out, up_out, down_out):
    faces = weigh(weights, BACK, OWN, integral)
    faces_out[...] = faces
    hot = jnp.concatenate(
        [
            jnp.where(lists[...] == iota((PEERS * BOTH, LANES), 1) + LANES * j, 1.0, 0.0)
            for j in range(4)
        ],
        axis=1,
    ).astype(BF16)
    sent = pick_rows(hot, face_table(faces))
    odd = lax.rem(position, 2) == 1
    first, second = sent[0:BOTH], sent[BOTH : 2 * BOTH]
    pair_out[0:BOTH, :] = jnp.where(odd, second, first)
    pair_out[BOTH : 2 * BOTH, :] = jnp.where(odd, first, second)
    behind_up = lax.rem(position, 4) < 2
    ahead, behind = sent[2 * BOTH : 3 * BOTH], sent[3 * BOTH : 4 * BOTH]
    up_out[...] = jnp.where(behind_up, behind, ahead)
    down_out[...] = jnp.where(behind_up, ahead, behind)


def list_column(fine, coarse):
    row = iota((PEERS * BOTH, LANES), 0)
    peer = (row >= BOTH).astype(jnp.int32) + (row >= 2 * BOTH).astype(jnp.int32)
    peer = peer + (row >= 3 * BOTH).astype(jnp.int32)
    inner = row - BOTH * peer
    total = jnp.zeros((PEERS * BOTH, LANES), F32)
    for kind, entries in enumerate((fine, coarse)):
        here = iota((PEERS * BOTH, LANES), 1) == inner - kind * SLOTS
        for k in range(PEERS):
            total = total + jnp.where(here & (peer == k), entries[k : k + 1, :], 0.0)
    column = jnp.sum(total, axis=1, keepdims=True)
    return jnp.broadcast_to(column, (PEERS * BOTH, LANES)).astype(jnp.int32)


def first_kernel(
    place, dofs, star, stiff_time, face_back, fine_send, coarse_send, labels, *rest
):
    later = rest[:7]
    (
        state_out, low_out, tail_out, faces_out, pair_out, up_out, down_out,
        weights_out, star_out, labels_out, lists_out,
    ) = rest[7:18]
    later_out = rest[18:25]
    raw, dofs_here, time_here, back_here, wide, fine_here, coarse_here, ready = rest[25:]
    position = place[0]
    moves = [
        (dofs, dofs_here),
        (stiff_time, time_here),
        (face_back, back_here),
        (star, star_out),
        (fine_send, fine_here),
        (coarse_send, coarse_here),
        (labels, labels_out),
    ]
    first = len(moves)
    moves += list(zip(later, later_out))
    copies = [
        pltpu.make_async_copy(source, target, ready.at[number])
        for number, (source, target) in enumerate(moves)
    ]
    for copy in copies:
        copy.start()
    for copy in copies[1:3]:
        copy.wait()
    chain_weights(time_here, back_here, weights_out, raw)
    copies[0].wait()
    state = jnp.concatenate([dofs_here[q] for q in range(NQ)], axis=1)
    state_out[...] = state
    copies[3].wait()
    chain = chain_of(state, star_out, weights_out)
    integral = integral_of(chain, taylor_weights(0.0, 1.0 / SUBSTEPS))
    low_out[...] = integral[0:VPAD]
    for copy in copies[4:first]:
        copy.wait()
    wide[...] = jnp.zeros(wide.shape, F32)
    wide[0:PEERS, 0:SLOTS] = fine_here[...].astype(F32)
    wide[8 : 8 + PEERS, 0:SLOTS] = coarse_here[...].astype(F32)
    lists_out[...] = list_column(wide[0:PEERS], wide[8 : 8 + PEERS])
    project_and_send(
        integral, weights_out, lists_out, position, faces_out, pair_out, up_out, down_out
    )
    tail_out[...] = jnp.concatenate(chain[1:], axis=0)
    for copy in copies[first:]:
        copy.wait()


def prepare_kernel(
    state, tail, source, orientation, flux_other, face_front, face_turn, stiff_vol,
    coarse_out, slot_flux_out, slot_code_out, slot_hot_out, lift_out, slot_lift_out,
    table, fronts, tall, slot_tall,
):
    chain = [state[...]]
    start = 0
    for _, _, padded, _ in LEVELS:
        chain.append(tail[start : start + padded, :])
        start += padded
    for step in range(1, SUBSTEPS):
        coarse_out[step - 1] = integral_of(
            chain, taylor_weights(step / SUBSTEPS, (step + 1) / SUBSTEPS)
        )
    row = iota((LANES, LANES), 0)
    peer = (row >= BOTH).astype(jnp.int32) + (row >= 2 * BOTH).astype(jnp.int32)
    peer = peer + (row >= 3 * BOTH).astype(jnp.int32)
    inner = row - BOTH * peer
    kind = (inner >= SLOTS).astype(jnp.int32)
    wanted = kind * (PEERS * SLOTS - SLOTS) + peer * SLOTS + inner + FACES
    wanted = jnp.where(row < PEERS * BOTH, wanted, -1)
    blocks = [jnp.where(source[i : i + 1, :] == wanted, 1.0, 0.0) for i in range(4)]
    slot_hot_out[...] = blocks[0] + blocks[1] + blocks[2] + blocks[3]
    hot = jnp.concatenate(blocks, axis=1).astype(BF16)
    codes = jnp.concatenate(
        [
            jnp.where(iota((16, LANES), 0) - 3 * i == orientation[i : i + 1, :], 1.0, 0.0)
            for i in range(4)
        ],
        axis=1,
    ).astype(BF16)
    dims = (((1,), (1,)), ((), ()))
    slot_code_out[...] = lax.dot_general(codes, hot, dims, preferred_element_type=F32)
    table[...] = jnp.zeros(table.shape, F32)
    for i in range(4):
        for q in range(NQ):
            table[16 * q : 16 * q + NQ, lanes(i)] = flux_other[q, :, i, :]
    slot_flux_out[...] = pick_across(table[...], hot)

    fronts[...] = jnp.zeros(fronts.shape, F32)
    tall[...] = jnp.zeros(tall.shape, F32)
    slot_tall[...] = jnp.zeros(slot_tall.shape, F32)
    for i in range(4):
        fronts[0:NF, i * LANES : i * LANES + NB] = face_front[:, i, :]
    for code in range(3):
        turned = lax.dot_general(
            face_turn[code], fronts[0:NF, :], (((0,), (0,)), ((), ())),
            precision=HIGHEST, preferred_element_type=F32,
        )
        for i in range(4):
            start = FPAD * (3 * i + code)
            tall[start : start + NF, :] = -turned[:, lanes(i)]
            start = SLOT_PAD * (3 * i + code)
            slot_tall[start : start + NF, :] = -turned[:, lanes(i)]
    for i in range(4):
        start = REM + FPAD * i
        tall[start : start + NF, :] = -fronts[0:NF, lanes(i)]
    for d in range(3):
        start = REM + OWN + VPAD * d
        tall[start : start + NLOW, 0:NB] = stiff_vol[d]
    lift_out[...] = jnp.transpose(tall[...])[0:NB]
    whole = jnp.transpose(slot_tall[...])[0:PART]
    top = whole.astype(BF16)
    slot_lift_out[0:PART, 0:SLOT_REM] = top
    slot_lift_out[0:PART, SLOT_REM:] = top
    slot_lift_out[PART:, 0:SLOT_REM] = (whole - top.astype(F32)).astype(BF16)
    slot_lift_out[PART:, SLOT_REM:] = jnp.zeros((PART, SLOT_REM), BF16)


def local_kernel(
    state, low, faces, star, flux_self, flux_other, source, orientation, lift, out, stack,
):
    column = iota((FACES, LANES), 0)
    hot = jnp.concatenate(
        [
            jnp.where(column == source[i : i + 1, :], 1.0, 0.0).astype(BF16)
            for i in range(4)
        ],
        axis=1,
    )
    found = pick(face_table(faces[...]), hot)
    for d in range(3):
        totals = products(
            [lambda q: low[:, lanes(q)]], lambda _, q, p: star[q, p, d : d + 1, :], VPAD
        )
        base = REM + OWN + VPAD * d
        for p in range(NQ):
            stack[base : base + VPAD, lanes(p)] = totals[p]
    for i in range(4):
        totals = products(
            [lambda q: faces[i * FPAD : (i + 1) * FPAD, lanes(q)]],
            lambda _, q, p: flux_self[q, p, i : i + 1, :],
            FPAD,
        )
        for p in range(NQ):
            stack[REM + FPAD * i : REM + FPAD * (i + 1), lanes(p)] = totals[p]
    for i in range(4):
        totals = products(
            [lambda q: found[q * FPAD : (q + 1) * FPAD, lanes(i)]],
            lambda _, q, p: flux_other[q, p, i : i + 1, :],
            FPAD,
        )
        for code in range(3):
            mask = jnp.where(orientation[i : i + 1, :] == code, 1.0, 0.0)
            base = FPAD * (3 * i + code)
            for p in range(NQ):
                stack[base : base + FPAD, lanes(p)] = totals[p] * mask
    out[...] = state[...] + jnp.dot(
        lift[:, 0:DEEP], stack[...], precision=HIGH, preferred_element_type=F32
    )


def remote_part(position, near, upper, lower, slot_flux, slot_code, slot_hot, lift, stack):
    odd = lax.rem(position, 2) == 1
    behind_up = lax.rem(position, 4) < 2
    up, down = upper[...], lower[...]
    behind = jnp.where(behind_up, up, down)
    ahead = jnp.where(behind_up, down, up)
    here = jnp.where(odd, near[0:BOTH, :], near[2 * BOTH : 3 * BOTH, :])
    relayed = slice(BOTH, 2 * BOTH)
    rows = jnp.concatenate(
        [
            jnp.where(odd, here, behind[relayed]),
            jnp.where(odd, ahead[relayed], here),
            behind[0:BOTH],
            ahead[0:BOTH],
            jnp.zeros((LANES - PEERS * BOTH, WIDTH), F32),
        ],
        axis=0,
    )
    received = jnp.transpose(rows)
    totals = products(
        [lambda q: received[q * FPAD : (q + 1) * FPAD]],
        lambda _, q, p: slot_flux[16 * q + p : 16 * q + p + 1, :],
        FPAD,
    )
    codes = [
        jnp.broadcast_to(slot_code[code : code + 1, :], (SLOT_PAD, LANES)).astype(BF16)
        for code in range(12)
    ]
    gap = jnp.zeros((SLOT_PAD - FPAD, LANES), F32)
    for p in range(NQ):
        for half, part in enumerate(halves(jnp.concatenate([totals[p], gap], axis=0))):
            for code in range(12):
                start = SLOT_REM * half + SLOT_PAD * code
                stack[start : start + SLOT_PAD, lanes(p)] = part * codes[code]
    lifted = jnp.dot(lift[...], stack[...], preferred_element_type=F32)
    lifted = lifted[0:NB] + lifted[PART : PART + NB]
    by_slot = jnp.concatenate([lifted[:, lanes(p)] for p in range(NQ)], axis=0)
    by_element = pick(by_slot, slot_hot[...].astype(BF16))
    return jnp.concatenate([by_element[p * NB : (p + 1) * NB] for p in range(NQ)], axis=1)


def next_kernel(
    place, state, near, upper, lower, slot_flux, slot_code, slot_hot, lift,
    star, coarse, labels, weights, lists,
    state_out, low_out, faces_out, pair_out, up_out, down_out, stack, *, step,
):
    position = place[0]
    now = state[...] + remote_part(
        position, near, upper, lower, slot_flux, slot_code, slot_hot, lift, stack
    )
    state_out[...] = now
    chain = chain_of(now, star, weights)
    fine = integral_of(chain, taylor_weights(0.0, 1.0 / SUBSTEPS))
    mask = labels[...] == 1
    integral = jnp.concatenate(
        [jnp.where(mask, fine[:, lanes(q)], coarse[step - 1, :, lanes(q)]) for q in range(NQ)],
        axis=1,
    )
    low_out[...] = integral[0:VPAD]
    project_and_send(
        integral, weights, lists, position, faces_out, pair_out, up_out, down_out
    )


def last_kernel(
    place, state, near, upper, lower, slot_flux, slot_code, slot_hot, lift, out, stack
):
    total = state[...] + remote_part(
        place[0], near, upper, lower, slot_flux, slot_code, slot_hot, lift, stack
    )
    for q in range(NQ):
        out[q] = total[:, lanes(q)]


def floats(*shape):
    return jax.ShapeDtypeStruct(shape, F32)


def call(kernel, args, outs, scratch, scalars=0, inside=False, flops=2.0e7):
    smem = pl.BlockSpec(memory_space=pltpu.SMEM)
    vmem = pl.BlockSpec(memory_space=pltpu.VMEM)
    given = pl.BlockSpec(memory_space=pl.ANY) if inside else vmem
    if inside:
        args = args[:scalars] + tuple(
            pltpu.with_memory_space_constraint(item, pltpu.HBM) for item in args[scalars:]
        )
    moved = 4 * sum(math.prod(item.shape) for item in list(args) + list(outs))
    return pl.pallas_call(
        kernel,
        in_specs=[smem] * scalars + [given] * (len(args) - scalars),
        out_specs=[vmem] * len(outs),
        out_shape=outs,
        scratch_shapes=[
            pltpu.VMEM(item, F32) if isinstance(item, tuple) else item for item in scratch
        ],
        compiler_params=pltpu.CompilerParams(vmem_limit_bytes=40 * 2**20),
        cost_estimate=pl.CostEstimate(flops=int(flops), bytes_accessed=moved, transcendentals=0),
    )(*args)


def swaps(count, first):
    pairs = []
    for low in range(count - 2):
        if low % 4 in (first, first + 1):
            pairs += [(low, low + 2), (low + 2, low)]
    return pairs


def local(
    dofs, star, flux_self, flux_other, labels, neighbour_source, orientation,
    fine_send, coarse_send, stiff_time, stiff_vol, face_back, face_front, face_turn,
):
    count = lax.axis_size("dom")
    pairs = [[low, low + 1] for low in range(0, count, 2)]
    place = lax.axis_index("dom").astype(jnp.int32)
    partner_relay = jnp.where(place % 2 == 1, BOTH, 3 * BOTH)
    place = place.reshape(1)
    labels = labels.reshape(1, LANES)
    later = (
        flux_self.transpose(1, 2, 0, 3),
        flux_other.transpose(1, 2, 0, 3),
        neighbour_source,
        orientation,
        face_front.transpose(2, 0, 1),
        face_turn,
        stiff_vol.transpose(0, 2, 1),
    )
    star = star.transpose(1, 2, 0, 3)
    back = face_back.transpose(1, 0, 2)
    message = floats(BOTH, WIDTH)
    stack = pltpu.VMEM((2 * SLOT_REM, COLS), BF16)
    sent_shapes = [floats(OWN, COLS), floats(2 * BOTH, WIDTH), message, message]
    like = lambda item: jax.ShapeDtypeStruct(item.shape, item.dtype)
    found = call(
        first_kernel,
        (place, dofs.transpose(1, 0, 2), star, stiff_time, back, fine_send, coarse_send, labels)
        + later,
        [floats(NB, COLS), floats(VPAD, COLS), floats(TAIL, COLS)]
        + sent_shapes
        + [jax.ShapeDtypeStruct((CHAIN_ROWS, 2 * LANES), BF16), like(star), like(labels)]
        + [jax.ShapeDtypeStruct((PEERS * BOTH, LANES), jnp.int32)]
        + [like(item) for item in later],
        [(CHAIN_ROWS, LANES), (NQ, NB, LANES), stiff_time.shape, back.shape, (16, LANES)]
        + [pltpu.VMEM(item.shape, jnp.int32) for item in (fine_send, coarse_send)]
        + [pltpu.SemaphoreType.DMA((7 + len(later),))],
        scalars=1,
        inside=True,
    )
    state, low, tail, faces, pair, up, down, weights, star, labels, lists = found[:11]
    flux_self, flux_other, source, orientation, front, turn, vol = found[11:]
    coarse, slot_flux, slot_code, slot_hot, lift, slot_lift = call(
        prepare_kernel,
        (state, tail, source, orientation, flux_other, front, turn, vol),
        [floats(SUBSTEPS - 1, NB, COLS), floats(16 * NQ, LANES), floats(16, LANES), floats(LANES, LANES), floats(NB, DEEP_PAD),
         jax.ShapeDtypeStruct((2 * PART, 2 * SLOT_REM), BF16)],
        [(16 * NQ, FACES), (FPAD, FACES), (DEEP_PAD, LANES), (SLOT_REM, LANES)],
    )
    for step in range(SUBSTEPS):
        near = lax.all_gather(pair, "dom", axis_index_groups=pairs, tiled=True)
        relayed = lax.dynamic_slice(near, (partner_relay, 0), (BOTH, WIDTH))
        lower = jnp.concatenate([down, relayed], axis=0)
        lower, up, relayed = lax.optimization_barrier((lower, up, relayed))
        upper = jnp.concatenate([up, relayed], axis=0)
        upper = lax.ppermute(upper, "dom", swaps(count, 2))
        lower = lax.ppermute(lower, "dom", swaps(count, 0))
        (state,) = call(
            local_kernel,
            (state, low, faces, star, flux_self, flux_other, source, orientation, lift),
            [floats(NB, COLS)],
            [(DEEP, COLS)],
        )
        received = (place, state, near, upper, lower, slot_flux, slot_code, slot_hot, slot_lift)
        if step + 1 < SUBSTEPS:
            state, low, faces, pair, up, down = call(
                functools.partial(next_kernel, step=step + 1),
                received + (star, coarse, labels, weights, lists),
                [floats(NB, COLS), floats(VPAD, COLS)] + sent_shapes,
                [stack],
                scalars=1,
            )
    (result,) = call(
        last_kernel, received, [floats(NQ, NB, LANES)], [stack], scalars=1
    )
    return result.transpose(1, 0, 2)


def solution(mesh):
    split = P(None, None, "dom")
    face = P(None, None, None, "dom")
    row = P(None, "dom")
    in_specs = (split, face, face, face, P("dom"), row, row, row, row, P(), P(), P(), P(), P())
    return jax.shard_map(local, mesh=mesh, in_specs=in_specs, out_specs=split, check_vma=False)
```

```python
import functools
import math

import jax
import jax.numpy as jnp
from jax import lax
from jax.experimental import pallas as pl
from jax.experimental.pallas import tpu as pltpu
from jax.sharding import PartitionSpec as P

ORDER = 6
SUBSTEPS = 4
NQ = 9
NB = 56
NLOW = 35
NF = 21
PEERS = 4
SLOTS = 12
LANES = 128
FPAD = 24
VPAD = 40
BOTH = 2 * SLOTS
WIDTH = 256
COLS = NQ * LANES
FACES = 4 * LANES
REM = 12 * FPAD
SLOT_PAD = 32
SLOT_REM = 12 * SLOT_PAD
OWN = 4 * FPAD
DEEP = REM + OWN + 3 * VPAD
DEEP_PAD = 512
LEVELS = [(0, 35, 40, 128), (128, 20, 24, 80), (208, 10, 16, 48), (256, 4, 8, 32), (288, 1, 8, 32)]
BACK = 320
CHAIN_ROWS = BACK + OWN
TAIL = 96
PART = 64
TWOS = 5
NARROW = TWOS * LANES
STAR_ROWS = 40
HIGH = lax.Precision.HIGH
HIGHEST = lax.Precision.HIGHEST
F32 = jnp.float32
BF16 = jnp.bfloat16


def taylor_weights(start, stop):
    return [
        (stop ** (depth + 1) - start ** (depth + 1)) / math.factorial(depth + 1)
        for depth in range(ORDER)
    ]


def lanes(index):
    return slice(index * LANES, (index + 1) * LANES)


def iota(shape, dim):
    return lax.broadcasted_iota(jnp.int32, shape, dim)


def halves(value):
    top = value.astype(BF16)
    return top, (value - top.astype(F32)).astype(BF16)


def pick(value, hot):
    return jnp.dot(
        jnp.concatenate(halves(value), axis=1),
        jnp.concatenate([hot, hot], axis=0),
        preferred_element_type=F32,
    )


def pick_rows(hot, value):
    return lax.dot_general(
        jnp.concatenate([hot, hot], axis=1),
        jnp.concatenate(halves(value), axis=1),
        (((1,), (1,)), ((), ())),
        preferred_element_type=F32,
    )


def pick_across(value, hot):
    return lax.dot_general(
        jnp.concatenate(halves(value), axis=1),
        jnp.concatenate([hot, hot], axis=1),
        (((1,), (1,)), ((), ())),
        preferred_element_type=F32,
    )


def gather_exact(value, hot):
    top, rest = halves(value)
    middle, low = halves(value - top.astype(F32))
    return lax.dot_general(
        jnp.concatenate([top, middle, low], axis=1),
        jnp.concatenate([hot, hot, hot], axis=1),
        (((1,), (1,)), ((), ())),
        preferred_element_type=F32,
    )


def first_half(rows):
    return iota((rows, LANES), 1) < PART


def paired(blocks):
    rows = blocks[0].shape[0]
    blocks = list(blocks) + [jnp.zeros_like(blocks[0])]
    return jnp.concatenate(
        [jnp.where(first_half(rows), blocks[2 * t], blocks[2 * t + 1]) for t in range(TWOS)],
        axis=1,
    )


def place_of(q):
    return LANES * (q % 2) + FPAD * (q // 2)


def stacked(value):
    top = value.astype(BF16).astype(F32)
    rest = value - top
    fill = PART - value.shape[0]
    gap = [jnp.zeros((fill, value.shape[1]), F32)] if fill else []
    return jnp.concatenate([top] + gap + [rest] + gap + [top] + gap, axis=0).astype(BF16)


def products(blocks, row_of, count=NQ):
    totals = [None] * NQ
    for q in range(count):
        for position, block in enumerate(blocks):
            left = block(q)
            for p in range(NQ):
                term = left * row_of(position, q, p)
                totals[p] = term if totals[p] is None else totals[p] + term
    return totals


def chain_weights(stiff_time, face_back, out, tips, raw):
    raw[...] = jnp.zeros(raw.shape, F32)
    for start, valid, padded, _ in LEVELS:
        for d in range(3):
            raw[start + d * padded : start + d * padded + valid, 0:NB] = stiff_time[d, 0:valid, :]
    for j in range(4):
        raw[BACK + j * FPAD : BACK + j * FPAD + NF, 0:NB] = face_back[:, j, :]
    once = raw[...]
    top = once.astype(BF16).astype(F32)
    out[:, 0:LANES] = (top + pltpu.roll(top, PART, 1)).astype(BF16)
    out[:, LANES : 2 * LANES] = (once - top).astype(BF16)
    start = LEVELS[-1][0]
    turned = jnp.transpose(once[start : start + LANES])
    for d in range(3):
        column = turned[0:8, 8 * d : 8 * d + 1]
        tips[8 * d : 8 * d + 8, :] = jnp.broadcast_to(column, (8, LANES))
    tips[24 : 24 + OWN, :] = jnp.broadcast_to(once[BACK : BACK + OWN, 0:1], (OWN, LANES))


def weigh(weights, start, rows, value):
    return jnp.dot(
        weights[start : start + rows, 0 : 3 * PART], stacked(value), preferred_element_type=F32
    )


def wide_sums(block, star):
    blocks = [functools.partial(block, d) for d in range(3)]
    return products(blocks, lambda d, q, p: star[q, p, d : d + 1, :])


def narrow_sums(block, star):
    return products(
        [functools.partial(block, d) for d in range(3)],
        lambda d, t, p: star[STAR_ROWS * t + 4 * p + d : STAR_ROWS * t + 4 * p + d + 1, :],
        TWOS,
    )


def narrow_join(totals):
    half = first_half(totals[0].shape[0])
    totals = list(totals) + [jnp.zeros_like(totals[0])]
    pieces = []
    for t in range(TWOS):
        even, odd = totals[2 * t], totals[2 * t + 1]
        crossed = pltpu.roll(jnp.where(half, odd, even), PART, 1)
        pieces.append(jnp.where(half, even, odd) + crossed)
    return jnp.concatenate(pieces, axis=1)


def wide_join(totals):
    return jnp.concatenate(totals, axis=1)


def chain_of(first, star, weights, tips, sums, join):
    now = first
    chain = [first]
    for start, _, padded, rows in LEVELS[:-1]:
        found = weigh(weights, start, rows, now)
        now = join(
            sums(lambda d, c: found[d * padded : (d + 1) * padded, lanes(c)], star)
        )
        chain.append(now)
    totals = sums(lambda d, c: now[:, lanes(c)] * tips[8 * d : 8 * d + 8, :], star)
    return chain, join([jnp.sum(total, axis=0, keepdims=True) for total in totals])


def with_end(integral, faces, end, tips):
    row = jnp.where(iota((8, end.shape[1]), 0) == 0, end, 0.0)
    low = jnp.concatenate([integral[0:8] + row, integral[8:VPAD]], axis=0)
    column = tips[24 : 24 + OWN, :]
    count = end.shape[1] // LANES
    faces = [faces[:, lanes(c)] + column * end[:, lanes(c)] for c in range(count)]
    return low, jnp.concatenate(faces, axis=1)


def integral_of(chain, weights):
    pieces = []
    edges = [0, 8, 16, 24, 40, 56]
    for low, high in zip(edges[:-1], edges[1:]):
        total = None
        for depth in range(len(chain)):
            if chain[depth].shape[0] < high:
                continue
            term = (weights[depth] * (-1) ** depth) * chain[depth][low:high]
            total = term if total is None else total + term
        pieces.append(total)
    return jnp.concatenate(pieces, axis=0)


def face_table(faces):
    def block(q):
        return jnp.concatenate(
            [faces[j * FPAD : (j + 1) * FPAD, lanes(q)] for j in range(4)], axis=1
        )

    even = [block(q) for q in range(0, NQ, 2)]
    odd = [block(q) for q in range(1, NQ, 2)]
    return jnp.concatenate(
        even
        + [jnp.zeros((LANES - len(even) * FPAD, FACES), F32)]
        + odd
        + [jnp.zeros((LANES - len(odd) * FPAD, FACES), F32)],
        axis=0,
    )


def narrow_table(faces):
    rows = [
        jnp.concatenate([faces[j * FPAD : (j + 1) * FPAD, lanes(t)] for j in range(4)], axis=1)
        for t in range(TWOS)
    ]
    return jnp.concatenate(rows + [jnp.zeros((LANES - TWOS * FPAD, FACES), F32)], axis=0)


def list_rows():
    row = iota((PEERS * BOTH, LANES), 0)
    peer = (row >= BOTH).astype(jnp.int32) + (row >= 2 * BOTH).astype(jnp.int32)
    peer = peer + (row >= 3 * BOTH).astype(jnp.int32)
    return peer, row - BOTH * peer


def list_hot(lists, face):
    return lists[...] == iota((PEERS * BOTH, LANES), 1) + LANES * face


def deliver(sent, position, pair_out, up_out, down_out):
    odd = lax.rem(position, 2) == 1
    first, second = sent[0:BOTH], sent[BOTH : 2 * BOTH]
    pair_out[0:BOTH, :] = jnp.where(odd, second, first)
    pair_out[BOTH : 2 * BOTH, :] = jnp.where(odd, first, second)
    behind_up = lax.rem(position, 4) < 2
    ahead, behind = sent[2 * BOTH : 3 * BOTH], sent[3 * BOTH : 4 * BOTH]
    up_out[...] = jnp.where(behind_up, behind, ahead)
    down_out[...] = jnp.where(behind_up, ahead, behind)


def list_column(fine, coarse):
    peer, inner = list_rows()
    total = jnp.zeros((PEERS * BOTH, LANES), F32)
    for kind, entries in enumerate((fine, coarse)):
        here = iota((PEERS * BOTH, LANES), 1) == inner - kind * SLOTS
        for k in range(PEERS):
            total = total + jnp.where(here & (peer == k), entries[k : k + 1, :], 0.0)
    column = jnp.sum(total, axis=1, keepdims=True)
    return jnp.broadcast_to(column, (PEERS * BOTH, LANES)).astype(jnp.int32)


def first_kernel(
    place, dofs, star, stiff_time, face_back, fine_send, coarse_send, labels, *rest
):
    later = rest[:7]
    (
        state_out, low_out, tail_out, faces_out, pair_out, up_out, down_out,
        weights_out, tips_out, star_out, labels_out, lists_out,
    ) = rest[7:19]
    later_out = rest[19:26]
    raw, dofs_here, time_here, back_here, wide, fine_here, coarse_here, ready = rest[26:]
    position = place[0]
    moves = [
        (dofs, dofs_here),
        (stiff_time, time_here),
        (face_back, back_here),
        (star, star_out),
        (fine_send, fine_here),
        (coarse_send, coarse_here),
        (labels, labels_out),
    ]
    first = len(moves)
    moves += list(zip(later, later_out))
    copies = [
        pltpu.make_async_copy(source, target, ready.at[number])
        for number, (source, target) in enumerate(moves)
    ]
    for copy in copies:
        copy.start()
    for copy in copies[1:3]:
        copy.wait()
    chain_weights(time_here, back_here, weights_out, tips_out, raw)
    copies[0].wait()
    state = jnp.concatenate([dofs_here[q] for q in range(NQ)], axis=1)
    state_out[...] = state
    copies[3].wait()
    chain, end = chain_of(state, star_out, weights_out, tips_out, wide_sums, wide_join)
    first_weights = taylor_weights(0.0, 1.0 / SUBSTEPS)
    integral = integral_of(chain, first_weights)
    for copy in copies[4:first]:
        copy.wait()
    wide[...] = jnp.zeros(wide.shape, F32)
    wide[0:PEERS, 0:SLOTS] = fine_here[...].astype(F32)
    wide[8 : 8 + PEERS, 0:SLOTS] = coarse_here[...].astype(F32)
    lists_out[...] = list_column(wide[0:PEERS], wide[8 : 8 + PEERS])
    faces = weigh(weights_out, BACK, OWN, integral)
    low, faces = with_end(integral, faces, -first_weights[-1] * end, tips_out)
    low_out[...] = low
    faces_out[...] = faces
    hot = jnp.concatenate(
        [jnp.where(list_hot(lists_out, j), 1.0, 0.0) for j in range(4)], axis=1
    ).astype(BF16)
    deliver(pick_rows(hot, face_table(faces)), position, pair_out, up_out, down_out)
    end = jnp.where(iota((8, COLS), 0) == 0, end, 0.0)
    tail_out[...] = jnp.concatenate(chain[1:] + [end], axis=0)
    for copy in copies[first:]:
        copy.wait()


def prepare_kernel(
    state, tail, source, orientation, flux_other, face_front, face_turn, stiff_vol,
    star, labels, lists,
    coarse_out, slot_flux_out, slot_code_out, slot_hot_out, lift_out, slot_lift_out,
    narrow_hot_out, slot_narrow_out, star_out, send_out,
    table, fronts, tall, slot_tall, flat,
):
    fine = labels[...] == 1
    before = (iota((LANES, LANES), 0) < iota((LANES, LANES), 1)).astype(F32).astype(BF16)
    marks = jnp.broadcast_to(jnp.where(fine, 1.0, 0.0), (16, LANES)).astype(BF16)
    rank = jnp.dot(marks, before, preferred_element_type=F32)[0:1].astype(jnp.int32)
    rank = jnp.where(fine, rank, -1)
    lane = iota((LANES, LANES), 0)
    lane = jnp.where(lane >= PART, lane - PART, lane)
    narrow_hot = jnp.where(rank == lane, 1.0, 0.0).astype(BF16)
    narrow_hot_out[...] = narrow_hot
    flat[...] = jnp.zeros(flat.shape, F32)
    for q in range(NQ):
        for p in range(NQ):
            start = STAR_ROWS * q + 4 * p
            flat[start : start + 3, :] = star[q, p]
    gathered = gather_exact(flat[...], narrow_hot)
    stars = [gathered[STAR_ROWS * q : STAR_ROWS * (q + 1)] for q in range(NQ)]
    packed = paired(stars)
    for t in range(TWOS):
        star_out[STAR_ROWS * t : STAR_ROWS * (t + 1), :] = packed[:, lanes(t)]
    _, inner = list_rows()
    half = first_half(PEERS * BOTH)
    across = (((1,), (1,)), ((), ()))
    for j in range(4):
        chosen = jnp.where(list_hot(lists, j) & (inner < SLOTS), 1.0, 0.0).astype(BF16)
        found = lax.dot_general(chosen, narrow_hot, across, preferred_element_type=F32)
        send_out[0 : PEERS * BOTH, lanes(j)] = jnp.where(half, found, 0.0).astype(BF16)
        send_out[PEERS * BOTH :, lanes(j)] = jnp.where(half, 0.0, found).astype(BF16)
    chain = [state[...]]
    start = 0
    for _, _, padded, _ in LEVELS:
        chain.append(tail[start : start + padded, :])
        start += padded
    for step in range(1, SUBSTEPS):
        coarse_out[step - 1] = integral_of(
            chain, taylor_weights(step / SUBSTEPS, (step + 1) / SUBSTEPS)
        )
    row = iota((LANES, LANES), 0)
    peer = (row >= BOTH).astype(jnp.int32) + (row >= 2 * BOTH).astype(jnp.int32)
    peer = peer + (row >= 3 * BOTH).astype(jnp.int32)
    inner = row - BOTH * peer
    kind = (inner >= SLOTS).astype(jnp.int32)
    wanted = kind * (PEERS * SLOTS - SLOTS) + peer * SLOTS + inner + FACES
    wanted = jnp.where(row < PEERS * BOTH, wanted, -1)
    blocks = [jnp.where(source[i : i + 1, :] == wanted, 1.0, 0.0) for i in range(4)]
    slot_hot = (blocks[0] + blocks[1] + blocks[2] + blocks[3]).astype(BF16)
    slot_hot_out[...] = slot_hot
    slot_narrow_out[...] = lax.dot_general(
        slot_hot, narrow_hot, across, preferred_element_type=F32
    ).astype(BF16)
    hot = jnp.concatenate(blocks, axis=1).astype(BF16)
    codes = jnp.concatenate(
        [
            jnp.where(iota((16, LANES), 0) - 3 * i == orientation[i : i + 1, :], 1.0, 0.0)
            for i in range(4)
        ],
        axis=1,
    ).astype(BF16)
    dims = (((1,), (1,)), ((), ()))
    found = lax.dot_general(codes, hot, dims, preferred_element_type=F32)
    for code in range(12):
        slot_code_out[SLOT_PAD * code : SLOT_PAD * (code + 1), :] = jnp.broadcast_to(
            found[code : code + 1], (SLOT_PAD, LANES)
        ).astype(BF16)
    table[...] = jnp.zeros(table.shape, F32)
    for i in range(4):
        for q in range(NQ):
            table[16 * q : 16 * q + NQ, lanes(i)] = flux_other[q, :, i, :]
    slot_flux_out[...] = pick_across(table[...], hot)

    fronts[...] = jnp.zeros(fronts.shape, F32)
    tall[...] = jnp.zeros(tall.shape, F32)
    slot_tall[...] = jnp.zeros(slot_tall.shape, F32)
    for i in range(4):
        fronts[0:NF, i * LANES : i * LANES + NB] = face_front[:, i, :]
    for code in range(3):
        turned = lax.dot_general(
            face_turn[code], fronts[0:NF, :], (((0,), (0,)), ((), ())),
            precision=HIGHEST, preferred_element_type=F32,
        )
        for i in range(4):
            start = FPAD * (3 * i + code)
            tall[start : start + NF, :] = -turned[:, lanes(i)]
            start = SLOT_PAD * (3 * i + code)
            slot_tall[start : start + NF, :] = -turned[:, lanes(i)]
    for i in range(4):
        start = REM + FPAD * i
        tall[start : start + NF, :] = -fronts[0:NF, lanes(i)]
    for d in range(3):
        start = REM + OWN + VPAD * d
        tall[start : start + NLOW, 0:NB] = stiff_vol[d]
    lift_out[...] = jnp.transpose(tall[...])[0:NB]
    whole = jnp.transpose(slot_tall[...])[0:PART]
    top = whole.astype(BF16)
    slot_lift_out[0:PART, 0:SLOT_REM] = top
    slot_lift_out[0:PART, SLOT_REM:] = top
    slot_lift_out[PART:, 0:SLOT_REM] = (whole - top.astype(F32)).astype(BF16)
    slot_lift_out[PART:, SLOT_REM:] = jnp.zeros((PART, SLOT_REM), BF16)


def local_kernel(*refs, step):
    if step == 0:
        state, low, faces, *rest = refs
        state, low, faces = state[...], low[...], faces[...]
    else:
        state, by_slot, slot_hot, low, faces, coarse_faces, *rest = refs
    star, flux_self, flux_other, source, orientation, lift, *rest = rest
    coarse, weights, lists, narrow_hot, labels, *rest = rest
    out, *rest = rest
    if step > 0:
        state = state[...] + by_elements(by_slot[...], slot_hot[...])
        back = jnp.transpose(narrow_hot[...].astype(F32))
        half = iota((LANES, LANES), 1) < PART
        spread = jnp.concatenate(
            [
                jnp.transpose(jnp.where(half, back, 0.0)),
                jnp.transpose(jnp.where(half, 0.0, back)),
            ],
            axis=1,
        ).astype(BF16)
        both = VPAD + OWN
        rows = [
            part[:, lanes(t)] for t in range(TWOS) for part in (low, faces)
        ]
        wide = pick(jnp.concatenate(rows, axis=0), spread)
        wide = [wide[both * t : both * (t + 1)] for t in range(TWOS)]
        wide = jnp.concatenate(wide, axis=1)[:, 0:COLS]
        fine = labels[...] == 1
        fine = jnp.concatenate([fine] * NQ, axis=1)
        low = jnp.where(fine, wide[0:VPAD], coarse[step - 1, 0:VPAD, :])
        faces = jnp.where(fine, wide[VPAD:both], coarse_faces[...])
    if step + 1 < SUBSTEPS:
        narrow_out, next_faces_out, next_sent_out, stack = rest
        next_faces = weigh(weights, BACK, OWN, coarse[step])
        next_faces_out[...] = next_faces
        _, inner = list_rows()
        hot = jnp.concatenate(
            [jnp.where(list_hot(lists, j) & (inner >= SLOTS), 1.0, 0.0) for j in range(4)],
            axis=1,
        ).astype(BF16)
        next_sent_out[...] = pick_rows(hot, face_table(next_faces))
    else:
        (stack,) = rest
    column = iota((FACES, LANES), 0)
    hot = jnp.concatenate(
        [
            jnp.where(column == source[i : i + 1, :], 1.0, 0.0).astype(BF16)
            for i in range(4)
        ],
        axis=1,
    )
    found = pick(face_table(faces), hot)
    for d in range(3):
        totals = products(
            [lambda q: low[:, lanes(q)]], lambda _, q, p: star[q, p, d : d + 1, :]
        )
        base = REM + OWN + VPAD * d
        for p in range(NQ):
            stack[base : base + VPAD, lanes(p)] = totals[p]
    for i in range(4):
        totals = products(
            [lambda q: faces[i * FPAD : (i + 1) * FPAD, lanes(q)]],
            lambda _, q, p: flux_self[q, p, i : i + 1, :],
        )
        for p in range(NQ):
            stack[REM + FPAD * i : REM + FPAD * (i + 1), lanes(p)] = totals[p]
    for i in range(4):
        totals = products(
            [lambda q: found[place_of(q) : place_of(q) + FPAD, lanes(i)]],
            lambda _, q, p: flux_other[q, p, i : i + 1, :],
        )
        for code in range(3):
            mask = jnp.where(orientation[i : i + 1, :] == code, 1.0, 0.0)
            base = FPAD * (3 * i + code)
            for p in range(NQ):
                stack[base : base + FPAD, lanes(p)] = totals[p] * mask
    total = state + jnp.dot(
        lift[:, 0:DEEP], stack[...], precision=HIGH, preferred_element_type=F32
    )
    out[...] = total
    if step + 1 < SUBSTEPS:
        tall = jnp.concatenate([total[:, lanes(q)] for q in range(NQ)], axis=0)
        found = pick_across(tall, narrow_hot[...])
        narrow_out[...] = paired([found[NB * q : NB * (q + 1)] for q in range(NQ)])


def by_elements(by_slot, slot_hot):
    found = pick(by_slot, slot_hot)
    return jnp.concatenate([found[NB * p : NB * (p + 1)] for p in range(NQ)], axis=1)


def remote_part(position, near, upper, lower, slot_flux, slot_code, lift):
    odd = lax.rem(position, 2) == 1
    behind_up = lax.rem(position, 4) < 2
    up, down = upper[...], lower[...]
    behind = jnp.where(behind_up, up, down)
    ahead = jnp.where(behind_up, down, up)
    here = jnp.where(odd, near[0:BOTH, :], near[2 * BOTH : 3 * BOTH, :])
    relayed = slice(BOTH, 2 * BOTH)
    rows = jnp.concatenate(
        [
            jnp.where(odd, here, behind[relayed]),
            jnp.where(odd, ahead[relayed], here),
            behind[0:BOTH],
            ahead[0:BOTH],
            jnp.zeros((LANES - PEERS * BOTH, WIDTH), F32),
        ],
        axis=0,
    )
    received = jnp.transpose(rows)
    totals = products(
        [lambda q: received[place_of(q) : place_of(q) + FPAD]],
        lambda _, q, p: slot_flux[16 * q + p : 16 * q + p + 1, :],
    )
    codes = [slot_code[SLOT_PAD * code : SLOT_PAD * (code + 1), :] for code in range(12)]
    gap = jnp.zeros((SLOT_PAD - FPAD, LANES), F32)
    columns = []
    for p in range(NQ):
        both = halves(jnp.concatenate([totals[p], gap], axis=0))
        masked = [part * mask for part in both for mask in codes]
        columns.append(jnp.concatenate(masked, axis=0))
    masked = jnp.concatenate(columns, axis=1)
    lifted = jnp.dot(lift[...], masked, preferred_element_type=F32)
    lifted = lifted[0:NB] + lifted[PART : PART + NB]
    return jnp.concatenate([lifted[:, lanes(p)] for p in range(NQ)], axis=0)


def next_kernel(
    place, near, upper, lower, slot_flux, slot_code, lift,
    narrow, slot_narrow, star, weights, tips, send_hot, coarse_sent,
    by_slot_out, low_out, faces_out, pair_out, up_out, down_out,
):
    position = place[0]
    by_slot = remote_part(position, near, upper, lower, slot_flux, slot_code, lift)
    by_slot_out[...] = by_slot
    found = pick(by_slot, slot_narrow[...])
    now = narrow[...] + paired([found[NB * p : NB * (p + 1)] for p in range(NQ)])
    chain, end = chain_of(now, star, weights, tips, narrow_sums, narrow_join)
    first_weights = taylor_weights(0.0, 1.0 / SUBSTEPS)
    integral = integral_of(chain, first_weights)
    faces = weigh(weights, BACK, OWN, integral)
    low, faces = with_end(integral, faces, -first_weights[-1] * end, tips)
    low_out[...] = low
    faces_out[...] = faces
    found = pick_rows(send_hot[...], narrow_table(faces))
    rows = PEERS * BOTH
    sent = jnp.concatenate([found[0:rows], found[rows : 2 * rows]], axis=1) + coarse_sent[...]
    deliver(sent, position, pair_out, up_out, down_out)


def last_kernel(
    place, near, upper, lower, slot_flux, slot_code, lift, state, slot_hot, out
):
    by_slot = remote_part(place[0], near, upper, lower, slot_flux, slot_code, lift)
    total = state[...] + by_elements(by_slot, slot_hot[...])
    for q in range(NQ):
        out[q] = total[:, lanes(q)]


def floats(*shape):
    return jax.ShapeDtypeStruct(shape, F32)


def call(kernel, args, outs, scratch, scalars=0, inside=False, flops=2.0e7):
    smem = pl.BlockSpec(memory_space=pltpu.SMEM)
    vmem = pl.BlockSpec(memory_space=pltpu.VMEM)
    given = pl.BlockSpec(memory_space=pl.ANY) if inside else vmem
    if inside:
        args = args[:scalars] + tuple(
            pltpu.with_memory_space_constraint(item, pltpu.HBM) for item in args[scalars:]
        )
    moved = 4 * sum(math.prod(item.shape) for item in list(args) + list(outs))
    return pl.pallas_call(
        kernel,
        in_specs=[smem] * scalars + [given] * (len(args) - scalars),
        out_specs=[vmem] * len(outs),
        out_shape=outs,
        scratch_shapes=[
            pltpu.VMEM(item, F32) if isinstance(item, tuple) else item for item in scratch
        ],
        compiler_params=pltpu.CompilerParams(vmem_limit_bytes=40 * 2**20),
        cost_estimate=pl.CostEstimate(flops=int(flops), bytes_accessed=moved, transcendentals=0),
    )(*args)


def swaps(count, first):
    pairs = []
    for low in range(count - 2):
        if low % 4 in (first, first + 1):
            pairs += [(low, low + 2), (low + 2, low)]
    return pairs


def local(
    dofs, star, flux_self, flux_other, labels, neighbour_source, orientation,
    fine_send, coarse_send, stiff_time, stiff_vol, face_back, face_front, face_turn,
):
    count = lax.axis_size("dom")
    pairs = [[low, low + 1] for low in range(0, count, 2)]
    place = lax.axis_index("dom").astype(jnp.int32)
    partner_relay = jnp.where(place % 2 == 1, BOTH, 3 * BOTH)
    place = place.reshape(1)
    labels = labels.reshape(1, LANES)
    later = (
        flux_self.transpose(1, 2, 0, 3),
        flux_other.transpose(1, 2, 0, 3),
        neighbour_source,
        orientation,
        face_front.transpose(2, 0, 1),
        face_turn,
        stiff_vol.transpose(0, 2, 1),
    )
    star = star.transpose(1, 2, 0, 3)
    back = face_back.transpose(1, 0, 2)
    message = floats(BOTH, WIDTH)
    sent_shapes = [floats(OWN, COLS), floats(2 * BOTH, WIDTH), message, message]
    like = lambda item: jax.ShapeDtypeStruct(item.shape, item.dtype)
    found = call(
        first_kernel,
        (place, dofs.transpose(1, 0, 2), star, stiff_time, back, fine_send, coarse_send, labels)
        + later,
        [floats(NB, COLS), floats(VPAD, COLS), floats(TAIL, COLS)]
        + sent_shapes
        + [jax.ShapeDtypeStruct((CHAIN_ROWS, 2 * LANES), BF16)]
        + [floats(24 + OWN, LANES), like(star), like(labels)]
        + [jax.ShapeDtypeStruct((PEERS * BOTH, LANES), jnp.int32)]
        + [like(item) for item in later],
        [(CHAIN_ROWS, LANES), (NQ, NB, LANES), stiff_time.shape, back.shape, (16, LANES)]
        + [pltpu.VMEM(item.shape, jnp.int32) for item in (fine_send, coarse_send)]
        + [pltpu.SemaphoreType.DMA((7 + len(later),))],
        scalars=1,
        inside=True,
    )
    state, low, tail, faces, pair, up, down, weights, tips, star, labels, lists = found[:12]
    flux_self, flux_other, source, orientation, front, turn, vol = found[12:]
    halved = lambda *shape: jax.ShapeDtypeStruct(shape, BF16)
    prepared = call(
        prepare_kernel,
        (state, tail, source, orientation, flux_other, front, turn, vol, star, labels, lists),
        [
            floats(SUBSTEPS - 1, NB, COLS), floats(16 * NQ, LANES), halved(SLOT_REM, LANES),
            halved(LANES, LANES), floats(NB, DEEP_PAD), halved(2 * PART, 2 * SLOT_REM),
            halved(LANES, LANES), halved(LANES, LANES), floats(TWOS * STAR_ROWS, LANES),
            halved(2 * PEERS * BOTH, FACES),
        ],
        [
            (16 * NQ, FACES), (FPAD, FACES), (DEEP_PAD, LANES), (SLOT_REM, LANES),
            (NQ * STAR_ROWS, LANES),
        ],
    )
    coarse, slot_flux, slot_code, slot_hot, lift, slot_lift = prepared[:6]
    narrow_hot, slot_narrow, narrow_star, send_hot = prepared[6:]
    fixed = (star, flux_self, flux_other, source, orientation, lift)
    fixed += (coarse, weights, lists, narrow_hot, labels)
    known = (state, low, faces)
    for step in range(SUBSTEPS):
        near = lax.all_gather(pair, "dom", axis_index_groups=pairs, tiled=True)
        relayed = lax.dynamic_slice(near, (partner_relay, 0), (BOTH, WIDTH))
        lower = jnp.concatenate([down, relayed], axis=0)
        lower, up, relayed = lax.optimization_barrier((lower, up, relayed))
        upper = jnp.concatenate([up, relayed], axis=0)
        upper = lax.ppermute(upper, "dom", swaps(count, 2))
        lower = lax.ppermute(lower, "dom", swaps(count, 0))
        ahead = [floats(NB, NARROW), floats(OWN, COLS), floats(PEERS * BOTH, WIDTH)]
        state, *made = call(
            functools.partial(local_kernel, step=step),
            known + fixed,
            [floats(NB, COLS)] + (ahead if step + 1 < SUBSTEPS else []),
            [(DEEP, COLS)],
        )
        received = (place, near, upper, lower, slot_flux, slot_code, slot_lift)
        if step + 1 < SUBSTEPS:
            narrow, coarse_faces, coarse_sent = made
            by_slot, low, faces, pair, up, down = call(
                next_kernel,
                received
                + (narrow, slot_narrow, narrow_star, weights, tips, send_hot, coarse_sent),
                [floats(NQ * NB, LANES), floats(VPAD, NARROW), floats(OWN, NARROW)]
                + sent_shapes[1:],
                [],
                scalars=1,
            )
            known = (state, by_slot, slot_hot, low, faces, coarse_faces)
    (result,) = call(
        last_kernel, received + (state, slot_hot), [floats(NQ, NB, LANES)], [], scalars=1
    )
    return result.transpose(1, 0, 2)


def solution(mesh):
    split = P(None, None, "dom")
    face = P(None, None, None, "dom")
    row = P(None, "dom")
    in_specs = (split, face, face, face, P("dom"), row, row, row, row, P(), P(), P(), P(), P())
    return jax.shard_map(local, mesh=mesh, in_specs=in_specs, out_specs=split, check_vma=False)
```

```python
import functools
import math

import jax
import jax.numpy as jnp
from jax import lax
from jax.experimental import pallas as pl
from jax.experimental.pallas import tpu as pltpu
from jax.sharding import PartitionSpec as P

ORDER = 6
SUBSTEPS = 4
NQ = 9
NB = 56
NLOW = 35
NF = 21
PEERS = 4
SLOTS = 12
LANES = 128
FPAD = 24
VPAD = 40
BOTH = 2 * SLOTS
WIDTH = 256
COLS = NQ * LANES
FACES = 4 * LANES
REM = 12 * FPAD
SLOT_PAD = 32
SLOT_REM = 12 * SLOT_PAD
OWN = 4 * FPAD
DEEP = REM + OWN + 3 * VPAD
DEEP_PAD = 512
LEVELS = [(0, 35, 40, 128), (128, 20, 24, 80), (208, 10, 16, 48), (256, 4, 8, 32), (288, 1, 8, 32)]
BACK = 320
CHAIN_ROWS = BACK + OWN
TAIL = 96
PART = 64
TWOS = 5
NARROW = TWOS * LANES
STAR_ROWS = 40
HIGH = lax.Precision.HIGH
HIGHEST = lax.Precision.HIGHEST
F32 = jnp.float32
BF16 = jnp.bfloat16


def taylor_weights(start, stop):
    return [
        (stop ** (depth + 1) - start ** (depth + 1)) / math.factorial(depth + 1)
        for depth in range(ORDER)
    ]


def lanes(index):
    return slice(index * LANES, (index + 1) * LANES)


def iota(shape, dim):
    return lax.broadcasted_iota(jnp.int32, shape, dim)


def halves(value):
    top = value.astype(BF16)
    return top, (value - top.astype(F32)).astype(BF16)


def pick(value, hot):
    return jnp.dot(
        jnp.concatenate(halves(value), axis=1),
        jnp.concatenate([hot, hot], axis=0),
        preferred_element_type=F32,
    )


def pick_rows(hot, value):
    return lax.dot_general(
        jnp.concatenate([hot, hot], axis=1),
        jnp.concatenate(halves(value), axis=1),
        (((1,), (1,)), ((), ())),
        preferred_element_type=F32,
    )


def pick_across(value, hot):
    return lax.dot_general(
        jnp.concatenate(halves(value), axis=1),
        jnp.concatenate([hot, hot], axis=1),
        (((1,), (1,)), ((), ())),
        preferred_element_type=F32,
    )


def gather_exact(value, hot):
    top, rest = halves(value)
    middle, low = halves(value - top.astype(F32))
    return lax.dot_general(
        jnp.concatenate([top, middle, low], axis=1),
        jnp.concatenate([hot, hot, hot], axis=1),
        (((1,), (1,)), ((), ())),
        preferred_element_type=F32,
    )


def first_half(rows):
    return iota((rows, LANES), 1) < PART


def paired(blocks):
    rows = blocks[0].shape[0]
    blocks = list(blocks) + [jnp.zeros_like(blocks[0])]
    return jnp.concatenate(
        [jnp.where(first_half(rows), blocks[2 * t], blocks[2 * t + 1]) for t in range(TWOS)],
        axis=1,
    )


def place_of(q):
    return LANES * (q % 2) + FPAD * (q // 2)


def stacked(value):
    top = value.astype(BF16).astype(F32)
    rest = value - top
    fill = PART - value.shape[0]
    gap = [jnp.zeros((fill, value.shape[1]), F32)] if fill else []
    return jnp.concatenate([top] + gap + [rest] + gap + [top] + gap, axis=0).astype(BF16)


def products(blocks, row_of, count=NQ):
    totals = [None] * NQ
    for q in range(count):
        for position, block in enumerate(blocks):
            left = block(q)
            for p in range(NQ):
                term = left * row_of(position, q, p)
                totals[p] = term if totals[p] is None else totals[p] + term
    return totals


def chain_weights(stiff_time, face_back, out, tips, raw):
    raw[...] = jnp.zeros(raw.shape, F32)
    for start, valid, padded, _ in LEVELS:
        for d in range(3):
            raw[start + d * padded : start + d * padded + valid, 0:NB] = stiff_time[d, 0:valid, :]
    for j in range(4):
        raw[BACK + j * FPAD : BACK + j * FPAD + NF, 0:NB] = face_back[:, j, :]
    once = raw[...]
    top = once.astype(BF16).astype(F32)
    out[:, 0:LANES] = (top + pltpu.roll(top, PART, 1)).astype(BF16)
    out[:, LANES : 2 * LANES] = (once - top).astype(BF16)
    start = LEVELS[-1][0]
    turned = jnp.transpose(once[start : start + LANES])
    for d in range(3):
        column = turned[0:8, 8 * d : 8 * d + 1]
        tips[8 * d : 8 * d + 8, :] = jnp.broadcast_to(column, (8, LANES))
    tips[24 : 24 + OWN, :] = jnp.broadcast_to(once[BACK : BACK + OWN, 0:1], (OWN, LANES))


def weigh(weights, start, rows, value):
    return jnp.dot(
        weights[start : start + rows, 0 : 3 * PART], stacked(value), preferred_element_type=F32
    )


def wide_sums(block, star):
    blocks = [functools.partial(block, d) for d in range(3)]
    return products(blocks, lambda d, q, p: star[q, p, d : d + 1, :])


def narrow_sums(block, star):
    return products(
        [functools.partial(block, d) for d in range(3)],
        lambda d, t, p: star[STAR_ROWS * t + 4 * p + d : STAR_ROWS * t + 4 * p + d + 1, :],
        TWOS,
    )


def narrow_join(totals):
    half = first_half(totals[0].shape[0])
    totals = list(totals) + [jnp.zeros_like(totals[0])]
    pieces = []
    for t in range(TWOS):
        even, odd = totals[2 * t], totals[2 * t + 1]
        crossed = pltpu.roll(jnp.where(half, odd, even), PART, 1)
        pieces.append(jnp.where(half, even, odd) + crossed)
    return jnp.concatenate(pieces, axis=1)


def wide_join(totals):
    return jnp.concatenate(totals, axis=1)


def chain_of(first, star, weights, tips, sums, join):
    now = first
    chain = [first]
    for start, _, padded, rows in LEVELS[:-1]:
        found = weigh(weights, start, rows, now)
        now = join(
            sums(lambda d, c: found[d * padded : (d + 1) * padded, lanes(c)], star)
        )
        chain.append(now)
    totals = sums(lambda d, c: now[:, lanes(c)] * tips[8 * d : 8 * d + 8, :], star)
    return chain, join([jnp.sum(total, axis=0, keepdims=True) for total in totals])


def with_end(integral, faces, end, tips):
    row = jnp.where(iota((8, end.shape[1]), 0) == 0, end, 0.0)
    low = jnp.concatenate([integral[0:8] + row, integral[8:VPAD]], axis=0)
    column = tips[24 : 24 + OWN, :]
    count = end.shape[1] // LANES
    faces = [faces[:, lanes(c)] + column * end[:, lanes(c)] for c in range(count)]
    return low, jnp.concatenate(faces, axis=1)


def integral_of(chain, weights):
    pieces = []
    edges = [0, 8, 16, 24, 40, 56]
    for low, high in zip(edges[:-1], edges[1:]):
        total = None
        for depth in range(len(chain)):
            if chain[depth].shape[0] < high:
                continue
            term = (weights[depth] * (-1) ** depth) * chain[depth][low:high]
            total = term if total is None else total + term
        pieces.append(total)
    return jnp.concatenate(pieces, axis=0)


def face_table(faces):
    def block(q):
        return jnp.concatenate(
            [faces[j * FPAD : (j + 1) * FPAD, lanes(q)] for j in range(4)], axis=1
        )

    even = [block(q) for q in range(0, NQ, 2)]
    odd = [block(q) for q in range(1, NQ, 2)]
    return jnp.concatenate(
        even
        + [jnp.zeros((LANES - len(even) * FPAD, FACES), F32)]
        + odd
        + [jnp.zeros((LANES - len(odd) * FPAD, FACES), F32)],
        axis=0,
    )


def narrow_table(faces):
    rows = [
        jnp.concatenate([faces[j * FPAD : (j + 1) * FPAD, lanes(t)] for j in range(4)], axis=1)
        for t in range(TWOS)
    ]
    return jnp.concatenate(rows + [jnp.zeros((LANES - TWOS * FPAD, FACES), F32)], axis=0)


def list_rows():
    row = iota((PEERS * BOTH, LANES), 0)
    peer = (row >= BOTH).astype(jnp.int32) + (row >= 2 * BOTH).astype(jnp.int32)
    peer = peer + (row >= 3 * BOTH).astype(jnp.int32)
    return peer, row - BOTH * peer


def list_hot(lists, face):
    return lists[...] == iota((PEERS * BOTH, LANES), 1) + LANES * face


def deliver(sent, position, pair_out, cross_out):
    odd = lax.rem(position, 2) == 1
    first, second = sent[0:BOTH], sent[BOTH : 2 * BOTH]
    pair_out[0:BOTH, :] = jnp.where(odd, second, first)
    pair_out[BOTH : 3 * BOTH, :] = sent[2 * BOTH : 4 * BOTH]
    cross_out[...] = jnp.where(odd, first, second)


def list_column(fine, coarse):
    peer, inner = list_rows()
    total = jnp.zeros((PEERS * BOTH, LANES), F32)
    for kind, entries in enumerate((fine, coarse)):
        here = iota((PEERS * BOTH, LANES), 1) == inner - kind * SLOTS
        for k in range(PEERS):
            total = total + jnp.where(here & (peer == k), entries[k : k + 1, :], 0.0)
    column = jnp.sum(total, axis=1, keepdims=True)
    return jnp.broadcast_to(column, (PEERS * BOTH, LANES)).astype(jnp.int32)


def first_kernel(
    place, dofs, star, stiff_time, face_back, fine_send, coarse_send, labels, *rest
):
    later = rest[:7]
    (
        state_out, low_out, tail_out, faces_out, pair_out, cross_out,
        weights_out, tips_out, star_out, labels_out, lists_out,
    ) = rest[7:18]
    later_out = rest[18:25]
    raw, dofs_here, time_here, back_here, wide, fine_here, coarse_here, ready = rest[25:]
    position = place[0]
    moves = [
        (dofs, dofs_here),
        (stiff_time, time_here),
        (face_back, back_here),
        (star, star_out),
        (fine_send, fine_here),
        (coarse_send, coarse_here),
        (labels, labels_out),
    ]
    first = len(moves)
    moves += list(zip(later, later_out))
    copies = [
        pltpu.make_async_copy(source, target, ready.at[number])
        for number, (source, target) in enumerate(moves)
    ]
    for copy in copies:
        copy.start()
    for copy in copies[1:3]:
        copy.wait()
    chain_weights(time_here, back_here, weights_out, tips_out, raw)
    copies[0].wait()
    state = jnp.concatenate([dofs_here[q] for q in range(NQ)], axis=1)
    state_out[...] = state
    copies[3].wait()
    chain, end = chain_of(state, star_out, weights_out, tips_out, wide_sums, wide_join)
    first_weights = taylor_weights(0.0, 1.0 / SUBSTEPS)
    integral = integral_of(chain, first_weights)
    for copy in copies[4:first]:
        copy.wait()
    wide[...] = jnp.zeros(wide.shape, F32)
    wide[0:PEERS, 0:SLOTS] = fine_here[...].astype(F32)
    wide[8 : 8 + PEERS, 0:SLOTS] = coarse_here[...].astype(F32)
    lists_out[...] = list_column(wide[0:PEERS], wide[8 : 8 + PEERS])
    faces = weigh(weights_out, BACK, OWN, integral)
    low, faces = with_end(integral, faces, -first_weights[-1] * end, tips_out)
    low_out[...] = low
    faces_out[...] = faces
    hot = jnp.concatenate(
        [jnp.where(list_hot(lists_out, j), 1.0, 0.0) for j in range(4)], axis=1
    ).astype(BF16)
    deliver(pick_rows(hot, face_table(faces)), position, pair_out, cross_out)
    end = jnp.where(iota((8, COLS), 0) == 0, end, 0.0)
    tail_out[...] = jnp.concatenate(chain[1:] + [end], axis=0)
    for copy in copies[first:]:
        copy.wait()


def prepare_kernel(
    state, tail, source, orientation, flux_other, face_front, face_turn, stiff_vol,
    star, labels, lists,
    coarse_out, slot_flux_out, slot_code_out, slot_hot_out, lift_out, slot_lift_out,
    narrow_hot_out, slot_narrow_out, star_out, send_out,
    table, fronts, tall, slot_tall, flat,
):
    fine = labels[...] == 1
    before = (iota((LANES, LANES), 0) < iota((LANES, LANES), 1)).astype(F32).astype(BF16)
    marks = jnp.broadcast_to(jnp.where(fine, 1.0, 0.0), (16, LANES)).astype(BF16)
    rank = jnp.dot(marks, before, preferred_element_type=F32)[0:1].astype(jnp.int32)
    rank = jnp.where(fine, rank, -1)
    lane = iota((LANES, LANES), 0)
    lane = jnp.where(lane >= PART, lane - PART, lane)
    narrow_hot = jnp.where(rank == lane, 1.0, 0.0).astype(BF16)
    narrow_hot_out[...] = narrow_hot
    flat[...] = jnp.zeros(flat.shape, F32)
    for q in range(NQ):
        for p in range(NQ):
            start = STAR_ROWS * q + 4 * p
            flat[start : start + 3, :] = star[q, p]
    gathered = gather_exact(flat[...], narrow_hot)
    stars = [gathered[STAR_ROWS * q : STAR_ROWS * (q + 1)] for q in range(NQ)]
    packed = paired(stars)
    for t in range(TWOS):
        star_out[STAR_ROWS * t : STAR_ROWS * (t + 1), :] = packed[:, lanes(t)]
    _, inner = list_rows()
    half = first_half(PEERS * BOTH)
    across = (((1,), (1,)), ((), ()))
    for j in range(4):
        chosen = jnp.where(list_hot(lists, j) & (inner < SLOTS), 1.0, 0.0).astype(BF16)
        found = lax.dot_general(chosen, narrow_hot, across, preferred_element_type=F32)
        send_out[0 : PEERS * BOTH, lanes(j)] = jnp.where(half, found, 0.0).astype(BF16)
        send_out[PEERS * BOTH :, lanes(j)] = jnp.where(half, 0.0, found).astype(BF16)
    chain = [state[...]]
    start = 0
    for _, _, padded, _ in LEVELS:
        chain.append(tail[start : start + padded, :])
        start += padded
    for step in range(1, SUBSTEPS):
        coarse_out[step - 1] = integral_of(
            chain, taylor_weights(step / SUBSTEPS, (step + 1) / SUBSTEPS)
        )
    row = iota((LANES, LANES), 0)
    peer = (row >= BOTH).astype(jnp.int32) + (row >= 2 * BOTH).astype(jnp.int32)
    peer = peer + (row >= 3 * BOTH).astype(jnp.int32)
    inner = row - BOTH * peer
    kind = (inner >= SLOTS).astype(jnp.int32)
    wanted = kind * (PEERS * SLOTS - SLOTS) + peer * SLOTS + inner + FACES
    wanted = jnp.where(row < PEERS * BOTH, wanted, -1)
    blocks = [jnp.where(source[i : i + 1, :] == wanted, 1.0, 0.0) for i in range(4)]
    slot_hot = (blocks[0] + blocks[1] + blocks[2] + blocks[3]).astype(BF16)
    slot_hot_out[...] = slot_hot
    slot_narrow_out[...] = lax.dot_general(
        slot_hot, narrow_hot, across, preferred_element_type=F32
    ).astype(BF16)
    hot = jnp.concatenate(blocks, axis=1).astype(BF16)
    codes = jnp.concatenate(
        [
            jnp.where(iota((16, LANES), 0) - 3 * i == orientation[i : i + 1, :], 1.0, 0.0)
            for i in range(4)
        ],
        axis=1,
    ).astype(BF16)
    dims = (((1,), (1,)), ((), ()))
    found = lax.dot_general(codes, hot, dims, preferred_element_type=F32)
    for code in range(12):
        slot_code_out[SLOT_PAD * code : SLOT_PAD * (code + 1), :] = jnp.broadcast_to(
            found[code : code + 1], (SLOT_PAD, LANES)
        ).astype(BF16)
    table[...] = jnp.zeros(table.shape, F32)
    for i in range(4):
        for q in range(NQ):
            table[16 * q : 16 * q + NQ, lanes(i)] = flux_other[q, :, i, :]
    slot_flux_out[...] = pick_across(table[...], hot)

    fronts[...] = jnp.zeros(fronts.shape, F32)
    tall[...] = jnp.zeros(tall.shape, F32)
    slot_tall[...] = jnp.zeros(slot_tall.shape, F32)
    for i in range(4):
        fronts[0:NF, i * LANES : i * LANES + NB] = face_front[:, i, :]
    for code in range(3):
        turned = lax.dot_general(
            face_turn[code], fronts[0:NF, :], (((0,), (0,)), ((), ())),
            precision=HIGHEST, preferred_element_type=F32,
        )
        for i in range(4):
            start = FPAD * (3 * i + code)
            tall[start : start + NF, :] = -turned[:, lanes(i)]
            start = SLOT_PAD * (3 * i + code)
            slot_tall[start : start + NF, :] = -turned[:, lanes(i)]
    for i in range(4):
        start = REM + FPAD * i
        tall[start : start + NF, :] = -fronts[0:NF, lanes(i)]
    for d in range(3):
        start = REM + OWN + VPAD * d
        tall[start : start + NLOW, 0:NB] = stiff_vol[d]
    lift_out[...] = jnp.transpose(tall[...])[0:NB]
    whole = jnp.transpose(slot_tall[...])[0:PART]
    top = whole.astype(BF16)
    slot_lift_out[0:PART, 0:SLOT_REM] = top
    slot_lift_out[0:PART, SLOT_REM:] = top
    slot_lift_out[PART:, 0:SLOT_REM] = (whole - top.astype(F32)).astype(BF16)
    slot_lift_out[PART:, SLOT_REM:] = jnp.zeros((PART, SLOT_REM), BF16)


def local_kernel(*refs, step):
    if step == 0:
        state, low, faces, *rest = refs
        state, low, faces = state[...], low[...], faces[...]
    else:
        state, by_slot, slot_hot, low, faces, coarse_faces, *rest = refs
    star, flux_self, flux_other, source, orientation, lift, *rest = rest
    coarse, weights, lists, narrow_hot, labels, *rest = rest
    out, *rest = rest
    if step > 0:
        state = state[...] + by_elements(by_slot[...], slot_hot[...])
        back = jnp.transpose(narrow_hot[...].astype(F32))
        half = iota((LANES, LANES), 1) < PART
        spread = jnp.concatenate(
            [
                jnp.transpose(jnp.where(half, back, 0.0)),
                jnp.transpose(jnp.where(half, 0.0, back)),
            ],
            axis=1,
        ).astype(BF16)
        both = VPAD + OWN
        rows = [
            part[:, lanes(t)] for t in range(TWOS) for part in (low, faces)
        ]
        wide = pick(jnp.concatenate(rows, axis=0), spread)
        wide = [wide[both * t : both * (t + 1)] for t in range(TWOS)]
        wide = jnp.concatenate(wide, axis=1)[:, 0:COLS]
        fine = labels[...] == 1
        fine = jnp.concatenate([fine] * NQ, axis=1)
        low = jnp.where(fine, wide[0:VPAD], coarse[step - 1, 0:VPAD, :])
        faces = jnp.where(fine, wide[VPAD:both], coarse_faces[...])
    if step + 1 < SUBSTEPS:
        narrow_out, next_faces_out, next_sent_out, stack = rest
        next_faces = weigh(weights, BACK, OWN, coarse[step])
        next_faces_out[...] = next_faces
        _, inner = list_rows()
        hot = jnp.concatenate(
            [jnp.where(list_hot(lists, j) & (inner >= SLOTS), 1.0, 0.0) for j in range(4)],
            axis=1,
        ).astype(BF16)
        next_sent_out[...] = pick_rows(hot, face_table(next_faces))
    else:
        (stack,) = rest
    column = iota((FACES, LANES), 0)
    hot = jnp.concatenate(
        [
            jnp.where(column == source[i : i + 1, :], 1.0, 0.0).astype(BF16)
            for i in range(4)
        ],
        axis=1,
    )
    found = pick(face_table(faces), hot)
    for d in range(3):
        totals = products(
            [lambda q: low[:, lanes(q)]], lambda _, q, p: star[q, p, d : d + 1, :]
        )
        base = REM + OWN + VPAD * d
        for p in range(NQ):
            stack[base : base + VPAD, lanes(p)] = totals[p]
    for i in range(4):
        totals = products(
            [lambda q: faces[i * FPAD : (i + 1) * FPAD, lanes(q)]],
            lambda _, q, p: flux_self[q, p, i : i + 1, :],
        )
        for p in range(NQ):
            stack[REM + FPAD * i : REM + FPAD * (i + 1), lanes(p)] = totals[p]
    for i in range(4):
        totals = products(
            [lambda q: found[place_of(q) : place_of(q) + FPAD, lanes(i)]],
            lambda _, q, p: flux_other[q, p, i : i + 1, :],
        )
        for code in range(3):
            mask = jnp.where(orientation[i : i + 1, :] == code, 1.0, 0.0)
            base = FPAD * (3 * i + code)
            for p in range(NQ):
                stack[base : base + FPAD, lanes(p)] = totals[p] * mask
    total = state + jnp.dot(
        lift[:, 0:DEEP], stack[...], precision=HIGH, preferred_element_type=F32
    )
    out[...] = total
    if step + 1 < SUBSTEPS:
        tall = jnp.concatenate([total[:, lanes(q)] for q in range(NQ)], axis=0)
        found = pick_across(tall, narrow_hot[...])
        narrow_out[...] = paired([found[NB * q : NB * (q + 1)] for q in range(NQ)])


def by_elements(by_slot, slot_hot):
    found = pick(by_slot, slot_hot)
    return jnp.concatenate([found[NB * p : NB * (p + 1)] for p in range(NQ)], axis=1)


def remote_part(position, near, upper, lower, slot_flux, slot_code, lift):
    odd = lax.rem(position, 2) == 1
    behind_up = lax.rem(position, 4) < 2
    up, down = upper[...], lower[...]
    behind = jnp.where(behind_up, up, down)
    ahead = jnp.where(behind_up, down, up)
    here = jnp.where(odd, near[0:BOTH, :], near[3 * BOTH : 4 * BOTH, :])
    rows = jnp.concatenate(
        [
            jnp.where(odd, here, behind[0:BOTH]),
            jnp.where(odd, ahead[0:BOTH], here),
            behind[BOTH : 2 * BOTH],
            ahead[BOTH : 2 * BOTH],
            jnp.zeros((LANES - PEERS * BOTH, WIDTH), F32),
        ],
        axis=0,
    )
    received = jnp.transpose(rows)
    totals = products(
        [lambda q: received[place_of(q) : place_of(q) + FPAD]],
        lambda _, q, p: slot_flux[16 * q + p : 16 * q + p + 1, :],
    )
    codes = [slot_code[SLOT_PAD * code : SLOT_PAD * (code + 1), :] for code in range(12)]
    gap = jnp.zeros((SLOT_PAD - FPAD, LANES), F32)
    columns = []
    for p in range(NQ):
        both = halves(jnp.concatenate([totals[p], gap], axis=0))
        masked = [part * mask for part in both for mask in codes]
        columns.append(jnp.concatenate(masked, axis=0))
    masked = jnp.concatenate(columns, axis=1)
    lifted = jnp.dot(lift[...], masked, preferred_element_type=F32)
    lifted = lifted[0:NB] + lifted[PART : PART + NB]
    return jnp.concatenate([lifted[:, lanes(p)] for p in range(NQ)], axis=0)


def next_kernel(
    place, near, upper, lower, slot_flux, slot_code, lift,
    narrow, slot_narrow, star, weights, tips, send_hot, coarse_sent,
    by_slot_out, low_out, faces_out, pair_out, cross_out,
):
    position = place[0]
    by_slot = remote_part(position, near, upper, lower, slot_flux, slot_code, lift)
    by_slot_out[...] = by_slot
    found = pick(by_slot, slot_narrow[...])
    now = narrow[...] + paired([found[NB * p : NB * (p + 1)] for p in range(NQ)])
    chain, end = chain_of(now, star, weights, tips, narrow_sums, narrow_join)
    first_weights = taylor_weights(0.0, 1.0 / SUBSTEPS)
    integral = integral_of(chain, first_weights)
    faces = weigh(weights, BACK, OWN, integral)
    low, faces = with_end(integral, faces, -first_weights[-1] * end, tips)
    low_out[...] = low
    faces_out[...] = faces
    found = pick_rows(send_hot[...], narrow_table(faces))
    rows = PEERS * BOTH
    sent = jnp.concatenate([found[0:rows], found[rows : 2 * rows]], axis=1) + coarse_sent[...]
    deliver(sent, position, pair_out, cross_out)


def last_kernel(
    place, near, upper, lower, slot_flux, slot_code, lift, state, slot_hot, out
):
    by_slot = remote_part(place[0], near, upper, lower, slot_flux, slot_code, lift)
    total = state[...] + by_elements(by_slot, slot_hot[...])
    for q in range(NQ):
        out[q] = total[:, lanes(q)]


def floats(*shape):
    return jax.ShapeDtypeStruct(shape, F32)


def call(kernel, args, outs, scratch, scalars=0, inside=False, flops=2.0e7):
    smem = pl.BlockSpec(memory_space=pltpu.SMEM)
    vmem = pl.BlockSpec(memory_space=pltpu.VMEM)
    given = pl.BlockSpec(memory_space=pl.ANY) if inside else vmem
    if inside:
        args = args[:scalars] + tuple(
            pltpu.with_memory_space_constraint(item, pltpu.HBM) for item in args[scalars:]
        )
    moved = 4 * sum(math.prod(item.shape) for item in list(args) + list(outs))
    return pl.pallas_call(
        kernel,
        in_specs=[smem] * scalars + [given] * (len(args) - scalars),
        out_specs=[vmem] * len(outs),
        out_shape=outs,
        scratch_shapes=[
            pltpu.VMEM(item, F32) if isinstance(item, tuple) else item for item in scratch
        ],
        compiler_params=pltpu.CompilerParams(vmem_limit_bytes=40 * 2**20),
        cost_estimate=pl.CostEstimate(flops=int(flops), bytes_accessed=moved, transcendentals=0),
    )(*args)


def swaps(count, first):
    pairs = []
    for low in range(2 * first, count - 2, 4):
        for one, other in ((low, low + 3), (low + 1, low + 2)):
            pairs += [(one, other), (other, one)]
    return pairs


def local(
    dofs, star, flux_self, flux_other, labels, neighbour_source, orientation,
    fine_send, coarse_send, stiff_time, stiff_vol, face_back, face_front, face_turn,
):
    count = lax.axis_size("dom")
    pairs = [[low, low + 1] for low in range(0, count, 2)]
    place = lax.axis_index("dom").astype(jnp.int32)
    partner = jnp.where(place % 2 == 1, BOTH, 4 * BOTH)
    upper_from = partner + jnp.where(place % 4 >= 2, 0, BOTH)
    lower_from = partner + jnp.where(place % 4 >= 2, BOTH, 0)
    place = place.reshape(1)
    labels = labels.reshape(1, LANES)
    later = (
        flux_self.transpose(1, 2, 0, 3),
        flux_other.transpose(1, 2, 0, 3),
        neighbour_source,
        orientation,
        face_front.transpose(2, 0, 1),
        face_turn,
        stiff_vol.transpose(0, 2, 1),
    )
    star = star.transpose(1, 2, 0, 3)
    back = face_back.transpose(1, 0, 2)
    message = floats(BOTH, WIDTH)
    sent_shapes = [floats(OWN, COLS), floats(3 * BOTH, WIDTH), message]
    like = lambda item: jax.ShapeDtypeStruct(item.shape, item.dtype)
    found = call(
        first_kernel,
        (place, dofs.transpose(1, 0, 2), star, stiff_time, back, fine_send, coarse_send, labels)
        + later,
        [floats(NB, COLS), floats(VPAD, COLS), floats(TAIL, COLS)]
        + sent_shapes
        + [jax.ShapeDtypeStruct((CHAIN_ROWS, 2 * LANES), BF16)]
        + [floats(24 + OWN, LANES), like(star), like(labels)]
        + [jax.ShapeDtypeStruct((PEERS * BOTH, LANES), jnp.int32)]
        + [like(item) for item in later],
        [(CHAIN_ROWS, LANES), (NQ, NB, LANES), stiff_time.shape, back.shape, (16, LANES)]
        + [pltpu.VMEM(item.shape, jnp.int32) for item in (fine_send, coarse_send)]
        + [pltpu.SemaphoreType.DMA((7 + len(later),))],
        scalars=1,
        inside=True,
    )
    state, low, tail, faces, pair, cross, weights, tips, star, labels, lists = found[:11]
    flux_self, flux_other, source, orientation, front, turn, vol = found[11:]
    halved = lambda *shape: jax.ShapeDtypeStruct(shape, BF16)
    prepared = call(
        prepare_kernel,
        (state, tail, source, orientation, flux_other, front, turn, vol, star, labels, lists),
        [
            floats(SUBSTEPS - 1, NB, COLS), floats(16 * NQ, LANES), halved(SLOT_REM, LANES),
            halved(LANES, LANES), floats(NB, DEEP_PAD), halved(2 * PART, 2 * SLOT_REM),
            halved(LANES, LANES), halved(LANES, LANES), floats(TWOS * STAR_ROWS, LANES),
            halved(2 * PEERS * BOTH, FACES),
        ],
        [
            (16 * NQ, FACES), (FPAD, FACES), (DEEP_PAD, LANES), (SLOT_REM, LANES),
            (NQ * STAR_ROWS, LANES),
        ],
    )
    coarse, slot_flux, slot_code, slot_hot, lift, slot_lift = prepared[:6]
    narrow_hot, slot_narrow, narrow_star, send_hot = prepared[6:]
    fixed = (star, flux_self, flux_other, source, orientation, lift)
    fixed += (coarse, weights, lists, narrow_hot, labels)
    known = (state, low, faces)
    for step in range(SUBSTEPS):
        near = lax.all_gather(pair, "dom", axis_index_groups=pairs, tiled=True)
        passed = lax.dynamic_slice(near, (lower_from, 0), (BOTH, WIDTH))
        lower = jnp.concatenate([cross, passed], axis=0)
        lower, cross, shared = lax.optimization_barrier((lower, cross, near))
        passed = lax.dynamic_slice(shared, (upper_from, 0), (BOTH, WIDTH))
        upper = jnp.concatenate([cross, passed], axis=0)
        upper = lax.ppermute(upper, "dom", swaps(count, 1))
        lower = lax.ppermute(lower, "dom", swaps(count, 0))
        ahead = [floats(NB, NARROW), floats(OWN, COLS), floats(PEERS * BOTH, WIDTH)]
        state, *made = call(
            functools.partial(local_kernel, step=step),
            known + fixed,
            [floats(NB, COLS)] + (ahead if step + 1 < SUBSTEPS else []),
            [(DEEP, COLS)],
        )
        received = (place, near, upper, lower, slot_flux, slot_code, slot_lift)
        if step + 1 < SUBSTEPS:
            narrow, coarse_faces, coarse_sent = made
            by_slot, low, faces, pair, cross = call(
                next_kernel,
                received
                + (narrow, slot_narrow, narrow_star, weights, tips, send_hot, coarse_sent),
                [floats(NQ * NB, LANES), floats(VPAD, NARROW), floats(OWN, NARROW)]
                + sent_shapes[1:],
                [],
                scalars=1,
            )
            known = (state, by_slot, slot_hot, low, faces, coarse_faces)
    (result,) = call(
        last_kernel, received + (state, slot_hot), [floats(NQ, NB, LANES)], [], scalars=1
    )
    return result.transpose(1, 0, 2)


def solution(mesh):
    split = P(None, None, "dom")
    face = P(None, None, None, "dom")
    row = P(None, "dom")
    in_specs = (split, face, face, face, P("dom"), row, row, row, row, P(), P(), P(), P(), P())
    return jax.shard_map(local, mesh=mesh, in_specs=in_specs, out_specs=split, check_vma=False)
```

```python
import functools
import math

import jax
import jax.numpy as jnp
from jax import lax
from jax.experimental import pallas as pl
from jax.experimental.pallas import tpu as pltpu
from jax.sharding import PartitionSpec as P

ORDER = 6
SUBSTEPS = 4
NQ = 9
NB = 56
NLOW = 35
NF = 21
PEERS = 4
SLOTS = 12
LANES = 128
FPAD = 24
VPAD = 40
BOTH = 2 * SLOTS
WIDTH = 256
COLS = NQ * LANES
FACES = 4 * LANES
REM = 12 * FPAD
SLOT_PAD = 32
SLOT_REM = 12 * SLOT_PAD
OWN = 4 * FPAD
DEEP = REM + OWN + 3 * VPAD
DEEP_PAD = 512
LEVELS = [(0, 35, 40, 128), (128, 20, 24, 80), (208, 10, 16, 48), (256, 4, 8, 32), (288, 1, 8, 32)]
BACK = 320
CHAIN_ROWS = BACK + OWN
TAIL = 96
PART = 64
TWOS = 5
NARROW = TWOS * LANES
STAR_ROWS = 40
HIGH = lax.Precision.HIGH
HIGHEST = lax.Precision.HIGHEST
F32 = jnp.float32
BF16 = jnp.bfloat16


def taylor_weights(start, stop):
    return [
        (stop ** (depth + 1) - start ** (depth + 1)) / math.factorial(depth + 1)
        for depth in range(ORDER)
    ]


def lanes(index):
    return slice(index * LANES, (index + 1) * LANES)


def iota(shape, dim):
    return lax.broadcasted_iota(jnp.int32, shape, dim)


def halves(value):
    top = value.astype(BF16)
    return top, (value - top.astype(F32)).astype(BF16)


def pick(value, hot):
    return jnp.dot(
        jnp.concatenate(halves(value), axis=1),
        jnp.concatenate([hot, hot], axis=0),
        preferred_element_type=F32,
    )


def pick_rows(hot, value):
    return lax.dot_general(
        jnp.concatenate([hot, hot], axis=1),
        jnp.concatenate(halves(value), axis=1),
        (((1,), (1,)), ((), ())),
        preferred_element_type=F32,
    )


def pick_across(value, hot):
    return lax.dot_general(
        jnp.concatenate(halves(value), axis=1),
        jnp.concatenate([hot, hot], axis=1),
        (((1,), (1,)), ((), ())),
        preferred_element_type=F32,
    )


def gather_exact(value, hot):
    top, rest = halves(value)
    middle, low = halves(value - top.astype(F32))
    return lax.dot_general(
        jnp.concatenate([top, middle, low], axis=1),
        jnp.concatenate([hot, hot, hot], axis=1),
        (((1,), (1,)), ((), ())),
        preferred_element_type=F32,
    )


def first_half(rows):
    return iota((rows, LANES), 1) < PART


def paired(blocks):
    rows = blocks[0].shape[0]
    blocks = list(blocks) + [jnp.zeros_like(blocks[0])]
    return jnp.concatenate(
        [jnp.where(first_half(rows), blocks[2 * t], blocks[2 * t + 1]) for t in range(TWOS)],
        axis=1,
    )


def place_of(q):
    return LANES * (q % 2) + FPAD * (q // 2)


def stacked(value):
    top = value.astype(BF16).astype(F32)
    rest = value - top
    fill = PART - value.shape[0]
    gap = [jnp.zeros((fill, value.shape[1]), F32)] if fill else []
    return jnp.concatenate([top] + gap + [rest] + gap + [top] + gap, axis=0).astype(BF16)


def products(blocks, row_of, count=NQ):
    totals = [None] * NQ
    for q in range(count):
        for position, block in enumerate(blocks):
            left = block(q)
            for p in range(NQ):
                term = left * row_of(position, q, p)
                totals[p] = term if totals[p] is None else totals[p] + term
    return totals


def chain_weights(stiff_time, face_back, out, tips, raw):
    raw[...] = jnp.zeros(raw.shape, F32)
    for start, valid, padded, _ in LEVELS:
        for d in range(3):
            raw[start + d * padded : start + d * padded + valid, 0:NB] = stiff_time[d, 0:valid, :]
    for j in range(4):
        raw[BACK + j * FPAD : BACK + j * FPAD + NF, 0:NB] = face_back[:, j, :]
    once = raw[...]
    top = once.astype(BF16).astype(F32)
    out[:, 0:LANES] = (top + pltpu.roll(top, PART, 1)).astype(BF16)
    out[:, LANES : 2 * LANES] = (once - top).astype(BF16)
    start = LEVELS[-1][0]
    turned = jnp.transpose(once[start : start + LANES])
    for d in range(3):
        column = turned[0:8, 8 * d : 8 * d + 1]
        tips[8 * d : 8 * d + 8, :] = jnp.broadcast_to(column, (8, LANES))
    tips[24 : 24 + OWN, :] = jnp.broadcast_to(once[BACK : BACK + OWN, 0:1], (OWN, LANES))


def weigh(weights, start, rows, value):
    return jnp.dot(
        weights[start : start + rows, 0 : 3 * PART], stacked(value), preferred_element_type=F32
    )


def wide_sums(block, star):
    blocks = [functools.partial(block, d) for d in range(3)]
    return products(blocks, lambda d, q, p: star[q, p, d : d + 1, :])


def narrow_sums(block, star):
    return products(
        [functools.partial(block, d) for d in range(3)],
        lambda d, t, p: star[STAR_ROWS * t + 4 * p + d : STAR_ROWS * t + 4 * p + d + 1, :],
        TWOS,
    )


def narrow_join(totals):
    half = first_half(totals[0].shape[0])
    totals = list(totals) + [jnp.zeros_like(totals[0])]
    pieces = []
    for t in range(TWOS):
        even, odd = totals[2 * t], totals[2 * t + 1]
        crossed = pltpu.roll(jnp.where(half, odd, even), PART, 1)
        pieces.append(jnp.where(half, even, odd) + crossed)
    return jnp.concatenate(pieces, axis=1)


def wide_join(totals):
    return jnp.concatenate(totals, axis=1)


def chain_of(first, star, weights, tips, sums, join, arrived=None):
    now = first
    chain = [first]
    for start, _, padded, rows in LEVELS[:-1]:
        found = weigh(weights, start, rows, now)
        if arrived is not None and len(chain) == 1:
            arrived()
        now = join(
            sums(lambda d, c: found[d * padded : (d + 1) * padded, lanes(c)], star)
        )
        chain.append(now)
    totals = sums(lambda d, c: now[:, lanes(c)] * tips[8 * d : 8 * d + 8, :], star)
    return chain, join([jnp.sum(total, axis=0, keepdims=True) for total in totals])


def with_end(integral, faces, end, tips):
    row = jnp.where(iota((8, end.shape[1]), 0) == 0, end, 0.0)
    low = jnp.concatenate([integral[0:8] + row, integral[8:VPAD]], axis=0)
    column = tips[24 : 24 + OWN, :]
    count = end.shape[1] // LANES
    faces = [faces[:, lanes(c)] + column * end[:, lanes(c)] for c in range(count)]
    return low, jnp.concatenate(faces, axis=1)


def integral_of(chain, weights):
    pieces = []
    edges = [0, 8, 16, 24, 40, 56]
    for low, high in zip(edges[:-1], edges[1:]):
        total = None
        for depth in range(len(chain)):
            if chain[depth].shape[0] < high:
                continue
            term = (weights[depth] * (-1) ** depth) * chain[depth][low:high]
            total = term if total is None else total + term
        pieces.append(total)
    return jnp.concatenate(pieces, axis=0)


def face_table(faces):
    def block(q):
        return jnp.concatenate(
            [faces[j * FPAD : (j + 1) * FPAD, lanes(q)] for j in range(4)], axis=1
        )

    even = [block(q) for q in range(0, NQ, 2)]
    odd = [block(q) for q in range(1, NQ, 2)]
    return jnp.concatenate(
        even
        + [jnp.zeros((LANES - len(even) * FPAD, FACES), F32)]
        + odd
        + [jnp.zeros((LANES - len(odd) * FPAD, FACES), F32)],
        axis=0,
    )


def narrow_table(faces):
    rows = [
        jnp.concatenate([faces[j * FPAD : (j + 1) * FPAD, lanes(t)] for j in range(4)], axis=1)
        for t in range(TWOS)
    ]
    return jnp.concatenate(rows + [jnp.zeros((LANES - TWOS * FPAD, FACES), F32)], axis=0)


def list_rows():
    row = iota((PEERS * BOTH, LANES), 0)
    peer = (row >= BOTH).astype(jnp.int32) + (row >= 2 * BOTH).astype(jnp.int32)
    peer = peer + (row >= 3 * BOTH).astype(jnp.int32)
    return peer, row - BOTH * peer


def list_hot(lists, face):
    return lists[...] == iota((PEERS * BOTH, LANES), 1) + LANES * face


def deliver(sent, position, pair_out, cross_out):
    odd = lax.rem(position, 2) == 1
    first, second = sent[0:BOTH], sent[BOTH : 2 * BOTH]
    pair_out[0:BOTH, :] = jnp.where(odd, second, first)
    pair_out[BOTH : 3 * BOTH, :] = sent[2 * BOTH : 4 * BOTH]
    cross_out[...] = jnp.where(odd, first, second)


def list_column(fine, coarse):
    peer, inner = list_rows()
    total = jnp.zeros((PEERS * BOTH, LANES), F32)
    for kind, entries in enumerate((fine, coarse)):
        here = iota((PEERS * BOTH, LANES), 1) == inner - kind * SLOTS
        for k in range(PEERS):
            total = total + jnp.where(here & (peer == k), entries[k : k + 1, :], 0.0)
    column = jnp.sum(total, axis=1, keepdims=True)
    return jnp.broadcast_to(column, (PEERS * BOTH, LANES)).astype(jnp.int32)


def first_kernel(
    place, dofs, star, stiff_time, face_back, fine_send, coarse_send, labels, *rest
):
    later = rest[:7]
    (
        state_out, low_out, tail_out, faces_out, pair_out, cross_out,
        weights_out, tips_out, star_out, labels_out, lists_out,
    ) = rest[7:18]
    later_out = rest[18:25]
    raw, dofs_here, time_here, back_here, wide, fine_here, coarse_here, ready = rest[25:]
    position = place[0]
    moves = [
        (dofs, dofs_here),
        (stiff_time, time_here),
        (face_back, back_here),
        (star, star_out),
        (fine_send, fine_here),
        (coarse_send, coarse_here),
        (labels, labels_out),
    ]
    first = len(moves)
    moves += list(zip(later, later_out))
    copies = [
        pltpu.make_async_copy(source, target, ready.at[number])
        for number, (source, target) in enumerate(moves)
    ]
    for copy in (copies[1], copies[2], copies[0], *copies[3:]):
        copy.start()
    for copy in copies[1:3]:
        copy.wait()
    chain_weights(time_here, back_here, weights_out, tips_out, raw)
    copies[0].wait()
    state = jnp.concatenate([dofs_here[q] for q in range(NQ)], axis=1)
    state_out[...] = state
    chain, end = chain_of(
        state, star_out, weights_out, tips_out, wide_sums, wide_join, copies[3].wait
    )
    first_weights = taylor_weights(0.0, 1.0 / SUBSTEPS)
    integral = integral_of(chain, first_weights)
    for copy in copies[4:first]:
        copy.wait()
    wide[...] = jnp.zeros(wide.shape, F32)
    wide[0:PEERS, 0:SLOTS] = fine_here[...].astype(F32)
    wide[8 : 8 + PEERS, 0:SLOTS] = coarse_here[...].astype(F32)
    lists_out[...] = list_column(wide[0:PEERS], wide[8 : 8 + PEERS])
    faces = weigh(weights_out, BACK, OWN, integral)
    low, faces = with_end(integral, faces, -first_weights[-1] * end, tips_out)
    low_out[...] = low
    faces_out[...] = faces
    hot = jnp.concatenate(
        [jnp.where(list_hot(lists_out, j), 1.0, 0.0) for j in range(4)], axis=1
    ).astype(BF16)
    deliver(pick_rows(hot, face_table(faces)), position, pair_out, cross_out)
    end = jnp.where(iota((8, COLS), 0) == 0, end, 0.0)
    tail_out[...] = jnp.concatenate(chain[1:] + [end], axis=0)
    for copy in copies[first:]:
        copy.wait()


def prepare_kernel(
    source, orientation, flux_other, face_front, face_turn, stiff_vol,
    star, labels, lists,
    slot_flux_out, slot_code_out, slot_hot_out, lift_out, slot_lift_out,
    narrow_hot_out, slot_narrow_out, star_out, send_out,
    table, fronts, tall, slot_tall, flat,
):
    fine = labels[...] == 1
    before = (iota((LANES, LANES), 0) < iota((LANES, LANES), 1)).astype(F32).astype(BF16)
    marks = jnp.broadcast_to(jnp.where(fine, 1.0, 0.0), (16, LANES)).astype(BF16)
    rank = jnp.dot(marks, before, preferred_element_type=F32)[0:1].astype(jnp.int32)
    rank = jnp.where(fine, rank, -1)
    lane = iota((LANES, LANES), 0)
    lane = jnp.where(lane >= PART, lane - PART, lane)
    narrow_hot = jnp.where(rank == lane, 1.0, 0.0).astype(BF16)
    narrow_hot_out[...] = narrow_hot
    flat[...] = jnp.zeros(flat.shape, F32)
    for q in range(NQ):
        for p in range(NQ):
            start = STAR_ROWS * q + 4 * p
            flat[start : start + 3, :] = star[q, p]
    gathered = gather_exact(flat[...], narrow_hot)
    stars = [gathered[STAR_ROWS * q : STAR_ROWS * (q + 1)] for q in range(NQ)]
    packed = paired(stars)
    for t in range(TWOS):
        star_out[STAR_ROWS * t : STAR_ROWS * (t + 1), :] = packed[:, lanes(t)]
    _, inner = list_rows()
    half = first_half(PEERS * BOTH)
    across = (((1,), (1,)), ((), ()))
    for j in range(4):
        chosen = jnp.where(list_hot(lists, j) & (inner < SLOTS), 1.0, 0.0).astype(BF16)
        found = lax.dot_general(chosen, narrow_hot, across, preferred_element_type=F32)
        send_out[0 : PEERS * BOTH, lanes(j)] = jnp.where(half, found, 0.0).astype(BF16)
        send_out[PEERS * BOTH :, lanes(j)] = jnp.where(half, 0.0, found).astype(BF16)
    row = iota((LANES, LANES), 0)
    peer = (row >= BOTH).astype(jnp.int32) + (row >= 2 * BOTH).astype(jnp.int32)
    peer = peer + (row >= 3 * BOTH).astype(jnp.int32)
    inner = row - BOTH * peer
    kind = (inner >= SLOTS).astype(jnp.int32)
    wanted = kind * (PEERS * SLOTS - SLOTS) + peer * SLOTS + inner + FACES
    wanted = jnp.where(row < PEERS * BOTH, wanted, -1)
    blocks = [jnp.where(source[i : i + 1, :] == wanted, 1.0, 0.0) for i in range(4)]
    slot_hot = (blocks[0] + blocks[1] + blocks[2] + blocks[3]).astype(BF16)
    slot_hot_out[...] = slot_hot
    slot_narrow_out[...] = lax.dot_general(
        slot_hot, narrow_hot, across, preferred_element_type=F32
    ).astype(BF16)
    hot = jnp.concatenate(blocks, axis=1).astype(BF16)
    codes = jnp.concatenate(
        [
            jnp.where(iota((16, LANES), 0) - 3 * i == orientation[i : i + 1, :], 1.0, 0.0)
            for i in range(4)
        ],
        axis=1,
    ).astype(BF16)
    dims = (((1,), (1,)), ((), ()))
    found = lax.dot_general(codes, hot, dims, preferred_element_type=F32)
    for code in range(12):
        slot_code_out[SLOT_PAD * code : SLOT_PAD * (code + 1), :] = jnp.broadcast_to(
            found[code : code + 1], (SLOT_PAD, LANES)
        ).astype(BF16)
    table[...] = jnp.zeros(table.shape, F32)
    for i in range(4):
        for q in range(NQ):
            table[16 * q : 16 * q + NQ, lanes(i)] = flux_other[q, :, i, :]
    slot_flux_out[...] = pick_across(table[...], hot)

    fronts[...] = jnp.zeros(fronts.shape, F32)
    tall[...] = jnp.zeros(tall.shape, F32)
    slot_tall[...] = jnp.zeros(slot_tall.shape, F32)
    for i in range(4):
        fronts[0:NF, i * LANES : i * LANES + NB] = face_front[:, i, :]
    for code in range(3):
        turned = lax.dot_general(
            face_turn[code], fronts[0:NF, :], (((0,), (0,)), ((), ())),
            precision=HIGHEST, preferred_element_type=F32,
        )
        for i in range(4):
            start = FPAD * (3 * i + code)
            tall[start : start + NF, :] = -turned[:, lanes(i)]
            start = SLOT_PAD * (3 * i + code)
            slot_tall[start : start + NF, :] = -turned[:, lanes(i)]
    for i in range(4):
        start = REM + FPAD * i
        tall[start : start + NF, :] = -fronts[0:NF, lanes(i)]
    for d in range(3):
        start = REM + OWN + VPAD * d
        tall[start : start + NLOW, 0:NB] = stiff_vol[d]
    lift_out[...] = jnp.transpose(tall[...])[0:NB]
    whole = jnp.transpose(slot_tall[...])[0:PART]
    top = whole.astype(BF16)
    slot_lift_out[0:PART, 0:SLOT_REM] = top
    slot_lift_out[0:PART, SLOT_REM:] = top
    slot_lift_out[PART:, 0:SLOT_REM] = (whole - top.astype(F32)).astype(BF16)
    slot_lift_out[PART:, SLOT_REM:] = jnp.zeros((PART, SLOT_REM), BF16)


def local_kernel(*refs, step):
    if step == 0:
        state, low, faces, *rest = refs
        state, low, faces = state[...], low[...], faces[...]
    else:
        state, by_slot, slot_hot, low, faces, coarse_low, coarse_faces, *rest = refs
    star, flux_self, flux_other, source, orientation, lift, *rest = rest
    begin, tail, weights, lists, narrow_hot, labels, *rest = rest
    out, *rest = rest
    if step > 0:
        state = state[...] + by_elements(by_slot[...], slot_hot[...])
        back = jnp.transpose(narrow_hot[...].astype(F32))
        half = iota((LANES, LANES), 1) < PART
        spread = jnp.concatenate(
            [
                jnp.transpose(jnp.where(half, back, 0.0)),
                jnp.transpose(jnp.where(half, 0.0, back)),
            ],
            axis=1,
        ).astype(BF16)
        both = VPAD + OWN
        rows = [
            part[:, lanes(t)] for t in range(TWOS) for part in (low, faces)
        ]
        wide = pick(jnp.concatenate(rows, axis=0), spread)
        wide = [wide[both * t : both * (t + 1)] for t in range(TWOS)]
        wide = jnp.concatenate(wide, axis=1)[:, 0:COLS]
        fine = labels[...] == 1
        fine = jnp.concatenate([fine] * NQ, axis=1)
        low = jnp.where(fine, wide[0:VPAD], coarse_low[...])
        faces = jnp.where(fine, wide[VPAD:both], coarse_faces[...])
    if step + 1 < SUBSTEPS:
        narrow_out, next_low_out, next_faces_out, next_sent_out, stack = rest
        chain = [begin[...]]
        start = 0
        for _, _, padded, _ in LEVELS:
            chain.append(tail[start : start + padded, :])
            start += padded
        coarse = integral_of(
            chain, taylor_weights((step + 1) / SUBSTEPS, (step + 2) / SUBSTEPS)
        )
        next_low_out[...] = coarse[0:VPAD]
        next_faces = weigh(weights, BACK, OWN, coarse)
        next_faces_out[...] = next_faces
        _, inner = list_rows()
        hot = jnp.concatenate(
            [jnp.where(list_hot(lists, j) & (inner >= SLOTS), 1.0, 0.0) for j in range(4)],
            axis=1,
        ).astype(BF16)
        next_sent_out[...] = pick_rows(hot, face_table(next_faces))
    else:
        (stack,) = rest
    column = iota((FACES, LANES), 0)
    hot = jnp.concatenate(
        [
            jnp.where(column == source[i : i + 1, :], 1.0, 0.0).astype(BF16)
            for i in range(4)
        ],
        axis=1,
    )
    found = pick(face_table(faces), hot)
    for d in range(3):
        totals = products(
            [lambda q: low[:, lanes(q)]], lambda _, q, p: star[q, p, d : d + 1, :]
        )
        base = REM + OWN + VPAD * d
        for p in range(NQ):
            stack[base : base + VPAD, lanes(p)] = totals[p]
    for i in range(4):
        totals = products(
            [lambda q: faces[i * FPAD : (i + 1) * FPAD, lanes(q)]],
            lambda _, q, p: flux_self[q, p, i : i + 1, :],
        )
        for p in range(NQ):
            stack[REM + FPAD * i : REM + FPAD * (i + 1), lanes(p)] = totals[p]
    for i in range(4):
        totals = products(
            [lambda q: found[place_of(q) : place_of(q) + FPAD, lanes(i)]],
            lambda _, q, p: flux_other[q, p, i : i + 1, :],
        )
        for code in range(3):
            mask = jnp.where(orientation[i : i + 1, :] == code, 1.0, 0.0)
            base = FPAD * (3 * i + code)
            for p in range(NQ):
                stack[base : base + FPAD, lanes(p)] = totals[p] * mask
    total = state + jnp.dot(
        lift[:, 0:DEEP], stack[...], precision=HIGH, preferred_element_type=F32
    )
    out[...] = total
    if step + 1 < SUBSTEPS:
        tall = jnp.concatenate([total[:, lanes(q)] for q in range(NQ)], axis=0)
        found = pick_across(tall, narrow_hot[...])
        narrow_out[...] = paired([found[NB * q : NB * (q + 1)] for q in range(NQ)])


def by_elements(by_slot, slot_hot):
    found = pick(by_slot, slot_hot)
    return jnp.concatenate([found[NB * p : NB * (p + 1)] for p in range(NQ)], axis=1)


def remote_part(position, near, upper, lower, slot_flux, slot_code, lift):
    odd = lax.rem(position, 2) == 1
    behind_up = lax.rem(position, 4) < 2
    up, down = upper[...], lower[...]
    behind = jnp.where(behind_up, up, down)
    ahead = jnp.where(behind_up, down, up)
    here = jnp.where(odd, near[0:BOTH, :], near[3 * BOTH : 4 * BOTH, :])
    rows = jnp.concatenate(
        [
            jnp.where(odd, here, behind[0:BOTH]),
            jnp.where(odd, ahead[0:BOTH], here),
            behind[BOTH : 2 * BOTH],
            ahead[BOTH : 2 * BOTH],
            jnp.zeros((LANES - PEERS * BOTH, WIDTH), F32),
        ],
        axis=0,
    )
    received = jnp.transpose(rows)
    totals = products(
        [lambda q: received[place_of(q) : place_of(q) + FPAD]],
        lambda _, q, p: slot_flux[16 * q + p : 16 * q + p + 1, :],
    )
    codes = [slot_code[SLOT_PAD * code : SLOT_PAD * (code + 1), :] for code in range(12)]
    gap = jnp.zeros((SLOT_PAD - FPAD, LANES), F32)
    columns = []
    for p in range(NQ):
        both = halves(jnp.concatenate([totals[p], gap], axis=0))
        masked = [part * mask for part in both for mask in codes]
        columns.append(jnp.concatenate(masked, axis=0))
    masked = jnp.concatenate(columns, axis=1)
    lifted = jnp.dot(lift[...], masked, preferred_element_type=F32)
    lifted = lifted[0:NB] + lifted[PART : PART + NB]
    return jnp.concatenate([lifted[:, lanes(p)] for p in range(NQ)], axis=0)


def next_kernel(
    place, near, upper, lower, slot_flux, slot_code, lift,
    narrow, slot_narrow, star, weights, tips, send_hot, coarse_sent,
    by_slot_out, low_out, faces_out, pair_out, cross_out,
):
    position = place[0]
    by_slot = remote_part(position, near, upper, lower, slot_flux, slot_code, lift)
    by_slot_out[...] = by_slot
    found = pick(by_slot, slot_narrow[...])
    now = narrow[...] + paired([found[NB * p : NB * (p + 1)] for p in range(NQ)])
    chain, end = chain_of(now, star, weights, tips, narrow_sums, narrow_join)
    first_weights = taylor_weights(0.0, 1.0 / SUBSTEPS)
    integral = integral_of(chain, first_weights)
    faces = weigh(weights, BACK, OWN, integral)
    low, faces = with_end(integral, faces, -first_weights[-1] * end, tips)
    low_out[...] = low
    faces_out[...] = faces
    found = pick_rows(send_hot[...], narrow_table(faces))
    rows = PEERS * BOTH
    sent = jnp.concatenate([found[0:rows], found[rows : 2 * rows]], axis=1) + coarse_sent[...]
    deliver(sent, position, pair_out, cross_out)


def last_kernel(
    place, near, upper, lower, slot_flux, slot_code, lift, state, slot_hot, out
):
    by_slot = remote_part(place[0], near, upper, lower, slot_flux, slot_code, lift)
    total = state[...] + by_elements(by_slot, slot_hot[...])
    for q in range(NQ):
        out[q] = total[:, lanes(q)]


def floats(*shape):
    return jax.ShapeDtypeStruct(shape, F32)


def call(kernel, args, outs, scratch, scalars=0, inside=False, flops=2.0e7):
    smem = pl.BlockSpec(memory_space=pltpu.SMEM)
    vmem = pl.BlockSpec(memory_space=pltpu.VMEM)
    given = pl.BlockSpec(memory_space=pl.ANY) if inside else vmem
    if inside:
        args = args[:scalars] + tuple(
            pltpu.with_memory_space_constraint(item, pltpu.HBM) for item in args[scalars:]
        )
    moved = 4 * sum(math.prod(item.shape) for item in list(args) + list(outs))
    return pl.pallas_call(
        kernel,
        in_specs=[smem] * scalars + [given] * (len(args) - scalars),
        out_specs=[vmem] * len(outs),
        out_shape=outs,
        scratch_shapes=[
            pltpu.VMEM(item, F32) if isinstance(item, tuple) else item for item in scratch
        ],
        compiler_params=pltpu.CompilerParams(vmem_limit_bytes=40 * 2**20),
        cost_estimate=pl.CostEstimate(flops=int(flops), bytes_accessed=moved, transcendentals=0),
    )(*args)


def swaps(count, first):
    pairs = []
    for low in range(2 * first, count - 2, 4):
        for one, other in ((low, low + 3), (low + 1, low + 2)):
            pairs += [(one, other), (other, one)]
    return pairs


def local(
    dofs, star, flux_self, flux_other, labels, neighbour_source, orientation,
    fine_send, coarse_send, stiff_time, stiff_vol, face_back, face_front, face_turn,
):
    count = lax.axis_size("dom")
    pairs = [[low, low + 1] for low in range(0, count, 2)]
    place = lax.axis_index("dom").astype(jnp.int32)
    partner = jnp.where(place % 2 == 1, BOTH, 4 * BOTH)
    upper_from = partner + jnp.where(place % 4 >= 2, 0, BOTH)
    lower_from = partner + jnp.where(place % 4 >= 2, BOTH, 0)
    place = place.reshape(1)
    labels = labels.reshape(1, LANES)
    later = (
        flux_self.transpose(1, 2, 0, 3),
        flux_other.transpose(1, 2, 0, 3),
        neighbour_source,
        orientation,
        face_front.transpose(2, 0, 1),
        face_turn,
        stiff_vol.transpose(0, 2, 1),
    )
    star = star.transpose(1, 2, 0, 3)
    back = face_back.transpose(1, 0, 2)
    message = floats(BOTH, WIDTH)
    sent_shapes = [floats(OWN, COLS), floats(3 * BOTH, WIDTH), message]
    like = lambda item: jax.ShapeDtypeStruct(item.shape, item.dtype)
    found = call(
        first_kernel,
        (place, dofs.transpose(1, 0, 2), star, stiff_time, back, fine_send, coarse_send, labels)
        + later,
        [floats(NB, COLS), floats(VPAD, COLS), floats(TAIL, COLS)]
        + sent_shapes
        + [jax.ShapeDtypeStruct((CHAIN_ROWS, 2 * LANES), BF16)]
        + [floats(24 + OWN, LANES), like(star), like(labels)]
        + [jax.ShapeDtypeStruct((PEERS * BOTH, LANES), jnp.int32)]
        + [like(item) for item in later],
        [(CHAIN_ROWS, LANES), (NQ, NB, LANES), stiff_time.shape, back.shape, (16, LANES)]
        + [pltpu.VMEM(item.shape, jnp.int32) for item in (fine_send, coarse_send)]
        + [pltpu.SemaphoreType.DMA((7 + len(later),))],
        scalars=1,
        inside=True,
    )
    state, low, tail, faces, pair, cross, weights, tips, star, labels, lists = found[:11]
    flux_self, flux_other, source, orientation, front, turn, vol = found[11:]
    halved = lambda *shape: jax.ShapeDtypeStruct(shape, BF16)
    prepared = call(
        prepare_kernel,
        (source, orientation, flux_other, front, turn, vol, star, labels, lists),
        [
            floats(16 * NQ, LANES), halved(SLOT_REM, LANES),
            halved(LANES, LANES), floats(NB, DEEP_PAD), halved(2 * PART, 2 * SLOT_REM),
            halved(LANES, LANES), halved(LANES, LANES), floats(TWOS * STAR_ROWS, LANES),
            halved(2 * PEERS * BOTH, FACES),
        ],
        [
            (16 * NQ, FACES), (FPAD, FACES), (DEEP_PAD, LANES), (SLOT_REM, LANES),
            (NQ * STAR_ROWS, LANES),
        ],
    )
    slot_flux, slot_code, slot_hot, lift, slot_lift = prepared[:5]
    narrow_hot, slot_narrow, narrow_star, send_hot = prepared[5:]
    fixed = (star, flux_self, flux_other, source, orientation, lift)
    fixed += (state, tail, weights, lists, narrow_hot, labels)
    known = (state, low, faces)
    for step in range(SUBSTEPS):
        near = lax.all_gather(pair, "dom", axis_index_groups=pairs, tiled=True)
        passed = lax.dynamic_slice(near, (lower_from, 0), (BOTH, WIDTH))
        lower = jnp.concatenate([cross, passed], axis=0)
        lower, cross, shared = lax.optimization_barrier((lower, cross, near))
        passed = lax.dynamic_slice(shared, (upper_from, 0), (BOTH, WIDTH))
        upper = jnp.concatenate([cross, passed], axis=0)
        upper = lax.ppermute(upper, "dom", swaps(count, 1))
        lower = lax.ppermute(lower, "dom", swaps(count, 0))
        ahead = [floats(NB, NARROW), floats(VPAD, COLS), floats(OWN, COLS)]
        ahead += [floats(PEERS * BOTH, WIDTH)]
        state, *made = call(
            functools.partial(local_kernel, step=step),
            known + fixed,
            [floats(NB, COLS)] + (ahead if step + 1 < SUBSTEPS else []),
            [(DEEP, COLS)],
        )
        received = (place, near, upper, lower, slot_flux, slot_code, slot_lift)
        if step + 1 < SUBSTEPS:
            narrow, coarse_low, coarse_faces, coarse_sent = made
            by_slot, low, faces, pair, cross = call(
                next_kernel,
                received
                + (narrow, slot_narrow, narrow_star, weights, tips, send_hot, coarse_sent),
                [floats(NQ * NB, LANES), floats(VPAD, NARROW), floats(OWN, NARROW)]
                + sent_shapes[1:],
                [],
                scalars=1,
            )
            known = (state, by_slot, slot_hot, low, faces, coarse_low, coarse_faces)
    (result,) = call(
        last_kernel, received + (state, slot_hot), [floats(NQ, NB, LANES)], [], scalars=1
    )
    return result.transpose(1, 0, 2)


def solution(mesh):
    split = P(None, None, "dom")
    face = P(None, None, None, "dom")
    row = P(None, "dom")
    in_specs = (split, face, face, face, P("dom"), row, row, row, row, P(), P(), P(), P(), P())
    return jax.shard_map(local, mesh=mesh, in_specs=in_specs, out_specs=split, check_vma=False)
```

```python
import functools
import math

import jax
import jax.numpy as jnp
from jax import lax
from jax.experimental import pallas as pl
from jax.experimental.pallas import tpu as pltpu
from jax.sharding import PartitionSpec as P

ORDER = 6
SUBSTEPS = 4
NQ = 9
NB = 56
NLOW = 35
NF = 21
PEERS = 4
SLOTS = 12
LANES = 128
FPAD = 24
VPAD = 40
BOTH = 2 * SLOTS
WIDTH = 256
COLS = NQ * LANES
FACES = 4 * LANES
REM = 12 * FPAD
SLOT_PAD = 32
SLOT_REM = 12 * SLOT_PAD
OWN = 4 * FPAD
DEEP = REM + OWN + 3 * VPAD
DEEP_PAD = 512
LEVELS = [(0, 35, 40, 128), (128, 20, 24, 80), (208, 10, 16, 48), (256, 4, 8, 32), (288, 1, 8, 32)]
BACK = 320
CHAIN_ROWS = BACK + OWN
DEPTH_3 = 10
TIP_ROWS = 24 + OWN
TAIL = 96
PART = 64
TWOS = 5
NARROW = TWOS * LANES
STAR_ROWS = 40
HIGH = lax.Precision.HIGH
HIGHEST = lax.Precision.HIGHEST
F32 = jnp.float32
BF16 = jnp.bfloat16


def taylor_weights(start, stop):
    return [
        (stop ** (depth + 1) - start ** (depth + 1)) / math.factorial(depth + 1)
        for depth in range(ORDER)
    ]


def lanes(index):
    return slice(index * LANES, (index + 1) * LANES)


def iota(shape, dim):
    return lax.broadcasted_iota(jnp.int32, shape, dim)


def halves(value):
    top = value.astype(BF16)
    return top, (value - top.astype(F32)).astype(BF16)


def pick(value, hot):
    return jnp.dot(
        jnp.concatenate(halves(value), axis=1),
        jnp.concatenate([hot, hot], axis=0),
        preferred_element_type=F32,
    )


def pick_rows(hot, value):
    return lax.dot_general(
        jnp.concatenate([hot, hot], axis=1),
        jnp.concatenate(halves(value), axis=1),
        (((1,), (1,)), ((), ())),
        preferred_element_type=F32,
    )


def pick_across(value, hot):
    return lax.dot_general(
        jnp.concatenate(halves(value), axis=1),
        jnp.concatenate([hot, hot], axis=1),
        (((1,), (1,)), ((), ())),
        preferred_element_type=F32,
    )


def gather_exact(value, hot):
    top, rest = halves(value)
    middle, low = halves(value - top.astype(F32))
    return lax.dot_general(
        jnp.concatenate([top, middle, low], axis=1),
        jnp.concatenate([hot, hot, hot], axis=1),
        (((1,), (1,)), ((), ())),
        preferred_element_type=F32,
    )


def first_half(rows):
    return iota((rows, LANES), 1) < PART


def paired(blocks):
    rows = blocks[0].shape[0]
    blocks = list(blocks) + [jnp.zeros_like(blocks[0])]
    return jnp.concatenate(
        [jnp.where(first_half(rows), blocks[2 * t], blocks[2 * t + 1]) for t in range(TWOS)],
        axis=1,
    )


def place_of(q):
    return LANES * (q % 2) + FPAD * (q // 2)


def stacked(value):
    top = value.astype(BF16).astype(F32)
    rest = value - top
    fill = PART - value.shape[0]
    gap = [jnp.zeros((fill, value.shape[1]), F32)] if fill else []
    return jnp.concatenate([top] + gap + [rest] + gap + [top] + gap, axis=0).astype(BF16)


def products(blocks, row_of, count=NQ):
    totals = [None] * NQ
    for q in range(count):
        for position, block in enumerate(blocks):
            left = block(q)
            for p in range(NQ):
                term = left * row_of(position, q, p)
                totals[p] = term if totals[p] is None else totals[p] + term
    return totals


def chain_weights(stiff_time, face_back, out, tips, raw):
    raw[...] = jnp.zeros(raw.shape, F32)
    for start, valid, padded, _ in LEVELS:
        for d in range(3):
            raw[start + d * padded : start + d * padded + valid, 0:NB] = stiff_time[d, 0:valid, :]
    for j in range(4):
        raw[BACK + j * FPAD : BACK + j * FPAD + NF, 0:NB] = face_back[:, j, :]
    once = raw[...]
    top = once.astype(BF16).astype(F32)
    out[:, 0:LANES] = (top + pltpu.roll(top, PART, 1)).astype(BF16)
    out[:, LANES : 2 * LANES] = (once - top).astype(BF16)
    start = LEVELS[-1][0]
    turned = jnp.transpose(once[start : start + LANES])
    for d in range(3):
        column = turned[0:8, 8 * d : 8 * d + 1]
        tips[8 * d : 8 * d + 8, :] = jnp.broadcast_to(column, (8, LANES))
    tips[24 : 24 + OWN, :] = jnp.broadcast_to(once[BACK : BACK + OWN, 0:1], (OWN, LANES))
    start = LEVELS[3][0]
    for b in range(DEPTH_3):
        column = jnp.broadcast_to(once[start : start + 24, b : b + 1], (24, LANES))
        tips[TIP_ROWS + 24 * b : TIP_ROWS + 24 * (b + 1), :] = column


def weigh(weights, start, rows, value):
    return jnp.dot(
        weights[start : start + rows, 0 : 3 * PART], stacked(value), preferred_element_type=F32
    )


def wide_sums(block, star):
    blocks = [functools.partial(block, d) for d in range(3)]
    return products(blocks, lambda d, q, p: star[q, p, d : d + 1, :])


def narrow_sums(block, star):
    return products(
        [functools.partial(block, d) for d in range(3)],
        lambda d, t, p: star[STAR_ROWS * t + 4 * p + d : STAR_ROWS * t + 4 * p + d + 1, :],
        TWOS,
    )


def narrow_join(totals):
    half = first_half(totals[0].shape[0])
    totals = list(totals) + [jnp.zeros_like(totals[0])]
    pieces = []
    for t in range(TWOS):
        even, odd = totals[2 * t], totals[2 * t + 1]
        crossed = pltpu.roll(jnp.where(half, odd, even), PART, 1)
        pieces.append(jnp.where(half, even, odd) + crossed)
    return jnp.concatenate(pieces, axis=1)


def wide_join(totals):
    return jnp.concatenate(totals, axis=1)


def by_rows(value, tips):
    columns = []
    for c in range(value.shape[1] // LANES):
        total = None
        for b in range(DEPTH_3):
            column = tips[TIP_ROWS + 24 * b : TIP_ROWS + 24 * (b + 1), :]
            term = column * value[b : b + 1, lanes(c)]
            total = term if total is None else total + term
        columns.append(total)
    return jnp.concatenate(columns, axis=1)


def chain_of(first, star, weights, tips, sums, join):
    now = first
    chain = [first]
    for level, (start, _, padded, rows) in enumerate(LEVELS[:-1]):
        if level == 3 and sums is narrow_sums:
            found = by_rows(now, tips)
        else:
            found = weigh(weights, start, rows, now)
        now = join(
            sums(lambda d, c: found[d * padded : (d + 1) * padded, lanes(c)], star)
        )
        chain.append(now)
    totals = sums(lambda d, c: now[:, lanes(c)] * tips[8 * d : 8 * d + 8, :], star)
    return chain, join([jnp.sum(total, axis=0, keepdims=True) for total in totals])


def with_end(integral, faces, end, tips):
    row = jnp.where(iota((8, end.shape[1]), 0) == 0, end, 0.0)
    low = jnp.concatenate([integral[0:8] + row, integral[8:VPAD]], axis=0)
    column = tips[24 : 24 + OWN, :]
    count = end.shape[1] // LANES
    faces = [faces[:, lanes(c)] + column * end[:, lanes(c)] for c in range(count)]
    return low, jnp.concatenate(faces, axis=1)


def integral_of(chain, weights):
    pieces = []
    edges = [0, 8, 16, 24, 40, 56]
    for low, high in zip(edges[:-1], edges[1:]):
        total = None
        for depth in range(len(chain)):
            if chain[depth].shape[0] < high:
                continue
            term = (weights[depth] * (-1) ** depth) * chain[depth][low:high]
            total = term if total is None else total + term
        pieces.append(total)
    return jnp.concatenate(pieces, axis=0)


def face_table(faces):
    def block(q):
        return jnp.concatenate(
            [faces[j * FPAD : (j + 1) * FPAD, lanes(q)] for j in range(4)], axis=1
        )

    even = [block(q) for q in range(0, NQ, 2)]
    odd = [block(q) for q in range(1, NQ, 2)]
    return jnp.concatenate(
        even
        + [jnp.zeros((LANES - len(even) * FPAD, FACES), F32)]
        + odd
        + [jnp.zeros((LANES - len(odd) * FPAD, FACES), F32)],
        axis=0,
    )


def narrow_table(faces):
    rows = [
        jnp.concatenate([faces[j * FPAD : (j + 1) * FPAD, lanes(t)] for j in range(4)], axis=1)
        for t in range(TWOS)
    ]
    return jnp.concatenate(rows + [jnp.zeros((LANES - TWOS * FPAD, FACES), F32)], axis=0)


def list_rows():
    row = iota((PEERS * BOTH, LANES), 0)
    peer = (row >= BOTH).astype(jnp.int32) + (row >= 2 * BOTH).astype(jnp.int32)
    peer = peer + (row >= 3 * BOTH).astype(jnp.int32)
    return peer, row - BOTH * peer


def list_hot(lists, face):
    return lists[...] == iota((PEERS * BOTH, LANES), 1) + LANES * face


def deliver(sent, position, pair_out, cross_out):
    odd = lax.rem(position, 2) == 1
    first, second = sent[0:BOTH], sent[BOTH : 2 * BOTH]
    pair_out[0:BOTH, :] = jnp.where(odd, second, first)
    pair_out[BOTH : 3 * BOTH, :] = sent[2 * BOTH : 4 * BOTH]
    cross_out[...] = jnp.where(odd, first, second)


def list_column(fine, coarse):
    peer, inner = list_rows()
    total = jnp.zeros((PEERS * BOTH, LANES), F32)
    for kind, entries in enumerate((fine, coarse)):
        here = iota((PEERS * BOTH, LANES), 1) == inner - kind * SLOTS
        for k in range(PEERS):
            total = total + jnp.where(here & (peer == k), entries[k : k + 1, :], 0.0)
    column = jnp.sum(total, axis=1, keepdims=True)
    return jnp.broadcast_to(column, (PEERS * BOTH, LANES)).astype(jnp.int32)


def first_kernel(
    place, dofs, star, stiff_time, face_back, fine_send, coarse_send, labels, *rest
):
    later = rest[:7]
    (
        state_out, low_out, tail_out, faces_out, pair_out, cross_out,
        weights_out, tips_out, star_out, labels_out, lists_out,
    ) = rest[7:18]
    later_out = rest[18:25]
    raw, dofs_here, time_here, back_here, wide, fine_here, coarse_here, ready = rest[25:]
    position = place[0]
    moves = [
        (dofs, dofs_here),
        (stiff_time, time_here),
        (face_back, back_here),
        (star, star_out),
        (fine_send, fine_here),
        (coarse_send, coarse_here),
        (labels, labels_out),
    ]
    first = len(moves)
    moves += list(zip(later, later_out))
    copies = [
        pltpu.make_async_copy(source, target, ready.at[number])
        for number, (source, target) in enumerate(moves)
    ]
    for copy in copies:
        copy.start()
    for copy in copies[1:3]:
        copy.wait()
    chain_weights(time_here, back_here, weights_out, tips_out, raw)
    copies[0].wait()
    state = jnp.concatenate([dofs_here[q] for q in range(NQ)], axis=1)
    state_out[...] = state
    copies[3].wait()
    chain, end = chain_of(state, star_out, weights_out, tips_out, wide_sums, wide_join)
    first_weights = taylor_weights(0.0, 1.0 / SUBSTEPS)
    integral = integral_of(chain, first_weights)
    for copy in copies[4:first]:
        copy.wait()
    wide[...] = jnp.zeros(wide.shape, F32)
    wide[0:PEERS, 0:SLOTS] = fine_here[...].astype(F32)
    wide[8 : 8 + PEERS, 0:SLOTS] = coarse_here[...].astype(F32)
    lists_out[...] = list_column(wide[0:PEERS], wide[8 : 8 + PEERS])
    faces = weigh(weights_out, BACK, OWN, integral)
    low, faces = with_end(integral, faces, -first_weights[-1] * end, tips_out)
    low_out[...] = low
    faces_out[...] = faces
    hot = jnp.concatenate(
        [jnp.where(list_hot(lists_out, j), 1.0, 0.0) for j in range(4)], axis=1
    ).astype(BF16)
    deliver(pick_rows(hot, face_table(faces)), position, pair_out, cross_out)
    end = jnp.where(iota((8, COLS), 0) == 0, end, 0.0)
    tail_out[...] = jnp.concatenate(chain[1:] + [end], axis=0)
    for copy in copies[first:]:
        copy.wait()


def prepare_kernel(
    state, tail, source, orientation, flux_other, face_front, face_turn, stiff_vol,
    star, labels, lists,
    coarse_out, slot_flux_out, slot_code_out, slot_hot_out, lift_out, slot_lift_out,
    narrow_hot_out, slot_narrow_out, star_out, send_out,
    table, fronts, tall, slot_tall, flat,
):
    fine = labels[...] == 1
    before = (iota((LANES, LANES), 0) < iota((LANES, LANES), 1)).astype(F32).astype(BF16)
    marks = jnp.broadcast_to(jnp.where(fine, 1.0, 0.0), (16, LANES)).astype(BF16)
    rank = jnp.dot(marks, before, preferred_element_type=F32)[0:1].astype(jnp.int32)
    rank = jnp.where(fine, rank, -1)
    lane = iota((LANES, LANES), 0)
    lane = jnp.where(lane >= PART, lane - PART, lane)
    narrow_hot = jnp.where(rank == lane, 1.0, 0.0).astype(BF16)
    narrow_hot_out[...] = narrow_hot
    flat[...] = jnp.zeros(flat.shape, F32)
    for q in range(NQ):
        for p in range(NQ):
            start = STAR_ROWS * q + 4 * p
            flat[start : start + 3, :] = star[q, p]
    gathered = gather_exact(flat[...], narrow_hot)
    stars = [gathered[STAR_ROWS * q : STAR_ROWS * (q + 1)] for q in range(NQ)]
    packed = paired(stars)
    for t in range(TWOS):
        star_out[STAR_ROWS * t : STAR_ROWS * (t + 1), :] = packed[:, lanes(t)]
    _, inner = list_rows()
    half = first_half(PEERS * BOTH)
    across = (((1,), (1,)), ((), ()))
    for j in range(4):
        chosen = jnp.where(list_hot(lists, j) & (inner < SLOTS), 1.0, 0.0).astype(BF16)
        found = lax.dot_general(chosen, narrow_hot, across, preferred_element_type=F32)
        send_out[0 : PEERS * BOTH, lanes(j)] = jnp.where(half, found, 0.0).astype(BF16)
        send_out[PEERS * BOTH :, lanes(j)] = jnp.where(half, 0.0, found).astype(BF16)
    chain = [state[...]]
    start = 0
    for _, _, padded, _ in LEVELS:
        chain.append(tail[start : start + padded, :])
        start += padded
    for step in range(1, SUBSTEPS):
        coarse_out[step - 1] = integral_of(
            chain, taylor_weights(step / SUBSTEPS, (step + 1) / SUBSTEPS)
        )
    row = iota((LANES, LANES), 0)
    peer = (row >= BOTH).astype(jnp.int32) + (row >= 2 * BOTH).astype(jnp.int32)
    peer = peer + (row >= 3 * BOTH).astype(jnp.int32)
    inner = row - BOTH * peer
    kind = (inner >= SLOTS).astype(jnp.int32)
    wanted = kind * (PEERS * SLOTS - SLOTS) + peer * SLOTS + inner + FACES
    wanted = jnp.where(row < PEERS * BOTH, wanted, -1)
    blocks = [jnp.where(source[i : i + 1, :] == wanted, 1.0, 0.0) for i in range(4)]
    slot_hot = (blocks[0] + blocks[1] + blocks[2] + blocks[3]).astype(BF16)
    slot_hot_out[...] = slot_hot
    slot_narrow_out[...] = lax.dot_general(
        slot_hot, narrow_hot, across, preferred_element_type=F32
    ).astype(BF16)
    hot = jnp.concatenate(blocks, axis=1).astype(BF16)
    codes = jnp.concatenate(
        [
            jnp.where(iota((16, LANES), 0) - 3 * i == orientation[i : i + 1, :], 1.0, 0.0)
            for i in range(4)
        ],
        axis=1,
    ).astype(BF16)
    dims = (((1,), (1,)), ((), ()))
    found = lax.dot_general(codes, hot, dims, preferred_element_type=F32)
    for code in range(12):
        slot_code_out[SLOT_PAD * code : SLOT_PAD * (code + 1), :] = jnp.broadcast_to(
            found[code : code + 1], (SLOT_PAD, LANES)
        ).astype(BF16)
    table[...] = jnp.zeros(table.shape, F32)
    for i in range(4):
        for q in range(NQ):
            table[16 * q : 16 * q + NQ, lanes(i)] = flux_other[q, :, i, :]
    slot_flux_out[...] = pick_across(table[...], hot)

    fronts[...] = jnp.zeros(fronts.shape, F32)
    tall[...] = jnp.zeros(tall.shape, F32)
    slot_tall[...] = jnp.zeros(slot_tall.shape, F32)
    for i in range(4):
        fronts[0:NF, i * LANES : i * LANES + NB] = face_front[:, i, :]
    for code in range(3):
        turned = lax.dot_general(
            face_turn[code], fronts[0:NF, :], (((0,), (0,)), ((), ())),
            precision=HIGHEST, preferred_element_type=F32,
        )
        for i in range(4):
            start = FPAD * (3 * i + code)
            tall[start : start + NF, :] = -turned[:, lanes(i)]
            start = SLOT_PAD * (3 * i + code)
            slot_tall[start : start + NF, :] = -turned[:, lanes(i)]
    for i in range(4):
        start = REM + FPAD * i
        tall[start : start + NF, :] = -fronts[0:NF, lanes(i)]
    for d in range(3):
        start = REM + OWN + VPAD * d
        tall[start : start + NLOW, 0:NB] = stiff_vol[d]
    lift_out[...] = jnp.transpose(tall[...])[0:NB]
    whole = jnp.transpose(slot_tall[...])[0:PART]
    top = whole.astype(BF16)
    slot_lift_out[0:PART, 0:SLOT_REM] = top
    slot_lift_out[0:PART, SLOT_REM:] = top
    slot_lift_out[PART:, 0:SLOT_REM] = (whole - top.astype(F32)).astype(BF16)
    slot_lift_out[PART:, SLOT_REM:] = jnp.zeros((PART, SLOT_REM), BF16)


def local_kernel(*refs, step):
    if step == 0:
        state, low, faces, *rest = refs
        state, low, faces = state[...], low[...], faces[...]
    else:
        state, by_slot, slot_hot, low, faces, coarse_faces, *rest = refs
    star, flux_self, flux_other, source, orientation, lift, *rest = rest
    coarse, weights, lists, narrow_hot, labels, *rest = rest
    out, *rest = rest
    if step > 0:
        state = state[...] + by_elements(by_slot[...], slot_hot[...])
        back = jnp.transpose(narrow_hot[...].astype(F32))
        half = iota((LANES, LANES), 1) < PART
        spread = jnp.concatenate(
            [
                jnp.transpose(jnp.where(half, back, 0.0)),
                jnp.transpose(jnp.where(half, 0.0, back)),
            ],
            axis=1,
        ).astype(BF16)
        both = VPAD + OWN
        rows = [
            part[:, lanes(t)] for t in range(TWOS) for part in (low, faces)
        ]
        wide = pick(jnp.concatenate(rows, axis=0), spread)
        wide = [wide[both * t : both * (t + 1)] for t in range(TWOS)]
        wide = jnp.concatenate(wide, axis=1)[:, 0:COLS]
        fine = labels[...] == 1
        fine = jnp.concatenate([fine] * NQ, axis=1)
        low = jnp.where(fine, wide[0:VPAD], coarse[step - 1, 0:VPAD, :])
        faces = jnp.where(fine, wide[VPAD:both], coarse_faces[...])
    if step + 1 < SUBSTEPS:
        narrow_out, next_faces_out, next_sent_out, stack = rest
        next_faces = weigh(weights, BACK, OWN, coarse[step])
        next_faces_out[...] = next_faces
        _, inner = list_rows()
        hot = jnp.concatenate(
            [jnp.where(list_hot(lists, j) & (inner >= SLOTS), 1.0, 0.0) for j in range(4)],
            axis=1,
        ).astype(BF16)
        next_sent_out[...] = pick_rows(hot, face_table(next_faces))
    else:
        (stack,) = rest
    column = iota((FACES, LANES), 0)
    hot = jnp.concatenate(
        [
            jnp.where(column == source[i : i + 1, :], 1.0, 0.0).astype(BF16)
            for i in range(4)
        ],
        axis=1,
    )
    found = pick(face_table(faces), hot)
    for d in range(3):
        totals = products(
            [lambda q: low[:, lanes(q)]], lambda _, q, p: star[q, p, d : d + 1, :]
        )
        base = REM + OWN + VPAD * d
        for p in range(NQ):
            stack[base : base + VPAD, lanes(p)] = totals[p]
    for i in range(4):
        totals = products(
            [lambda q: faces[i * FPAD : (i + 1) * FPAD, lanes(q)]],
            lambda _, q, p: flux_self[q, p, i : i + 1, :],
        )
        for p in range(NQ):
            stack[REM + FPAD * i : REM + FPAD * (i + 1), lanes(p)] = totals[p]
    for i in range(4):
        totals = products(
            [lambda q: found[place_of(q) : place_of(q) + FPAD, lanes(i)]],
            lambda _, q, p: flux_other[q, p, i : i + 1, :],
        )
        for code in range(3):
            mask = jnp.where(orientation[i : i + 1, :] == code, 1.0, 0.0)
            base = FPAD * (3 * i + code)
            for p in range(NQ):
                stack[base : base + FPAD, lanes(p)] = totals[p] * mask
    total = state + jnp.dot(
        lift[:, 0:DEEP], stack[...], precision=HIGH, preferred_element_type=F32
    )
    out[...] = total
    if step + 1 < SUBSTEPS:
        tall = jnp.concatenate([total[:, lanes(q)] for q in range(NQ)], axis=0)
        found = pick_across(tall, narrow_hot[...])
        narrow_out[...] = paired([found[NB * q : NB * (q + 1)] for q in range(NQ)])


def by_elements(by_slot, slot_hot):
    found = pick(by_slot, slot_hot)
    return jnp.concatenate([found[NB * p : NB * (p + 1)] for p in range(NQ)], axis=1)


def remote_part(position, near, upper, lower, slot_flux, slot_code, lift):
    odd = lax.rem(position, 2) == 1
    behind_up = lax.rem(position, 4) < 2
    up, down = upper[...], lower[...]
    behind = jnp.where(behind_up, up, down)
    ahead = jnp.where(behind_up, down, up)
    here = jnp.where(odd, near[0:BOTH, :], near[3 * BOTH : 4 * BOTH, :])
    rows = jnp.concatenate(
        [
            jnp.where(odd, here, behind[0:BOTH]),
            jnp.where(odd, ahead[0:BOTH], here),
            behind[BOTH : 2 * BOTH],
            ahead[BOTH : 2 * BOTH],
            jnp.zeros((LANES - PEERS * BOTH, WIDTH), F32),
        ],
        axis=0,
    )
    received = jnp.transpose(rows)
    totals = products(
        [lambda q: received[place_of(q) : place_of(q) + FPAD]],
        lambda _, q, p: slot_flux[16 * q + p : 16 * q + p + 1, :],
    )
    codes = [slot_code[SLOT_PAD * code : SLOT_PAD * (code + 1), :] for code in range(12)]
    gap = jnp.zeros((SLOT_PAD - FPAD, LANES), F32)
    columns = []
    for p in range(NQ):
        both = halves(jnp.concatenate([totals[p], gap], axis=0))
        masked = [part * mask for part in both for mask in codes]
        columns.append(jnp.concatenate(masked, axis=0))
    masked = jnp.concatenate(columns, axis=1)
    lifted = jnp.dot(lift[...], masked, preferred_element_type=F32)
    lifted = lifted[0:NB] + lifted[PART : PART + NB]
    return jnp.concatenate([lifted[:, lanes(p)] for p in range(NQ)], axis=0)


def next_kernel(
    place, near, upper, lower, slot_flux, slot_code, lift,
    narrow, slot_narrow, star, weights, tips, send_hot, coarse_sent,
    by_slot_out, low_out, faces_out, pair_out, cross_out,
):
    position = place[0]
    by_slot = remote_part(position, near, upper, lower, slot_flux, slot_code, lift)
    by_slot_out[...] = by_slot
    found = pick(by_slot, slot_narrow[...])
    now = narrow[...] + paired([found[NB * p : NB * (p + 1)] for p in range(NQ)])
    chain, end = chain_of(now, star, weights, tips, narrow_sums, narrow_join)
    first_weights = taylor_weights(0.0, 1.0 / SUBSTEPS)
    integral = integral_of(chain, first_weights)
    faces = weigh(weights, BACK, OWN, integral)
    low, faces = with_end(integral, faces, -first_weights[-1] * end, tips)
    low_out[...] = low
    faces_out[...] = faces
    found = pick_rows(send_hot[...], narrow_table(faces))
    rows = PEERS * BOTH
    sent = jnp.concatenate([found[0:rows], found[rows : 2 * rows]], axis=1) + coarse_sent[...]
    deliver(sent, position, pair_out, cross_out)


def last_kernel(
    place, near, upper, lower, slot_flux, slot_code, lift, state, slot_hot, out
):
    by_slot = remote_part(place[0], near, upper, lower, slot_flux, slot_code, lift)
    total = state[...] + by_elements(by_slot, slot_hot[...])
    for q in range(NQ):
        out[q] = total[:, lanes(q)]


def floats(*shape):
    return jax.ShapeDtypeStruct(shape, F32)


def call(kernel, args, outs, scratch, scalars=0, inside=False, flops=2.0e7):
    smem = pl.BlockSpec(memory_space=pltpu.SMEM)
    vmem = pl.BlockSpec(memory_space=pltpu.VMEM)
    given = pl.BlockSpec(memory_space=pl.ANY) if inside else vmem
    if inside:
        args = args[:scalars] + tuple(
            pltpu.with_memory_space_constraint(item, pltpu.HBM) for item in args[scalars:]
        )
    moved = 4 * sum(math.prod(item.shape) for item in list(args) + list(outs))
    return pl.pallas_call(
        kernel,
        in_specs=[smem] * scalars + [given] * (len(args) - scalars),
        out_specs=[vmem] * len(outs),
        out_shape=outs,
        scratch_shapes=[
            pltpu.VMEM(item, F32) if isinstance(item, tuple) else item for item in scratch
        ],
        compiler_params=pltpu.CompilerParams(vmem_limit_bytes=40 * 2**20),
        cost_estimate=pl.CostEstimate(flops=int(flops), bytes_accessed=moved, transcendentals=0),
    )(*args)


def swaps(count, first):
    pairs = []
    for low in range(2 * first, count - 2, 4):
        for one, other in ((low, low + 3), (low + 1, low + 2)):
            pairs += [(one, other), (other, one)]
    return pairs


def local(
    dofs, star, flux_self, flux_other, labels, neighbour_source, orientation,
    fine_send, coarse_send, stiff_time, stiff_vol, face_back, face_front, face_turn,
):
    count = lax.axis_size("dom")
    pairs = [[low, low + 1] for low in range(0, count, 2)]
    place = lax.axis_index("dom").astype(jnp.int32)
    partner = jnp.where(place % 2 == 1, BOTH, 4 * BOTH)
    upper_from = partner + jnp.where(place % 4 >= 2, 0, BOTH)
    lower_from = partner + jnp.where(place % 4 >= 2, BOTH, 0)
    place = place.reshape(1)
    labels = labels.reshape(1, LANES)
    later = (
        flux_self.transpose(1, 2, 0, 3),
        flux_other.transpose(1, 2, 0, 3),
        neighbour_source,
        orientation,
        face_front.transpose(2, 0, 1),
        face_turn,
        stiff_vol.transpose(0, 2, 1),
    )
    star = star.transpose(1, 2, 0, 3)
    back = face_back.transpose(1, 0, 2)
    message = floats(BOTH, WIDTH)
    sent_shapes = [floats(OWN, COLS), floats(3 * BOTH, WIDTH), message]
    like = lambda item: jax.ShapeDtypeStruct(item.shape, item.dtype)
    found = call(
        first_kernel,
        (place, dofs.transpose(1, 0, 2), star, stiff_time, back, fine_send, coarse_send, labels)
        + later,
        [floats(NB, COLS), floats(VPAD, COLS), floats(TAIL, COLS)]
        + sent_shapes
        + [jax.ShapeDtypeStruct((CHAIN_ROWS, 2 * LANES), BF16)]
        + [floats(TIP_ROWS + 24 * DEPTH_3, LANES), like(star), like(labels)]
        + [jax.ShapeDtypeStruct((PEERS * BOTH, LANES), jnp.int32)]
        + [like(item) for item in later],
        [(CHAIN_ROWS, LANES), (NQ, NB, LANES), stiff_time.shape, back.shape, (16, LANES)]
        + [pltpu.VMEM(item.shape, jnp.int32) for item in (fine_send, coarse_send)]
        + [pltpu.SemaphoreType.DMA((7 + len(later),))],
        scalars=1,
        inside=True,
    )
    state, low, tail, faces, pair, cross, weights, tips, star, labels, lists = found[:11]
    flux_self, flux_other, source, orientation, front, turn, vol = found[11:]
    halved = lambda *shape: jax.ShapeDtypeStruct(shape, BF16)
    prepared = call(
        prepare_kernel,
        (state, tail, source, orientation, flux_other, front, turn, vol, star, labels, lists),
        [
            floats(SUBSTEPS - 1, NB, COLS), floats(16 * NQ, LANES), halved(SLOT_REM, LANES),
            halved(LANES, LANES), floats(NB, DEEP_PAD), halved(2 * PART, 2 * SLOT_REM),
            halved(LANES, LANES), halved(LANES, LANES), floats(TWOS * STAR_ROWS, LANES),
            halved(2 * PEERS * BOTH, FACES),
        ],
        [
            (16 * NQ, FACES), (FPAD, FACES), (DEEP_PAD, LANES), (SLOT_REM, LANES),
            (NQ * STAR_ROWS, LANES),
        ],
    )
    coarse, slot_flux, slot_code, slot_hot, lift, slot_lift = prepared[:6]
    narrow_hot, slot_narrow, narrow_star, send_hot = prepared[6:]
    fixed = (star, flux_self, flux_other, source, orientation, lift)
    fixed += (coarse, weights, lists, narrow_hot, labels)
    known = (state, low, faces)
    for step in range(SUBSTEPS):
        near = lax.all_gather(pair, "dom", axis_index_groups=pairs, tiled=True)
        passed = lax.dynamic_slice(near, (lower_from, 0), (BOTH, WIDTH))
        lower = jnp.concatenate([cross, passed], axis=0)
        lower, cross, shared = lax.optimization_barrier((lower, cross, near))
        passed = lax.dynamic_slice(shared, (upper_from, 0), (BOTH, WIDTH))
        upper = jnp.concatenate([cross, passed], axis=0)
        upper = lax.ppermute(upper, "dom", swaps(count, 1))
        lower = lax.ppermute(lower, "dom", swaps(count, 0))
        ahead = [floats(NB, NARROW), floats(OWN, COLS), floats(PEERS * BOTH, WIDTH)]
        state, *made = call(
            functools.partial(local_kernel, step=step),
            known + fixed,
            [floats(NB, COLS)] + (ahead if step + 1 < SUBSTEPS else []),
            [(DEEP, COLS)],
        )
        received = (place, near, upper, lower, slot_flux, slot_code, slot_lift)
        if step + 1 < SUBSTEPS:
            narrow, coarse_faces, coarse_sent = made
            by_slot, low, faces, pair, cross = call(
                next_kernel,
                received
                + (narrow, slot_narrow, narrow_star, weights, tips, send_hot, coarse_sent),
                [floats(NQ * NB, LANES), floats(VPAD, NARROW), floats(OWN, NARROW)]
                + sent_shapes[1:],
                [],
                scalars=1,
            )
            known = (state, by_slot, slot_hot, low, faces, coarse_faces)
    (result,) = call(
        last_kernel, received + (state, slot_hot), [floats(NQ, NB, LANES)], [], scalars=1
    )
    return result.transpose(1, 0, 2)


def solution(mesh):
    split = P(None, None, "dom")
    face = P(None, None, None, "dom")
    row = P(None, "dom")
    in_specs = (split, face, face, face, P("dom"), row, row, row, row, P(), P(), P(), P(), P())
    return jax.shard_map(local, mesh=mesh, in_specs=in_specs, out_specs=split, check_vma=False)
```

```python
import functools
import math

import jax
import jax.numpy as jnp
from jax import lax
from jax.experimental import pallas as pl
from jax.experimental.pallas import tpu as pltpu
from jax.sharding import PartitionSpec as P

ORDER = 6
SUBSTEPS = 4
NQ = 9
NB = 56
NLOW = 35
NF = 21
PEERS = 4
SLOTS = 12
LANES = 128
FPAD = 24
VPAD = 40
BOTH = 2 * SLOTS
WIDTH = 256
COLS = NQ * LANES
FACES = 4 * LANES
REM = 12 * FPAD
SLOT_PAD = 32
SLOT_REM = 12 * SLOT_PAD
OWN = 4 * FPAD
DEEP = REM + OWN + 3 * VPAD
DEEP_PAD = 512
LEVELS = [(0, 35, 40, 128), (128, 20, 24, 80), (208, 10, 16, 48), (256, 4, 8, 32), (288, 1, 8, 32)]
BACK = 320
CHAIN_ROWS = BACK + OWN
DEPTH_3 = 10
TIP_ROWS = 24 + OWN
TAIL = 96
PART = 64
TWOS = 5
NARROW = TWOS * LANES
STAR_ROWS = 40
HIGH = lax.Precision.HIGH
HIGHEST = lax.Precision.HIGHEST
F32 = jnp.float32
BF16 = jnp.bfloat16


def taylor_weights(start, stop):
    return [
        (stop ** (depth + 1) - start ** (depth + 1)) / math.factorial(depth + 1)
        for depth in range(ORDER)
    ]


def lanes(index):
    return slice(index * LANES, (index + 1) * LANES)


def iota(shape, dim):
    return lax.broadcasted_iota(jnp.int32, shape, dim)


def halves(value):
    top = value.astype(BF16)
    return top, (value - top.astype(F32)).astype(BF16)


def pick(value, hot):
    return jnp.dot(
        jnp.concatenate(halves(value), axis=1),
        jnp.concatenate([hot, hot], axis=0),
        preferred_element_type=F32,
    )


def pick_rows(hot, value):
    return lax.dot_general(
        jnp.concatenate([hot, hot], axis=1),
        jnp.concatenate(halves(value), axis=1),
        (((1,), (1,)), ((), ())),
        preferred_element_type=F32,
    )


def pick_across(value, hot):
    return lax.dot_general(
        jnp.concatenate(halves(value), axis=1),
        jnp.concatenate([hot, hot], axis=1),
        (((1,), (1,)), ((), ())),
        preferred_element_type=F32,
    )


def gather_exact(value, hot):
    top, rest = halves(value)
    middle, low = halves(value - top.astype(F32))
    return lax.dot_general(
        jnp.concatenate([top, middle, low], axis=1),
        jnp.concatenate([hot, hot, hot], axis=1),
        (((1,), (1,)), ((), ())),
        preferred_element_type=F32,
    )


def first_half(rows):
    return iota((rows, LANES), 1) < PART


def paired(blocks):
    rows = blocks[0].shape[0]
    blocks = list(blocks) + [jnp.zeros_like(blocks[0])]
    return jnp.concatenate(
        [jnp.where(first_half(rows), blocks[2 * t], blocks[2 * t + 1]) for t in range(TWOS)],
        axis=1,
    )


def place_of(q):
    return LANES * (q % 2) + FPAD * (q // 2)


def stacked(value):
    top = value.astype(BF16).astype(F32)
    rest = value - top
    fill = PART - value.shape[0]
    gap = [jnp.zeros((fill, value.shape[1]), F32)] if fill else []
    return jnp.concatenate([top] + gap + [rest] + gap + [top] + gap, axis=0).astype(BF16)


def products(blocks, row_of, count=NQ):
    totals = [None] * NQ
    for q in range(count):
        for position, block in enumerate(blocks):
            left = block(q)
            for p in range(NQ):
                term = left * row_of(position, q, p)
                totals[p] = term if totals[p] is None else totals[p] + term
    return totals


def chain_weights(stiff_time, face_back, out, tips, raw):
    raw[...] = jnp.zeros(raw.shape, F32)
    for start, valid, padded, _ in LEVELS:
        for d in range(3):
            raw[start + d * padded : start + d * padded + valid, 0:NB] = stiff_time[d, 0:valid, :]
    for j in range(4):
        raw[BACK + j * FPAD : BACK + j * FPAD + NF, 0:NB] = face_back[:, j, :]
    once = raw[...]
    top = once.astype(BF16).astype(F32)
    out[:, 0:LANES] = (top + pltpu.roll(top, PART, 1)).astype(BF16)
    out[:, LANES : 2 * LANES] = (once - top).astype(BF16)
    start = LEVELS[-1][0]
    turned = jnp.transpose(once[start : start + LANES])
    for d in range(3):
        column = turned[0:8, 8 * d : 8 * d + 1]
        tips[8 * d : 8 * d + 8, :] = jnp.broadcast_to(column, (8, LANES))
    tips[24 : 24 + OWN, :] = jnp.broadcast_to(once[BACK : BACK + OWN, 0:1], (OWN, LANES))
    start = LEVELS[3][0]
    for b in range(DEPTH_3):
        column = jnp.broadcast_to(once[start : start + 24, b : b + 1], (24, LANES))
        tips[TIP_ROWS + 24 * b : TIP_ROWS + 24 * (b + 1), :] = column


def weigh(weights, start, rows, value):
    return jnp.dot(
        weights[start : start + rows, 0 : 3 * PART], stacked(value), preferred_element_type=F32
    )


def wide_sums(block, star):
    blocks = [functools.partial(block, d) for d in range(3)]
    return products(blocks, lambda d, q, p: star[q, p, d : d + 1, :])


def narrow_sums(block, star):
    return products(
        [functools.partial(block, d) for d in range(3)],
        lambda d, t, p: star[STAR_ROWS * t + 4 * p + d : STAR_ROWS * t + 4 * p + d + 1, :],
        TWOS,
    )


def narrow_join(totals):
    half = first_half(totals[0].shape[0])
    totals = list(totals) + [jnp.zeros_like(totals[0])]
    pieces = []
    for t in range(TWOS):
        even, odd = totals[2 * t], totals[2 * t + 1]
        crossed = pltpu.roll(jnp.where(half, odd, even), PART, 1)
        pieces.append(jnp.where(half, even, odd) + crossed)
    return jnp.concatenate(pieces, axis=1)


def wide_join(totals):
    return jnp.concatenate(totals, axis=1)


def by_rows(value, tips):
    columns = []
    for c in range(value.shape[1] // LANES):
        total = None
        for b in range(DEPTH_3):
            column = tips[TIP_ROWS + 24 * b : TIP_ROWS + 24 * (b + 1), :]
            term = column * value[b : b + 1, lanes(c)]
            total = term if total is None else total + term
        columns.append(total)
    return jnp.concatenate(columns, axis=1)


def chain_of(first, star, weights, tips, sums, join):
    now = first
    chain = [first]
    for level, (start, _, padded, rows) in enumerate(LEVELS[:-1]):
        if level == 3:
            found = by_rows(now, tips)
        else:
            found = weigh(weights, start, rows, now)
        now = join(
            sums(lambda d, c: found[d * padded : (d + 1) * padded, lanes(c)], star)
        )
        chain.append(now)
    totals = sums(lambda d, c: now[:, lanes(c)] * tips[8 * d : 8 * d + 8, :], star)
    return chain, join([jnp.sum(total, axis=0, keepdims=True) for total in totals])


def with_end(integral, faces, end, tips):
    row = jnp.where(iota((8, end.shape[1]), 0) == 0, end, 0.0)
    low = jnp.concatenate([integral[0:8] + row, integral[8:VPAD]], axis=0)
    column = tips[24 : 24 + OWN, :]
    count = end.shape[1] // LANES
    faces = [faces[:, lanes(c)] + column * end[:, lanes(c)] for c in range(count)]
    return low, jnp.concatenate(faces, axis=1)


def integral_of(chain, weights):
    pieces = []
    edges = [0, 8, 16, 24, 40, 56]
    for low, high in zip(edges[:-1], edges[1:]):
        total = None
        for depth in range(len(chain)):
            if chain[depth].shape[0] < high:
                continue
            term = (weights[depth] * (-1) ** depth) * chain[depth][low:high]
            total = term if total is None else total + term
        pieces.append(total)
    return jnp.concatenate(pieces, axis=0)


def face_table(faces):
    def block(q):
        return jnp.concatenate(
            [faces[j * FPAD : (j + 1) * FPAD, lanes(q)] for j in range(4)], axis=1
        )

    even = [block(q) for q in range(0, NQ, 2)]
    odd = [block(q) for q in range(1, NQ, 2)]
    return jnp.concatenate(
        even
        + [jnp.zeros((LANES - len(even) * FPAD, FACES), F32)]
        + odd
        + [jnp.zeros((LANES - len(odd) * FPAD, FACES), F32)],
        axis=0,
    )


def narrow_table(faces):
    rows = [
        jnp.concatenate([faces[j * FPAD : (j + 1) * FPAD, lanes(t)] for j in range(4)], axis=1)
        for t in range(TWOS)
    ]
    return jnp.concatenate(rows + [jnp.zeros((LANES - TWOS * FPAD, FACES), F32)], axis=0)


def list_rows():
    row = iota((PEERS * BOTH, LANES), 0)
    peer = (row >= BOTH).astype(jnp.int32) + (row >= 2 * BOTH).astype(jnp.int32)
    peer = peer + (row >= 3 * BOTH).astype(jnp.int32)
    return peer, row - BOTH * peer


def list_hot(lists, face):
    return lists[...] == iota((PEERS * BOTH, LANES), 1) + LANES * face


def deliver(sent, position, pair_out, cross_out):
    odd = lax.rem(position, 2) == 1
    first, second = sent[0:BOTH], sent[BOTH : 2 * BOTH]
    pair_out[0:BOTH, :] = jnp.where(odd, second, first)
    pair_out[BOTH : 3 * BOTH, :] = sent[2 * BOTH : 4 * BOTH]
    cross_out[...] = jnp.where(odd, first, second)


def list_column(fine, coarse):
    peer, inner = list_rows()
    total = jnp.zeros((PEERS * BOTH, LANES), F32)
    for kind, entries in enumerate((fine, coarse)):
        here = iota((PEERS * BOTH, LANES), 1) == inner - kind * SLOTS
        for k in range(PEERS):
            total = total + jnp.where(here & (peer == k), entries[k : k + 1, :], 0.0)
    column = jnp.sum(total, axis=1, keepdims=True)
    return jnp.broadcast_to(column, (PEERS * BOTH, LANES)).astype(jnp.int32)


def first_kernel(
    place, dofs, star, stiff_time, face_back, fine_send, coarse_send, labels, *rest
):
    later = rest[:7]
    (
        state_out, low_out, tail_out, faces_out, pair_out, cross_out,
        weights_out, tips_out, star_out, labels_out, lists_out,
    ) = rest[7:18]
    later_out = rest[18:25]
    raw, dofs_here, time_here, back_here, wide, fine_here, coarse_here, ready = rest[25:]
    position = place[0]
    moves = [
        (dofs, dofs_here),
        (stiff_time, time_here),
        (face_back, back_here),
        (star, star_out),
        (fine_send, fine_here),
        (coarse_send, coarse_here),
        (labels, labels_out),
    ]
    first = len(moves)
    moves += list(zip(later, later_out))
    copies = [
        pltpu.make_async_copy(source, target, ready.at[number])
        for number, (source, target) in enumerate(moves)
    ]
    for copy in copies:
        copy.start()
    for copy in copies[1:3]:
        copy.wait()
    chain_weights(time_here, back_here, weights_out, tips_out, raw)
    copies[0].wait()
    state = jnp.concatenate([dofs_here[q] for q in range(NQ)], axis=1)
    state_out[...] = state
    copies[3].wait()
    chain, end = chain_of(state, star_out, weights_out, tips_out, wide_sums, wide_join)
    first_weights = taylor_weights(0.0, 1.0 / SUBSTEPS)
    integral = integral_of(chain, first_weights)
    for copy in copies[4:first]:
        copy.wait()
    wide[...] = jnp.zeros(wide.shape, F32)
    wide[0:PEERS, 0:SLOTS] = fine_here[...].astype(F32)
    wide[8 : 8 + PEERS, 0:SLOTS] = coarse_here[...].astype(F32)
    lists_out[...] = list_column(wide[0:PEERS], wide[8 : 8 + PEERS])
    faces = weigh(weights_out, BACK, OWN, integral)
    low, faces = with_end(integral, faces, -first_weights[-1] * end, tips_out)
    low_out[...] = low
    faces_out[...] = faces
    hot = jnp.concatenate(
        [jnp.where(list_hot(lists_out, j), 1.0, 0.0) for j in range(4)], axis=1
    ).astype(BF16)
    deliver(pick_rows(hot, face_table(faces)), position, pair_out, cross_out)
    end = jnp.where(iota((8, COLS), 0) == 0, end, 0.0)
    tail_out[...] = jnp.concatenate(chain[1:] + [end], axis=0)
    for copy in copies[first:]:
        copy.wait()


def prepare_kernel(
    state, tail, source, orientation, flux_other, face_front, face_turn, stiff_vol,
    star, labels, lists,
    coarse_out, slot_flux_out, slot_code_out, slot_hot_out, lift_out, slot_lift_out,
    narrow_hot_out, slot_narrow_out, star_out, send_out,
    table, fronts, tall, slot_tall, flat,
):
    fine = labels[...] == 1
    before = (iota((LANES, LANES), 0) < iota((LANES, LANES), 1)).astype(F32).astype(BF16)
    marks = jnp.broadcast_to(jnp.where(fine, 1.0, 0.0), (16, LANES)).astype(BF16)
    rank = jnp.dot(marks, before, preferred_element_type=F32)[0:1].astype(jnp.int32)
    rank = jnp.where(fine, rank, -1)
    lane = iota((LANES, LANES), 0)
    lane = jnp.where(lane >= PART, lane - PART, lane)
    narrow_hot = jnp.where(rank == lane, 1.0, 0.0).astype(BF16)
    narrow_hot_out[...] = narrow_hot
    flat[...] = jnp.zeros(flat.shape, F32)
    for q in range(NQ):
        for p in range(NQ):
            start = STAR_ROWS * q + 4 * p
            flat[start : start + 3, :] = star[q, p]
    gathered = gather_exact(flat[...], narrow_hot)
    stars = [gathered[STAR_ROWS * q : STAR_ROWS * (q + 1)] for q in range(NQ)]
    packed = paired(stars)
    for t in range(TWOS):
        star_out[STAR_ROWS * t : STAR_ROWS * (t + 1), :] = packed[:, lanes(t)]
    _, inner = list_rows()
    half = first_half(PEERS * BOTH)
    across = (((1,), (1,)), ((), ()))
    for j in range(4):
        chosen = jnp.where(list_hot(lists, j) & (inner < SLOTS), 1.0, 0.0).astype(BF16)
        found = lax.dot_general(chosen, narrow_hot, across, preferred_element_type=F32)
        send_out[0 : PEERS * BOTH, lanes(j)] = jnp.where(half, found, 0.0).astype(BF16)
        send_out[PEERS * BOTH :, lanes(j)] = jnp.where(half, 0.0, found).astype(BF16)
    chain = [state[...]]
    start = 0
    for _, _, padded, _ in LEVELS:
        chain.append(tail[start : start + padded, :])
        start += padded
    for step in range(1, SUBSTEPS):
        coarse_out[step - 1] = integral_of(
            chain, taylor_weights(step / SUBSTEPS, (step + 1) / SUBSTEPS)
        )
    row = iota((LANES, LANES), 0)
    peer = (row >= BOTH).astype(jnp.int32) + (row >= 2 * BOTH).astype(jnp.int32)
    peer = peer + (row >= 3 * BOTH).astype(jnp.int32)
    inner = row - BOTH * peer
    kind = (inner >= SLOTS).astype(jnp.int32)
    wanted = kind * (PEERS * SLOTS - SLOTS) + peer * SLOTS + inner + FACES
    wanted = jnp.where(row < PEERS * BOTH, wanted, -1)
    blocks = [jnp.where(source[i : i + 1, :] == wanted, 1.0, 0.0) for i in range(4)]
    slot_hot = (blocks[0] + blocks[1] + blocks[2] + blocks[3]).astype(BF16)
    slot_hot_out[...] = slot_hot
    slot_narrow_out[...] = lax.dot_general(
        slot_hot, narrow_hot, across, preferred_element_type=F32
    ).astype(BF16)
    hot = jnp.concatenate(blocks, axis=1).astype(BF16)
    codes = jnp.concatenate(
        [
            jnp.where(iota((16, LANES), 0) - 3 * i == orientation[i : i + 1, :], 1.0, 0.0)
            for i in range(4)
        ],
        axis=1,
    ).astype(BF16)
    dims = (((1,), (1,)), ((), ()))
    found = lax.dot_general(codes, hot, dims, preferred_element_type=F32)
    for code in range(12):
        slot_code_out[SLOT_PAD * code : SLOT_PAD * (code + 1), :] = jnp.broadcast_to(
            found[code : code + 1], (SLOT_PAD, LANES)
        ).astype(BF16)
    table[...] = jnp.zeros(table.shape, F32)
    for i in range(4):
        for q in range(NQ):
            table[16 * q : 16 * q + NQ, lanes(i)] = flux_other[q, :, i, :]
    slot_flux_out[...] = pick_across(table[...], hot)

    fronts[...] = jnp.zeros(fronts.shape, F32)
    tall[...] = jnp.zeros(tall.shape, F32)
    slot_tall[...] = jnp.zeros(slot_tall.shape, F32)
    for i in range(4):
        fronts[0:NF, i * LANES : i * LANES + NB] = face_front[:, i, :]
    for code in range(3):
        turned = lax.dot_general(
            face_turn[code], fronts[0:NF, :], (((0,), (0,)), ((), ())),
            precision=HIGHEST, preferred_element_type=F32,
        )
        for i in range(4):
            start = FPAD * (3 * i + code)
            tall[start : start + NF, :] = -turned[:, lanes(i)]
            start = SLOT_PAD * (3 * i + code)
            slot_tall[start : start + NF, :] = -turned[:, lanes(i)]
    for i in range(4):
        start = REM + FPAD * i
        tall[start : start + NF, :] = -fronts[0:NF, lanes(i)]
    for d in range(3):
        start = REM + OWN + VPAD * d
        tall[start : start + NLOW, 0:NB] = stiff_vol[d]
    lift_out[...] = jnp.transpose(tall[...])[0:NB]
    whole = jnp.transpose(slot_tall[...])[0:PART]
    top = whole.astype(BF16)
    slot_lift_out[0:PART, 0:SLOT_REM] = top
    slot_lift_out[0:PART, SLOT_REM:] = top
    slot_lift_out[PART:, 0:SLOT_REM] = (whole - top.astype(F32)).astype(BF16)
    slot_lift_out[PART:, SLOT_REM:] = jnp.zeros((PART, SLOT_REM), BF16)


def local_kernel(*refs, step):
    if step == 0:
        state, low, faces, *rest = refs
        state, low, faces = state[...], low[...], faces[...]
    else:
        state, by_slot, slot_hot, low, faces, coarse_faces, *rest = refs
    star, flux_self, flux_other, source, orientation, lift, *rest = rest
    coarse, weights, lists, narrow_hot, labels, *rest = rest
    out, *rest = rest
    if step > 0:
        state = state[...] + by_elements(by_slot[...], slot_hot[...])
        back = jnp.transpose(narrow_hot[...].astype(F32))
        half = iota((LANES, LANES), 1) < PART
        spread = jnp.concatenate(
            [
                jnp.transpose(jnp.where(half, back, 0.0)),
                jnp.transpose(jnp.where(half, 0.0, back)),
            ],
            axis=1,
        ).astype(BF16)
        both = VPAD + OWN
        rows = [
            part[:, lanes(t)] for t in range(TWOS) for part in (low, faces)
        ]
        wide = pick(jnp.concatenate(rows, axis=0), spread)
        wide = [wide[both * t : both * (t + 1)] for t in range(TWOS)]
        wide = jnp.concatenate(wide, axis=1)[:, 0:COLS]
        fine = labels[...] == 1
        fine = jnp.concatenate([fine] * NQ, axis=1)
        low = jnp.where(fine, wide[0:VPAD], coarse[step - 1, 0:VPAD, :])
        faces = jnp.where(fine, wide[VPAD:both], coarse_faces[...])
    if step + 1 < SUBSTEPS:
        narrow_out, next_faces_out, next_sent_out, stack = rest
        next_faces = weigh(weights, BACK, OWN, coarse[step])
        next_faces_out[...] = next_faces
        _, inner = list_rows()
        hot = jnp.concatenate(
            [jnp.where(list_hot(lists, j) & (inner >= SLOTS), 1.0, 0.0) for j in range(4)],
            axis=1,
        ).astype(BF16)
        next_sent_out[...] = pick_rows(hot, face_table(next_faces))
    else:
        (stack,) = rest
    column = iota((FACES, LANES), 0)
    hot = jnp.concatenate(
        [
            jnp.where(column == source[i : i + 1, :], 1.0, 0.0).astype(BF16)
            for i in range(4)
        ],
        axis=1,
    )
    found = pick(face_table(faces), hot)
    for d in range(3):
        totals = products(
            [lambda q: low[:, lanes(q)]], lambda _, q, p: star[q, p, d : d + 1, :]
        )
        base = REM + OWN + VPAD * d
        for p in range(NQ):
            stack[base : base + VPAD, lanes(p)] = totals[p]
    for i in range(4):
        totals = products(
            [lambda q: faces[i * FPAD : (i + 1) * FPAD, lanes(q)]],
            lambda _, q, p: flux_self[q, p, i : i + 1, :],
        )
        for p in range(NQ):
            stack[REM + FPAD * i : REM + FPAD * (i + 1), lanes(p)] = totals[p]
    for i in range(4):
        totals = products(
            [lambda q: found[place_of(q) : place_of(q) + FPAD, lanes(i)]],
            lambda _, q, p: flux_other[q, p, i : i + 1, :],
        )
        for code in range(3):
            mask = jnp.where(orientation[i : i + 1, :] == code, 1.0, 0.0)
            base = FPAD * (3 * i + code)
            for p in range(NQ):
                stack[base : base + FPAD, lanes(p)] = totals[p] * mask
    total = state + jnp.dot(
        lift[:, 0:DEEP], stack[...], precision=HIGH, preferred_element_type=F32
    )
    out[...] = total
    if step + 1 < SUBSTEPS:
        tall = jnp.concatenate([total[:, lanes(q)] for q in range(NQ)], axis=0)
        found = pick_across(tall, narrow_hot[...])
        narrow_out[...] = paired([found[NB * q : NB * (q + 1)] for q in range(NQ)])


def by_elements(by_slot, slot_hot):
    found = pick(by_slot, slot_hot)
    return jnp.concatenate([found[NB * p : NB * (p + 1)] for p in range(NQ)], axis=1)


def remote_part(position, near, upper, lower, slot_flux, slot_code, lift):
    odd = lax.rem(position, 2) == 1
    behind_up = lax.rem(position, 4) < 2
    up, down = upper[...], lower[...]
    behind = jnp.where(behind_up, up, down)
    ahead = jnp.where(behind_up, down, up)
    here = jnp.where(odd, near[0:BOTH, :], near[3 * BOTH : 4 * BOTH, :])
    rows = jnp.concatenate(
        [
            jnp.where(odd, here, behind[0:BOTH]),
            jnp.where(odd, ahead[0:BOTH], here),
            behind[BOTH : 2 * BOTH],
            ahead[BOTH : 2 * BOTH],
            jnp.zeros((LANES - PEERS * BOTH, WIDTH), F32),
        ],
        axis=0,
    )
    received = jnp.transpose(rows)
    totals = products(
        [lambda q: received[place_of(q) : place_of(q) + FPAD]],
        lambda _, q, p: slot_flux[16 * q + p : 16 * q + p + 1, :],
    )
    codes = [slot_code[SLOT_PAD * code : SLOT_PAD * (code + 1), :] for code in range(12)]
    gap = jnp.zeros((SLOT_PAD - FPAD, LANES), F32)
    columns = []
    for p in range(NQ):
        both = halves(jnp.concatenate([totals[p], gap], axis=0))
        masked = [part * mask for part in both for mask in codes]
        columns.append(jnp.concatenate(masked, axis=0))
    masked = jnp.concatenate(columns, axis=1)
    lifted = jnp.dot(lift[...], masked, preferred_element_type=F32)
    lifted = lifted[0:NB] + lifted[PART : PART + NB]
    return jnp.concatenate([lifted[:, lanes(p)] for p in range(NQ)], axis=0)


def next_kernel(
    place, near, upper, lower, slot_flux, slot_code, lift,
    narrow, slot_narrow, star, weights, tips, send_hot, coarse_sent,
    by_slot_out, low_out, faces_out, pair_out, cross_out,
):
    position = place[0]
    by_slot = remote_part(position, near, upper, lower, slot_flux, slot_code, lift)
    by_slot_out[...] = by_slot
    found = pick(by_slot, slot_narrow[...])
    now = narrow[...] + paired([found[NB * p : NB * (p + 1)] for p in range(NQ)])
    chain, end = chain_of(now, star, weights, tips, narrow_sums, narrow_join)
    first_weights = taylor_weights(0.0, 1.0 / SUBSTEPS)
    integral = integral_of(chain, first_weights)
    faces = weigh(weights, BACK, OWN, integral)
    low, faces = with_end(integral, faces, -first_weights[-1] * end, tips)
    low_out[...] = low
    faces_out[...] = faces
    found = pick_rows(send_hot[...], narrow_table(faces))
    rows = PEERS * BOTH
    sent = jnp.concatenate([found[0:rows], found[rows : 2 * rows]], axis=1) + coarse_sent[...]
    deliver(sent, position, pair_out, cross_out)


def last_kernel(
    place, near, upper, lower, slot_flux, slot_code, lift, state, slot_hot, out
):
    by_slot = remote_part(place[0], near, upper, lower, slot_flux, slot_code, lift)
    total = state[...] + by_elements(by_slot, slot_hot[...])
    for q in range(NQ):
        out[q] = total[:, lanes(q)]


def floats(*shape):
    return jax.ShapeDtypeStruct(shape, F32)


def call(kernel, args, outs, scratch, scalars=0, inside=False, flops=2.0e7):
    smem = pl.BlockSpec(memory_space=pltpu.SMEM)
    vmem = pl.BlockSpec(memory_space=pltpu.VMEM)
    given = pl.BlockSpec(memory_space=pl.ANY) if inside else vmem
    if inside:
        args = args[:scalars] + tuple(
            pltpu.with_memory_space_constraint(item, pltpu.HBM) for item in args[scalars:]
        )
    moved = 4 * sum(math.prod(item.shape) for item in list(args) + list(outs))
    return pl.pallas_call(
        kernel,
        in_specs=[smem] * scalars + [given] * (len(args) - scalars),
        out_specs=[vmem] * len(outs),
        out_shape=outs,
        scratch_shapes=[
            pltpu.VMEM(item, F32) if isinstance(item, tuple) else item for item in scratch
        ],
        compiler_params=pltpu.CompilerParams(vmem_limit_bytes=40 * 2**20),
        cost_estimate=pl.CostEstimate(flops=int(flops), bytes_accessed=moved, transcendentals=0),
    )(*args)


def swaps(count, first):
    pairs = []
    for low in range(2 * first, count - 2, 4):
        for one, other in ((low, low + 3), (low + 1, low + 2)):
            pairs += [(one, other), (other, one)]
    return pairs


def local(
    dofs, star, flux_self, flux_other, labels, neighbour_source, orientation,
    fine_send, coarse_send, stiff_time, stiff_vol, face_back, face_front, face_turn,
):
    count = lax.axis_size("dom")
    pairs = [[low, low + 1] for low in range(0, count, 2)]
    place = lax.axis_index("dom").astype(jnp.int32)
    partner = jnp.where(place % 2 == 1, BOTH, 4 * BOTH)
    upper_from = partner + jnp.where(place % 4 >= 2, 0, BOTH)
    lower_from = partner + jnp.where(place % 4 >= 2, BOTH, 0)
    place = place.reshape(1)
    labels = labels.reshape(1, LANES)
    later = (
        flux_self.transpose(1, 2, 0, 3),
        flux_other.transpose(1, 2, 0, 3),
        neighbour_source,
        orientation,
        face_front.transpose(2, 0, 1),
        face_turn,
        stiff_vol.transpose(0, 2, 1),
    )
    star = star.transpose(1, 2, 0, 3)
    back = face_back.transpose(1, 0, 2)
    message = floats(BOTH, WIDTH)
    sent_shapes = [floats(OWN, COLS), floats(3 * BOTH, WIDTH), message]
    like = lambda item: jax.ShapeDtypeStruct(item.shape, item.dtype)
    found = call(
        first_kernel,
        (place, dofs.transpose(1, 0, 2), star, stiff_time, back, fine_send, coarse_send, labels)
        + later,
        [floats(NB, COLS), floats(VPAD, COLS), floats(TAIL, COLS)]
        + sent_shapes
        + [jax.ShapeDtypeStruct((CHAIN_ROWS, 2 * LANES), BF16)]
        + [floats(TIP_ROWS + 24 * DEPTH_3, LANES), like(star), like(labels)]
        + [jax.ShapeDtypeStruct((PEERS * BOTH, LANES), jnp.int32)]
        + [like(item) for item in later],
        [(CHAIN_ROWS, LANES), (NQ, NB, LANES), stiff_time.shape, back.shape, (16, LANES)]
        + [pltpu.VMEM(item.shape, jnp.int32) for item in (fine_send, coarse_send)]
        + [pltpu.SemaphoreType.DMA((7 + len(later),))],
        scalars=1,
        inside=True,
    )
    state, low, tail, faces, pair, cross, weights, tips, star, labels, lists = found[:11]
    flux_self, flux_other, source, orientation, front, turn, vol = found[11:]
    halved = lambda *shape: jax.ShapeDtypeStruct(shape, BF16)
    prepared = call(
        prepare_kernel,
        (state, tail, source, orientation, flux_other, front, turn, vol, star, labels, lists),
        [
            floats(SUBSTEPS - 1, NB, COLS), floats(16 * NQ, LANES), halved(SLOT_REM, LANES),
            halved(LANES, LANES), floats(NB, DEEP_PAD), halved(2 * PART, 2 * SLOT_REM),
            halved(LANES, LANES), halved(LANES, LANES), floats(TWOS * STAR_ROWS, LANES),
            halved(2 * PEERS * BOTH, FACES),
        ],
        [
            (16 * NQ, FACES), (FPAD, FACES), (DEEP_PAD, LANES), (SLOT_REM, LANES),
            (NQ * STAR_ROWS, LANES),
        ],
    )
    coarse, slot_flux, slot_code, slot_hot, lift, slot_lift = prepared[:6]
    narrow_hot, slot_narrow, narrow_star, send_hot = prepared[6:]
    fixed = (star, flux_self, flux_other, source, orientation, lift)
    fixed += (coarse, weights, lists, narrow_hot, labels)
    known = (state, low, faces)
    for step in range(SUBSTEPS):
        near = lax.all_gather(pair, "dom", axis_index_groups=pairs, tiled=True)
        passed = lax.dynamic_slice(near, (lower_from, 0), (BOTH, WIDTH))
        lower = jnp.concatenate([cross, passed], axis=0)
        lower, cross, shared = lax.optimization_barrier((lower, cross, near))
        passed = lax.dynamic_slice(shared, (upper_from, 0), (BOTH, WIDTH))
        upper = jnp.concatenate([cross, passed], axis=0)
        upper = lax.ppermute(upper, "dom", swaps(count, 1))
        lower = lax.ppermute(lower, "dom", swaps(count, 0))
        ahead = [floats(NB, NARROW), floats(OWN, COLS), floats(PEERS * BOTH, WIDTH)]
        state, *made = call(
            functools.partial(local_kernel, step=step),
            known + fixed,
            [floats(NB, COLS)] + (ahead if step + 1 < SUBSTEPS else []),
            [(DEEP, COLS)],
        )
        received = (place, near, upper, lower, slot_flux, slot_code, slot_lift)
        if step + 1 < SUBSTEPS:
            narrow, coarse_faces, coarse_sent = made
            by_slot, low, faces, pair, cross = call(
                next_kernel,
                received
                + (narrow, slot_narrow, narrow_star, weights, tips, send_hot, coarse_sent),
                [floats(NQ * NB, LANES), floats(VPAD, NARROW), floats(OWN, NARROW)]
                + sent_shapes[1:],
                [],
                scalars=1,
            )
            known = (state, by_slot, slot_hot, low, faces, coarse_faces)
    (result,) = call(
        last_kernel, received + (state, slot_hot), [floats(NQ, NB, LANES)], [], scalars=1
    )
    return result.transpose(1, 0, 2)


def solution(mesh):
    split = P(None, None, "dom")
    face = P(None, None, None, "dom")
    row = P(None, "dom")
    in_specs = (split, face, face, face, P("dom"), row, row, row, row, P(), P(), P(), P(), P())
    return jax.shard_map(local, mesh=mesh, in_specs=in_specs, out_specs=split, check_vma=False)
```
